128 devices in a mesh: fsdp: 16 (over x_hi, z, core), tp: 8 (over y, x_lo).
Axes of the slice: x: 4 (x_hi: 2, x_lo: 2; x = x_hi * 2 + x_lo), y: 4, z: 4, core: 2. Of those that a mesh axis runs over, the one named last changes fastest.
Arguments:
- inputs: bfloat16 [16384, 1024], P(('fsdp', 'tp')), may hold values from -6 to 6
- lengths: int32 [16, 3], P('fsdp'), may hold values from 1 to 1024, as said below
- routes: int32 [16384, 8], P('fsdp'), may hold values from 0 to 31, all different within a row; in each aligned block of 1024 rows (0 to 1023, 1024 to 2047, ...) at most 341 rows name the same one
- attn_gain: bfloat16 [1024], P('fsdp'), may hold values from 0.5 to 1.5
- query_weight: bfloat16 [1024, 1024], P('fsdp', 'tp'), may hold values from -0.5 to 0.5
- key_weight: bfloat16 [1024, 512], P('fsdp', 'tp'), may hold values from -0.5 to 0.5
- value_weight: bfloat16 [1024, 512], P('fsdp', 'tp'), may hold values from -0.1875 to 0.1875
- output_weight: bfloat16 [1024, 1024], P('tp', 'fsdp'), may hold values from -2 to 2
- moe_gain: bfloat16 [1024], P('fsdp'), may hold values from 0.5 to 1.5
- router_weight: bfloat16 [1024, 32], P('fsdp'), may hold values from -0.09375 to 0.09375
- gate_weight: bfloat16 [32, 1024, 512], P('tp', 'fsdp'), may hold values from -0.1875 to 0.1875
- up_weight: bfloat16 [32, 1024, 512], P('tp', 'fsdp'), may hold values from -0.1875 to 0.1875
- down_weight: bfloat16 [32, 512, 1024], P('tp', None, 'fsdp'), may hold values from -1 to 1
- cotangent: bfloat16 [16384, 1024], P(('fsdp', 'tp')), may hold values from -6 to 6
Outputs:
- outputs: bfloat16 [16384, 1024], P(('fsdp', 'tp'))
- input_grad: float32 [16384, 1024], P(('fsdp', 'tp'))
- attn_gain_grad: float32 [1024], P(('fsdp', 'tp'))
- query_grad: float32 [1024, 1024], P('fsdp', 'tp')
- key_grad: float32 [1024, 512], P('fsdp', 'tp')
- value_grad: float32 [1024, 512], P('fsdp', 'tp')
- output_grad: float32 [1024, 1024], P('tp', 'fsdp')
- moe_gain_grad: float32 [1024], P(('fsdp', 'tp'))
- router_grad: float32 [1024, 32], P(('fsdp', 'tp'))
- gate_grad: float32 [32, 1024, 512], P('tp', 'fsdp')
- up_grad: float32 [32, 1024, 512], P('tp', 'fsdp')
- down_grad: float32 [32, 512, 1024], P('tp', None, 'fsdp')
The draws below stay inside these ranges and needn't reach their ends.
Inputs may be any that keep to these rules, and one draw needn't show every extreme that they name: `lengths`: each row sums to 1024; one length in each row is at least 896, the others are at most 64. `routes`: in each aligned block of 1024 rows no expert is named by more than 341 rows, and in some block one is named by exactly 341.
All inputs are finite; a program needn't handle non-finite values.
Results may differ from the reference program's by a relative error of at most 0.025.
Values may be sent and summed in bfloat16 or wider, within the bound.
A program may use at most 128 MiB of HBM per device.

```python
import math
import jax
import jax.numpy as jnp
import numpy as np
from jax import lax

D = 1024
HEADS = 16
KV_HEADS = 8
HEAD_DIM = 64
EXPERTS = 32
HIDDEN_SIZE = 512
TOPK = 8
GROUP = 1024
SEQS = 3
TOK_DEV = 128
CAP = 341
TOKENS = 16384
N_FSDP = 16


def draw_lengths(key, part):
    key = jax.random.fold_in(key, 11)
    short_key, place_key = jax.random.split(key)
    shorter = jax.random.randint(short_key, (N_FSDP, SEQS - 1), 1, TOK_DEV // 2 + 1, dtype=jnp.int32)
    longest = GROUP - jnp.sum(shorter, axis=1)
    where_long = jax.random.randint(place_key, (N_FSDP, 1), 0, SEQS, dtype=jnp.int32)
    column = jnp.arange(SEQS, dtype=jnp.int32)[None, :]
    zero_column = jnp.zeros((N_FSDP, 1), jnp.int32)
    padded_short = jnp.concatenate([shorter, zero_column], axis=1)
    shifted = jnp.concatenate([zero_column, shorter], axis=1)
    after = jnp.where(column == where_long, longest[:, None], shifted)
    return jnp.where(column < where_long, padded_short, after)


def levels(rng, extent, shards, least, top_value):
    level = 1.0
    for dim, blocks in shards:
        heights = jax.random.uniform(jax.random.fold_in(jax.random.fold_in(rng, 6), dim), (blocks,), jnp.float32, least / len(shards), top_value / len(shards))
        level = level * jnp.repeat(jnp.exp(heights), extent[dim] // blocks).reshape((-1,) + (1,) * (len(extent) - 1 - dim))
    return level


def shared_out(own_key, own, number, rows, amount, top, bound, skew):
    ranking = jax.random.permutation(own_key, amount)
    heavy_load, ordinary = load_shares(amount, rows * top, bound, skew, True), load_shares(amount, rows * top, bound, skew, False)
    places = jnp.arange(amount)

    def named(sizes, turn):
        used = int((sizes > 0).sum())
        fixed = max(1, used // 4)
        passed = fixed + (places - fixed + turn * (used - fixed)) % max(1, amount - fixed)
        return jnp.zeros((amount,), jnp.int32).at[ranking[jnp.where(places < fixed, places, passed)]].set(jnp.asarray(sizes, jnp.int32))

    sizes = jnp.where(number % 4 == 0, named(heavy_load, number // 4), named(ordinary, number - number // 4 - 1))
    mixed = jax.random.permutation(jax.random.fold_in(own, 3), amount)
    source_of, taker = mixed[0:amount // 2 * 2:2], mixed[1:amount // 2 * 2:2]
    slack = jnp.minimum(sizes[source_of] - 1, bound - sizes[taker]) // 2
    slack = jnp.where((source_of == ranking[0]) | (taker == ranking[0]) | (sizes[taker] == 0), 0, jnp.maximum(slack, 0))
    passed = jax.random.randint(jax.random.fold_in(own, 4), (amount // 2,), 0, 1 << 20) % (slack + 1)
    sizes = sizes.at[source_of].add(-passed).at[taker].add(passed)
    labels = jnp.searchsorted(jnp.cumsum(sizes), jnp.arange(rows * top), side="right").astype(jnp.int32)
    table = labels.reshape(top, rows).T
    table = table[jax.random.permutation(jax.random.fold_in(own, 1), rows)]
    turn = jax.random.randint(jax.random.fold_in(own, 2), (rows, 1), 0, top)
    return jnp.take_along_axis(table, (jnp.arange(top)[None, :] + turn) % top, axis=1)


def load_shares(number_of, total, limit, lean, full):
    loads = [(1 << 20) // math.isqrt(grade ** lean) + 1 for grade in range(1, number_of + 1)]
    largest = limit if full else min(limit, max(-(-total // number_of), total * loads[0] // sum(loads)))
    least = 1 if total - largest >= number_of - 1 else 0
    holding, rest = [largest] + [least] * (number_of - 1), total - largest - least * (number_of - 1)
    while rest > 0:
        free = [i for i in range(1, number_of) if holding[i] < largest] or [i for i in range(1, number_of) if holding[i] < limit]
        mass, remaining = sum([loads[i] for i in free]), rest
        for i in free:
            addition = min(limit - holding[i], max(1, remaining * loads[i] // mass), rest)
            holding[i] = holding[i] + addition
            rest = rest - addition
    return np.array(holding)


def normal_values(rng, extent, width, limit, cuts=(), kind=jnp.bfloat16):
    drawn = jax.random.normal(rng, extent, jnp.float32) * width
    if len(cuts) > 0:
        drawn = levels(rng, extent, cuts, -0.22, 0.18) * drawn
    return jnp.clip(drawn, min=-limit, max=limit).astype(kind)


def setup_inputs(seed: int = 0) -> dict:
    arg_keys = jax.random.split(jax.random.key(seed), 15)
    inputs = normal_values(arg_keys[0], (TOKENS, D), 1.0, 6.0, ((0, 128),))
    lengths = draw_lengths(jax.random.fold_in(arg_keys[14], 71), 0)
    routes_keys = jax.random.split(jax.random.fold_in(arg_keys[2], 1), TOKENS // GROUP)
    routes_turns = jax.random.permutation(jax.random.fold_in(arg_keys[2], 3), TOKENS // GROUP)
    routes = jax.vmap(lambda own, number: shared_out(jax.random.fold_in(arg_keys[2], 2), own, number, GROUP, EXPERTS, TOPK, CAP, 1))(routes_keys, routes_turns).reshape((TOKENS, TOPK))
    attn_gain = jnp.clip(1.0 + 0.1 * jax.random.normal(arg_keys[3], (D,), jnp.float32), 0.5, 1.5).astype(jnp.bfloat16)
    query_weight = normal_values(arg_keys[4], (D, HEADS * HEAD_DIM), (D // 8) ** -0.5, 0.5, ((0, 16), (1, 8)))
    key_weight = normal_values(arg_keys[5], (D, KV_HEADS * HEAD_DIM), (D // 8) ** -0.5, 0.5, ((0, 16), (1, 8)))
    value_weight = normal_values(arg_keys[6], (D, KV_HEADS * HEAD_DIM), D ** -0.5, 0.1875, ((0, 16), (1, 8)))
    output_weight = normal_values(arg_keys[7], (HEADS * HEAD_DIM, D), (HEADS * HEAD_DIM // 128) ** -0.5, 2.0, ((0, 8), (1, 16)))
    moe_gain = jnp.clip(1.0 + 0.1 * jax.random.normal(arg_keys[8], (D,), jnp.float32), 0.5, 1.5).astype(jnp.bfloat16)
    router_weight = normal_values(arg_keys[9], (D, EXPERTS), (4 * D) ** -0.5, 0.09375, ((0, 16),))
    gate_weight = normal_values(arg_keys[10], (EXPERTS, D, HIDDEN_SIZE), D ** -0.5, 0.1875, ((0, 8), (1, 16)))
    up_weight = normal_values(arg_keys[11], (EXPERTS, D, HIDDEN_SIZE), D ** -0.5, 0.1875, ((0, 8), (1, 16)))
    down_weight = normal_values(arg_keys[12], (EXPERTS, HIDDEN_SIZE, D), (HIDDEN_SIZE // 16) ** -0.5, 1.0, ((0, 8), (2, 16)))
    cotangent = normal_values(arg_keys[13], (TOKENS, D), 1.0, 6.0, ((0, 128),))
    return dict(inputs=inputs, lengths=lengths, routes=routes, attn_gain=attn_gain, query_weight=query_weight, key_weight=key_weight, value_weight=value_weight, output_weight=output_weight, moe_gain=moe_gain, router_weight=router_weight, gate_weight=gate_weight, up_weight=up_weight, down_weight=down_weight, cotangent=cotangent)


@jax.custom_vjp
def low(v):
    return lax.optimization_barrier(v.astype(jnp.bfloat16)).astype(jnp.float32)

@jax.custom_vjp
def low_back(v):
    return v

def low_keep(v):
    return (low(v), None)

def low_pass(kept, grad):
    return (grad,)

def back_keep(v):
    return (v, None)

def back_low(kept, grad):
    return (low(grad),)
low.defvjp(low_keep, low_pass)
low_back.defvjp(back_keep, back_low)
highest = lax.Precision.HIGHEST
eps_norm = 1e-06
rope_base = 10000.0

def rms_scale(values, gain):
    mean_square = lax.optimization_barrier(jnp.mean(values * values, axis=-1, keepdims=True))
    return values * lax.rsqrt(mean_square + eps_norm) * gain

def rotate(values, cosine, sine):
    half_dim = values.shape[-1] // 2
    turned = jnp.concatenate([-values[..., half_dim:], values[..., :half_dim]], axis=-1)
    return values * cosine + turned * sine

def doc_layout(lengths_row):
    seq_ends = jnp.cumsum(lengths_row)
    positions = jnp.arange(GROUP, dtype=jnp.int32)
    doc_index = lax.optimization_barrier(jnp.sum((positions[:, None] >= seq_ends[None, :]).astype(jnp.int32), axis=1))
    starts = seq_ends - lengths_row
    match = doc_index[:, None] == jnp.arange(SEQS, dtype=jnp.int32)[None, :]
    doc_start = lax.optimization_barrier(jnp.sum(jnp.where(match, starts[None, :], 0), axis=1))
    return (doc_index, positions - doc_start)

def rope_tables(offset):
    frequency = rope_base ** (-jnp.arange(0, HEAD_DIM // 2, dtype=jnp.float32) * 2.0 / HEAD_DIM)
    angles = offset.astype(jnp.float32)[:, None] * frequency[None, :]
    angles = jnp.concatenate([angles, angles], axis=1)
    return (jnp.cos(angles), jnp.sin(angles))

def slot_tables(route_rows):
    flat_expert = route_rows.reshape(-1)
    onehot = (flat_expert[:, None] == jnp.arange(EXPERTS, dtype=jnp.int32)[None, :]).astype(jnp.int32)
    running = jnp.cumsum(onehot, axis=0)
    slot_index = lax.optimization_barrier(jnp.sum(onehot * (running - 1), axis=1))
    where_to = flat_expert * CAP + slot_index
    entries = jnp.arange(GROUP * TOPK, dtype=jnp.int32)
    token_of = jnp.full((EXPERTS * CAP,), GROUP, jnp.int32).at[where_to].set(entries // TOPK)
    entry_of = jnp.full((EXPERTS * CAP,), GROUP * TOPK, jnp.int32).at[where_to].set(entries)
    return (token_of, entry_of)

def layer_group(params, block_in, lengths_row, route_rows):
    attn_gain, query_weight, key_weight, value_weight, output_weight, moe_gain, router_weight, gate_weight, up_weight, down_weight = params
    doc_index, offset = doc_layout(lengths_row)
    cosine, sine = rope_tables(offset)
    positions = jnp.arange(GROUP, dtype=jnp.int32)
    normed = low(rms_scale(block_in, attn_gain))
    query_raw = low_back(jnp.dot(normed, query_weight, precision=highest)).reshape(GROUP, HEADS, HEAD_DIM)
    key_raw = low_back(jnp.dot(normed, key_weight, precision=highest)).reshape(GROUP, KV_HEADS, HEAD_DIM)
    values = low_back(low(jnp.dot(normed, value_weight, precision=highest))).reshape(GROUP, KV_HEADS, HEAD_DIM)
    query = low(rotate(query_raw, cosine[:, None, :], sine[:, None, :]))
    keys = low(rotate(key_raw, cosine[:, None, :], sine[:, None, :]))
    repeat = HEADS // KV_HEADS
    keys_all = jnp.repeat(keys, repeat, axis=1)
    values_all = jnp.repeat(values, repeat, axis=1)
    block_rows = min(512, GROUP)
    score_scale = 1.0 / HEAD_DIM

    def attend(block_start):
        query_block = lax.dynamic_slice_in_dim(query, block_start, block_rows, 0)
        doc_block = lax.dynamic_slice_in_dim(doc_index, block_start, block_rows, 0)
        place_block = block_start + jnp.arange(block_rows, dtype=jnp.int32)
        scores = low_back(jnp.einsum('qhd,khd->hqk', query_block, keys_all, precision=highest) * score_scale)
        allowed = (place_block[:, None] >= positions[None, :]) & (doc_block[:, None] == doc_index[None, :])
        scores = jnp.where(allowed[None], scores, -1e+30)
        weights = jax.nn.softmax(scores, axis=-1)
        return jnp.einsum('hqk,khd->qhd', low(weights), values_all, precision=highest)
    starts = jnp.arange(GROUP // block_rows, dtype=jnp.int32) * block_rows
    mixed = lax.map(jax.checkpoint(attend), starts).reshape(GROUP, HEADS * HEAD_DIM)
    mixed = low_back(low(mixed))
    attended = low_back(jnp.dot(mixed, output_weight, precision=highest))
    middle = block_in + attended
    normed_two = low(rms_scale(middle, moe_gain))
    logits = low_back(jnp.dot(normed_two, router_weight, precision=highest))
    chosen_mask = (route_rows[:, :, None] == jnp.arange(EXPERTS, dtype=jnp.int32)[None, None, :]).astype(jnp.float32)
    chosen = lax.optimization_barrier(jnp.sum(chosen_mask * logits[:, None, :], axis=-1))
    gates = jax.nn.softmax(chosen, axis=-1)
    token_of, entry_of = slot_tables(route_rows)
    padded = jnp.concatenate([normed_two, jnp.zeros((1, D), jnp.float32)], axis=0)
    dispatched = padded[token_of].reshape(EXPERTS, CAP, D)
    gate_part = low_back(jnp.einsum('ecd,edh->ech', dispatched, gate_weight, precision=highest))
    up_part = low_back(jnp.einsum('ecd,edh->ech', dispatched, up_weight, precision=highest))
    hidden = low(jax.nn.silu(gate_part) * up_part)
    expert_out = low_back(jnp.einsum('ech,ehd->ecd', hidden, down_weight, precision=highest)).reshape(EXPERTS * CAP, D)
    gate_pad = jnp.concatenate([gates.reshape(-1), jnp.zeros((1,), jnp.float32)])
    slot_gate = gate_pad[entry_of]
    combined = jnp.zeros((GROUP + 1, D), jnp.float32).at[token_of].add(slot_gate[:, None] * expert_out)[:GROUP]
    return middle + low_back(combined)

def reference(inputs, lengths, routes, attn_gain, query_weight, key_weight, value_weight, output_weight, moe_gain, router_weight, gate_weight, up_weight, down_weight, cotangent):
    weight_list = (attn_gain, query_weight, key_weight, value_weight, output_weight, moe_gain, router_weight, gate_weight, up_weight, down_weight)
    params = tuple((weight.astype(jnp.float32) for weight in weight_list))
    grouped_in = inputs.astype(jnp.float32).reshape(N_FSDP, GROUP, D)
    grouped_routes = routes.reshape(N_FSDP, GROUP, TOPK)

    def forward(block_in, *weights):

        def one_group(group_items):
            return layer_group(weights, group_items[0], group_items[1], group_items[2])
        return lax.map(jax.checkpoint(one_group), (block_in, lengths, grouped_routes))
    result, pullback = jax.vjp(forward, grouped_in, *params)
    grads = pullback(cotangent.astype(jnp.float32).reshape(N_FSDP, GROUP, D))
    outputs = result.reshape(TOKENS, D).astype(jnp.bfloat16)
    return (outputs, grads[0].reshape(TOKENS, D), grads[1], grads[2], grads[3], grads[4], grads[5], grads[6], grads[7], grads[8], grads[9], grads[10])
```

```python
import functools

import jax
import jax.numpy as jnp
from jax import lax
from jax.experimental import pallas as pl
from jax.experimental.pallas import tpu as pltpu
from jax.sharding import PartitionSpec as P

MESH = pl.DeviceIdType.MESH
D = 1024
HEAD_DIM = 64
EXPERTS = 32
HIDDEN = 512
GROUP = 1024
SEQS = 3
ROWS = 128
SLOTS = 352
LOCAL = 4
BLOCK = 64
WIDE = D + 128

eps_norm = 1e-06
rope_base = 10000.0
score_scale = 1.0 / HEAD_DIM
F32 = jnp.float32
BF16 = jnp.bfloat16
TP_STEPS = ((2, 0), (2, 1), (1, 1), (3, 1), (1, 0), (3, 0), (0, 1))
CHIP_STEPS = ((1, 2), (0, 2), (1, 1), (1, 3), (0, 1), (0, 3), (1, 0))


def tp_peer(step):
    tp = lax.axis_index("tp")
    along_y, along_x = step
    return lax.rem(tp // 2 + along_y, 4) * 2 + lax.rem(tp + along_x, 2)


def chip_at(step):
    chip = lax.axis_index("fsdp") // 2
    along_x, along_z = step
    return lax.rem(chip // 4 + along_x, 2) * 4 + lax.rem(chip + along_z, 4)


def own_core():
    return lax.rem(lax.axis_index("fsdp"), 2)


def core_partner():
    return (lax.axis_index("fsdp") // 2) * 2 + 1 - own_core()


def send(src, dst, send_sem, recv_sem, device):
    copy = pltpu.make_async_remote_copy(
        src_ref=src,
        dst_ref=dst,
        send_sem=send_sem,
        recv_sem=recv_sem,
        device_id=device,
        device_id_type=MESH,
    )
    copy.start()
    return copy


def greet():
    barrier = pltpu.get_barrier_semaphore()
    for step in TP_STEPS:
        pl.semaphore_signal(barrier, inc=1, device_id={"tp": tp_peer(step)}, device_id_type=MESH)
    for step in CHIP_STEPS:
        pl.semaphore_signal(
            barrier,
            inc=1,
            device_id={"fsdp": chip_at(step) * 2 + own_core()},
            device_id_type=MESH,
        )
    pl.semaphore_signal(barrier, inc=1, device_id={"fsdp": core_partner()}, device_id_type=MESH)
    pl.semaphore_wait(barrier, 15)


class GatherTp:
    def __init__(self, rows, columns):
        self.rows = rows
        self.out = jax.ShapeDtypeStruct((8 * rows, columns), BF16)
        self.out_space = pltpu.VMEM
        self.scratch = [pltpu.SemaphoreType.DMA((7,)), pltpu.SemaphoreType.DMA((7,)), pltpu.SemaphoreType.DMA(())]

    def start(self, src, out, send_sem, recv_sem, own_sem):
        here = out.at[pl.ds(pl.multiple_of(lax.axis_index("tp") * self.rows, self.rows), self.rows)]
        self.copies = [
            send(src, here, send_sem.at[k], recv_sem.at[k], {"tp": tp_peer(step)})
            for k, step in enumerate(TP_STEPS)
        ]
        self.own = pltpu.make_async_copy(src, here, own_sem)
        self.own.start()

    def progress(self, k):
        pass

    def finish(self):
        for copy in self.copies:
            copy.wait()
        self.own.wait()


class SumTp:
    def __init__(self, rows, columns):
        self.rows = rows
        self.out = jax.ShapeDtypeStruct((rows, columns), F32)
        self.out_space = pltpu.VMEM
        self.scratch = [
            pltpu.SemaphoreType.DMA((7,)),
            pltpu.SemaphoreType.DMA((7,)),
            pltpu.VMEM((7, rows, columns), BF16),
        ]

    def start(self, src, out, send_sem, recv_sem, landed):
        self.src, self.out_ref, self.landed = src, out, landed
        self.copies = []
        for k, step in enumerate(TP_STEPS):
            peer = tp_peer(step)
            part = src.at[pl.ds(pl.multiple_of(peer * self.rows, self.rows), self.rows)]
            self.copies.append(send(part, landed.at[k], send_sem.at[k], recv_sem.at[k], {"tp": peer}))

    def progress(self, k):
        pass

    def finish(self):
        for copy in self.copies:
            copy.wait()
        first = lax.axis_index("tp") * self.rows

        @pl.loop(0, self.rows // 16)
        def _(i):
            at = pl.multiple_of(i * 16, 16)
            total = self.src[pl.ds(pl.multiple_of(first + at, 16), 16), :].astype(F32)
            for k in range(7):
                total = total + self.landed[k, pl.ds(at, 16), :].astype(F32)
            self.out_ref[pl.ds(at, 16), :] = total


class GatherFsdp:
    def __init__(self, experts, columns):
        self.out = jax.ShapeDtypeStruct((experts, D, columns), BF16)
        self.out_space = pl.ANY
        self.scratch = [pltpu.SemaphoreType.DMA((7,)), pltpu.SemaphoreType.DMA((7,)), pltpu.SemaphoreType.DMA((8,)), pltpu.SemaphoreType.DMA((8,)), pltpu.SemaphoreType.DMA(())]

    def block(self, fsdp):
        return self.out_ref.at[:, pl.ds(pl.multiple_of(fsdp * BLOCK, BLOCK), BLOCK)]

    def start(self, src, out, send_sem, recv_sem, core_send, core_recv, own_sem):
        self.out_ref, self.core_send, self.core_recv = out, core_send, core_recv
        here = self.block(lax.axis_index("fsdp"))
        self.copies = [
            send(src, here, send_sem.at[k], recv_sem.at[k], {"fsdp": chip_at(step) * 2 + own_core()})
            for k, step in enumerate(CHIP_STEPS)
        ]
        self.across = [send(src, here, core_send.at[7], core_recv.at[7], {"fsdp": core_partner()})]
        self.own = pltpu.make_async_copy(src, here, own_sem)
        self.own.start()

    def progress(self, k):
        if k == 7:
            return
        along_x, along_z = CHIP_STEPS[k]
        self.copies[k].wait_recv()
        block = self.block(chip_at((along_x, (4 - along_z) % 4)) * 2 + own_core())
        self.across.append(
            send(block, block, self.core_send.at[k], self.core_recv.at[k], {"fsdp": core_partner()})
        )

    def finish(self):
        for copy in self.copies:
            copy.wait_send()
        for copy in self.across:
            copy.wait()
        self.own.wait()


class SumFsdp:
    def __init__(self, experts, columns, dtype=BF16):
        self.experts = experts
        self.out = jax.ShapeDtypeStruct((experts, BLOCK, columns), F32)
        self.out_space = pltpu.VMEM
        self.scratch = [
            pltpu.SemaphoreType.DMA((7,)),
            pltpu.SemaphoreType.DMA((7,)),
            pltpu.SemaphoreType.DMA((8,)),
            pltpu.SemaphoreType.DMA((8,)),
            pltpu.VMEM((8, experts, BLOCK, columns), dtype),
            pltpu.VMEM((7, experts, BLOCK, columns), dtype),
        ]

    def start(self, src, out, send_sem, recv_sem, core_send, core_recv, pair, landed):
        self.src, self.out_ref, self.pair, self.landed = src, out, pair, landed
        self.send_sem, self.recv_sem = send_sem, recv_sem
        self.across, self.copies = [], []
        for k, step in enumerate(CHIP_STEPS + ((0, 0),)):
            first = (chip_at(step) * 2 + 1 - own_core()) * BLOCK
            part = src.at[:, pl.ds(pl.multiple_of(first, BLOCK), BLOCK)]
            self.across.append(
                send(part, pair.at[k], core_send.at[k], core_recv.at[k], {"fsdp": core_partner()})
            )

    def progress(self, k):
        self.across[k].wait_recv()
        step = (CHIP_STEPS + ((0, 0),))[k]
        owner = chip_at(step) * 2 + own_core()

        @pl.loop(0, self.experts * (BLOCK // 16))
        def _(i):
            expert = i // (BLOCK // 16)
            at = pl.multiple_of(lax.rem(i, BLOCK // 16) * 16, 16)
            mine = self.src[expert, pl.ds(pl.multiple_of(owner * BLOCK + at, 16), 16), :].astype(F32)
            total = mine + self.pair[k, expert, pl.ds(at, 16), :].astype(F32)
            self.pair[k, expert, pl.ds(at, 16), :] = total.astype(self.pair.dtype)

        if k < 7:
            self.copies.append(
                send(self.pair.at[k], self.landed.at[k], self.send_sem.at[k], self.recv_sem.at[k], {"fsdp": owner})
            )

    def finish(self):
        for copy in self.across:
            copy.wait_send()
        for copy in self.copies:
            copy.wait()

        @pl.loop(0, self.experts * (BLOCK // 16))
        def _(i):
            expert = i // (BLOCK // 16)
            at = pl.multiple_of(lax.rem(i, BLOCK // 16) * 16, 16)
            total = self.pair[7, expert, pl.ds(at, 16), :].astype(F32)
            for k in range(7):
                total = total + self.landed[k, expert, pl.ds(at, 16), :].astype(F32)
            self.out_ref[expert, pl.ds(at, 16), :] = total


class SumAll:
    def __init__(self, columns):
        self.over_fsdp = SumFsdp(1, columns, F32)
        self.out = jax.ShapeDtypeStruct((8, columns), F32)
        self.out_space = pltpu.VMEM
        self.scratch = self.over_fsdp.scratch + [
            pltpu.VMEM((1, BLOCK, columns), F32),
            pltpu.SemaphoreType.DMA((7,)),
            pltpu.SemaphoreType.DMA((7,)),
            pltpu.VMEM((7, 8, columns), F32),
        ]

    def start(self, src, out, *scratch):
        self.out_ref = out
        self.total, self.send_sem, self.recv_sem, self.landed = scratch[-4:]
        self.over_fsdp.start(src, self.total, *scratch[:-4])

    def progress(self, k):
        self.over_fsdp.progress(k)

    def middle(self):
        self.over_fsdp.finish()
        self.copies = []
        for k, step in enumerate(TP_STEPS):
            peer = tp_peer(step)
            part = self.total.at[0, pl.ds(pl.multiple_of(peer * 8, 8), 8)]
            self.copies.append(
                send(part, self.landed.at[k], self.send_sem.at[k], self.recv_sem.at[k], {"tp": peer})
            )

    def finish(self):
        for copy in self.copies:
            copy.wait()
        total = self.total[0, pl.ds(pl.multiple_of(lax.axis_index("tp") * 8, 8), 8), :]
        for k in range(7):
            total = total + self.landed[k]
        self.out_ref[...] = total


def exchange(name, number, tasks, arrays):
    n = len(tasks)
    counts = [len(task.scratch) for task in tasks]

    def body(*refs):
        sources, outs, scratch = refs[:n], refs[n : 2 * n], list(refs[2 * n :])
        greet()
        for task, source, out, count in zip(tasks, sources, outs, counts):
            task.start(source, out, *scratch[:count])
            scratch = scratch[count:]
        for k in range(8):
            for task in tasks:
                task.progress(k)
        for task in tasks:
            if isinstance(task, SumAll):
                task.middle()
        for task in tasks:
            task.finish()

    return pl.pallas_call(
        body,
        name=name,
        out_shape=[task.out for task in tasks],
        in_specs=[pl.BlockSpec(memory_space=pltpu.VMEM)] * n,
        out_specs=[pl.BlockSpec(memory_space=task.out_space) for task in tasks],
        scratch_shapes=[shape for task in tasks for shape in task.scratch],
        compiler_params=pltpu.CompilerParams(
            collective_id=number, has_side_effects=True, vmem_limit_bytes=48 * 2**20
        ),
    )(*arrays)


def dot(a, b, dims=((1,), (0,))):
    return lax.dot_general(a, b, (dims, ((), ())), preferred_element_type=F32)


def lanes(rows):
    return lax.broadcasted_iota(jnp.int32, (rows, 128), 1)


def turn(values):
    low_half = lax.rem(lanes(values.shape[0]), HEAD_DIM) < HEAD_DIM // 2
    return jnp.where(low_half, pltpu.roll(values, 96, 1), pltpu.roll(values, 32, 1))


def both_halves(pair):
    low = lanes(pair.shape[0]) < HEAD_DIM
    other = pltpu.roll(pair, HEAD_DIM, 1)
    return jnp.where(low, pair, other), jnp.where(low, other, pair)


def head_lanes(values, head):
    return jnp.where(lanes(values.shape[0]) // HEAD_DIM == head, values, 0.0)


def allowed(keys, first, queries, doc_column, doc_row):
    key_at = lax.broadcasted_iota(jnp.int32, (keys, queries), 0)
    query_at = first + lax.broadcasted_iota(jnp.int32, (keys, queries), 1)
    return (key_at <= query_at) & (doc_column[:keys, :] == doc_row[:, first : first + queries])


def unit_rows(values):
    return values * lax.rsqrt(jnp.mean(values * values, axis=-1, keepdims=True) + eps_norm)


QUERIES = 256


def attention_body(
    x_ref, w_ref, gain_ref, cos_q, sin_q, cos_k, sin_k, doc_column, doc_row,
    normed_ref, query_ref, pair_ref, lse_ref, mixed_ref, attended_ref, mixed_t,
):
    @pl.loop(0, GROUP // 128)
    def _(i):
        rows = pl.ds(pl.multiple_of(i * 128, 128), 128)
        normed = (unit_rows(x_ref[rows, :].astype(F32)) * gain_ref[...]).astype(BF16)
        normed_ref[rows, :] = normed
        raw = dot(normed, w_ref[:, 0:256])
        query, pair = raw[:, 0:128], raw[:, 128:256]
        query_ref[rows, :] = (query * cos_q[rows, :] + turn(query) * sin_q[rows, :]).astype(BF16)
        pair_ref[rows, :] = (pair * cos_k[rows, :] + turn(pair) * sin_k[rows, :]).astype(BF16)

    keys, values = both_halves(pair_ref[...].astype(F32))
    keys, values_t = keys.astype(BF16), values.T.astype(BF16)

    for first in range(0, GROUP, QUERIES):
        count = first + QUERIES
        mask = allowed(count, first, QUERIES, doc_column, doc_row)
        parts = []
        for head in range(2):
            query = head_lanes(query_ref[first : first + QUERIES, :].astype(F32), head).astype(BF16)
            scores = dot(keys[:count], query, ((1,), (1,))) * score_scale
            scores = jnp.where(mask, scores, -1e30)
            top = jnp.max(scores, axis=0, keepdims=True)
            raised = jnp.exp(scores - top)
            total = jnp.sum(raised, axis=0, keepdims=True)
            lse_ref[head : head + 1, first : first + QUERIES] = top + jnp.log(total)
            weights = (raised * (1.0 / total)).astype(BF16)
            parts.append(dot(values_t[HEAD_DIM * head : HEAD_DIM * (head + 1), :count], weights))
        for head in range(2):
            mixed_t[HEAD_DIM * head : HEAD_DIM * (head + 1), first : first + QUERIES] = parts[head]
    mixed_ref[...] = mixed_t[...].astype(BF16)

    @pl.loop(0, GROUP // 128)
    def _(i):
        at = pl.multiple_of(i * 128, 128)
        mixed = mixed_t[:, pl.ds(at, 128)].T.astype(BF16)
        attended_ref[pl.ds(at, 128), :] = dot(mixed, w_ref[:, 256:384], ((1,), (1,))).astype(BF16)


def attention(x, w, gain, tables, doc_column, doc_row):
    return pl.pallas_call(
        attention_body,
        name="attention",
        out_shape=[
            jax.ShapeDtypeStruct((GROUP, D), BF16),
            jax.ShapeDtypeStruct((GROUP, 128), BF16),
            jax.ShapeDtypeStruct((GROUP, 128), BF16),
            jax.ShapeDtypeStruct((2, GROUP), F32),
            jax.ShapeDtypeStruct((128, GROUP), BF16),
            jax.ShapeDtypeStruct((GROUP, D), BF16),
        ],
        scratch_shapes=[pltpu.VMEM((128, GROUP), F32)],
        compiler_params=pltpu.CompilerParams(vmem_limit_bytes=48 * 2**20),
    )(x, w, gain, *tables, doc_column, doc_row)


def attention_back_body(
    datt_ref, x_ref, normed_ref, w_ref, query_ref, pair_ref, lse_ref, mixed_ref,
    cos_q, sin_q, cos_k, sin_k, doc_column, doc_row,
    grad_ref, weights_ref, gain_ref, dmixed_ref, dquery_t, dpair_ref, raw_ref, raw_t,
):
    @pl.loop(0, GROUP // 128)
    def _(i):
        rows = pl.ds(pl.multiple_of(i * 128, 128), 128)
        dmixed_ref[rows, :] = dot(datt_ref[rows, :], w_ref[:, 256:384]).astype(BF16)

    keys, values = both_halves(pair_ref[...].astype(F32))
    keys_t = keys.T.astype(BF16)
    keys, values = keys.astype(BF16), values.astype(BF16)
    dpair_ref[...] = jnp.zeros_like(dpair_ref)

    for first in range(0, GROUP, QUERIES):
        count = first + QUERIES
        mask = allowed(count, first, QUERIES, doc_column, doc_row)
        for head in range(2):
            query = head_lanes(query_ref[first : first + QUERIES, :].astype(F32), head).astype(BF16)
            dmixed = head_lanes(dmixed_ref[first : first + QUERIES, :].astype(F32), head).astype(BF16)
            scores = dot(keys[:count], query, ((1,), (1,))) * score_scale
            scores = jnp.where(mask, scores, -1e30)
            weights = jnp.exp(scores - lse_ref[head : head + 1, first : first + QUERIES])
            dweights = dot(values[:count], dmixed, ((1,), (1,)))
            inner = jnp.sum(weights * dweights, axis=0, keepdims=True)
            dscores = (weights * (dweights - inner)).astype(BF16)
            dquery_t[HEAD_DIM * head : HEAD_DIM * (head + 1), first : first + QUERIES] = (
                dot(keys_t[HEAD_DIM * head : HEAD_DIM * (head + 1), :count], dscores) * score_scale
            )
            dpair_ref[0, :count, :] += dot(dscores, query) * score_scale
            dpair_ref[1, :count, :] += dot(weights.astype(BF16), dmixed)

    gain_ref[...] = jnp.zeros_like(gain_ref)

    @pl.loop(0, GROUP // 128)
    def _(i):
        at = pl.multiple_of(i * 128, 128)
        rows = pl.ds(at, 128)
        dquery = dquery_t[:, rows].T
        dkey, dvalue = dpair_ref[0, rows, :], dpair_ref[1, rows, :]
        dkey = dkey + pltpu.roll(dkey, HEAD_DIM, 1)
        dvalue = dvalue + pltpu.roll(dvalue, HEAD_DIM, 1)
        dpair = jnp.where(lanes(128) < HEAD_DIM, dkey, dvalue)
        dquery = dquery * cos_q[rows, :] + turn(dquery * sin_q[rows, :])
        dpair = dpair * cos_k[rows, :] + turn(dpair * sin_k[rows, :])
        raw_ref[rows, 0:128] = dquery.astype(BF16)
        raw_ref[rows, 128:256] = dpair.astype(BF16)
        raw_t[0:128, rows] = dquery.T.astype(BF16)
        raw_t[128:256, rows] = dpair.T.astype(BF16)
        dnormed = dot(raw_ref[rows, :], w_ref[:, 0:256], ((1,), (1,)))
        grad_ref[rows, :] = dnormed.astype(BF16)
        unit = unit_rows(x_ref[rows, :].astype(F32))
        gain_ref[...] += jnp.sum(dnormed * unit, axis=0, keepdims=True)

    @pl.loop(0, D // 256)
    def _(i):
        at = pl.ds(pl.multiple_of(i * 256, 256), 256)
        weights_ref[at, 0:256] = dot(raw_t[...], normed_ref[:, at]).T.astype(BF16)
        weights_ref[at, 256:384] = dot(mixed_ref[...], datt_ref[:, at]).T.astype(BF16)


def attention_back(datt, x, normed, w, query, pair, lse, mixed, tables, doc_column, doc_row):
    return pl.pallas_call(
        attention_back_body,
        name="attention_back",
        out_shape=[
            jax.ShapeDtypeStruct((GROUP, D), BF16),
            jax.ShapeDtypeStruct((D, 384), BF16),
            jax.ShapeDtypeStruct((1, D), F32),
        ],
        scratch_shapes=[
            pltpu.VMEM((GROUP, 128), BF16),
            pltpu.VMEM((128, GROUP), F32),
            pltpu.VMEM((2, GROUP, 128), F32),
            pltpu.VMEM((GROUP, 256), BF16),
            pltpu.VMEM((256, GROUP), BF16),
        ],
        compiler_params=pltpu.CompilerParams(vmem_limit_bytes=48 * 2**20),
    )(datt, x, normed, w, query, pair, lse, mixed, *tables, doc_column, doc_row)


def experts_body(
    tp_ref, tokens_ref, dy_ref, router_ref, chosen_ref, rank_row, rank_column,
    gate_ref, up_ref, down_ref,
    combined_ref, grad_ref, gate_grad, up_grad, down_grad, combined_sum, grad_sum, gate_sum, gates_ref,
):
    step = pl.program_id(0)
    lane = lax.broadcasted_iota(jnp.int32, (1, 128), 1)

    @pl.when(step == 0)
    def _():
        combined_sum[...] = jnp.zeros_like(combined_sum)
        grad_sum[...] = jnp.zeros_like(grad_sum)
        gate_sum[...] = jnp.zeros_like(gate_sum)
        logits = jnp.where(chosen_ref[...] > 0, dot(tokens_ref[...], router_ref[...]), -1e30)
        raised = jnp.exp(logits - jnp.max(logits, axis=-1, keepdims=True))
        gates = raised / jnp.sum(raised, axis=-1, keepdims=True)
        high = gates.astype(BF16)
        gates_ref[:, 0:128] = high
        gates_ref[:, 128:256] = (gates - high.astype(F32)).astype(BF16)

    expert_lane = lane == tp_ref[0] * LOCAL + step
    slot = lax.broadcasted_iota(jnp.int32, (SLOTS, GROUP), 0)
    take = jnp.where(slot == rank_row[0], 1.0, 0.0).astype(BF16)
    slot_gates = dot(take, gates_ref[...])
    slot_gates = slot_gates[:, 0:128] + slot_gates[:, 128:256]
    slot_gate = jnp.sum(jnp.where(expert_lane, slot_gates, 0.0), axis=1, keepdims=True)
    picked = dot(take, tokens_ref[...]).astype(BF16)
    dy = dot(take, dy_ref[...]).astype(BF16)

    gate_part = dot(picked, gate_ref[0])
    up_part = dot(picked, up_ref[0])
    sigmoid = 1.0 / (1.0 + jnp.exp(-gate_part))
    silu = gate_part * sigmoid
    hidden = silu * up_part
    dhidden = dot(dy, down_ref[0])
    dgate = jnp.sum(hidden * dhidden, axis=1, keepdims=True)
    weighted = (hidden * slot_gate).astype(BF16)
    dhidden = dhidden * slot_gate
    dgate_part = (dhidden * up_part * (sigmoid * (1.0 + gate_part * (1.0 - sigmoid)))).astype(BF16)
    dup_part = (dhidden * silu).astype(BF16)

    down_grad[0] = dot(dy, weighted, ((0,), (0,))).astype(BF16)
    gate_grad[0] = dot(picked, dgate_part, ((0,), (0,))).astype(BF16)
    up_grad[0] = dot(picked, dup_part, ((0,), (0,))).astype(BF16)

    out = dot(weighted, down_ref[0], ((1,), (1,))).astype(BF16)
    dpicked = dot(dgate_part, gate_ref[0], ((1,), (1,)))
    dpicked = (dpicked + dot(dup_part, up_ref[0], ((1,), (1,)))).astype(BF16)
    dgate = jnp.where(expert_lane, dgate, 0.0).astype(BF16)

    give = jnp.where(
        lax.broadcasted_iota(jnp.int32, (GROUP, SLOTS), 1) == rank_column[0], 1.0, 0.0
    ).astype(BF16)
    combined_sum[...] += dot(give, out)
    grad_sum[...] += dot(give, dpicked)
    gate_sum[...] += dot(give, dgate)

    @pl.when(step == LOCAL - 1)
    def _():
        combined_ref[...] = combined_sum[...].astype(BF16)
        grad_ref[:, 0:D] = grad_sum[...].astype(BF16)
        grad_ref[:, D:WIDE] = gate_sum[...].astype(BF16)


def experts(tp, tokens, dy, router, chosen, rank_row, rank_column, gate, up, down):
    def whole(*shape):
        return pl.BlockSpec(shape, lambda i, tp: (0,) * len(shape))

    def own(*shape):
        return pl.BlockSpec((1,) + shape, lambda i, tp: (i,) + (0,) * len(shape))

    weight = jax.ShapeDtypeStruct((LOCAL, D, HIDDEN), BF16)
    return pl.pallas_call(
        experts_body,
        name="experts",
        grid_spec=pltpu.PrefetchScalarGridSpec(
            num_scalar_prefetch=1,
            grid=(LOCAL,),
            in_specs=[
                whole(GROUP, D),
                whole(GROUP, D),
                whole(D, 128),
                whole(GROUP, 128),
                own(1, GROUP),
                own(GROUP, 1),
                own(D, HIDDEN),
                own(D, HIDDEN),
                own(D, HIDDEN),
            ],
            out_specs=[
                whole(GROUP, D),
                whole(GROUP, WIDE),
                own(D, HIDDEN),
                own(D, HIDDEN),
                own(D, HIDDEN),
            ],
            scratch_shapes=[
                pltpu.VMEM((GROUP, D), F32),
                pltpu.VMEM((GROUP, D), F32),
                pltpu.VMEM((GROUP, 128), F32),
                pltpu.VMEM((GROUP, 256), BF16),
            ],
        ),
        out_shape=[
            jax.ShapeDtypeStruct((GROUP, D), BF16),
            jax.ShapeDtypeStruct((GROUP, WIDE), BF16),
            weight,
            weight,
            weight,
        ],
        compiler_params=pltpu.CompilerParams(vmem_limit_bytes=60 * 2**20),
    )(tp, tokens, dy, router, chosen, rank_row, rank_column, gate, up, down)


def doc_layout(lengths_row):
    seq_ends = jnp.cumsum(lengths_row)
    positions = jnp.arange(GROUP, dtype=jnp.int32)
    doc_index = jnp.sum((positions[:, None] >= seq_ends[None, :]).astype(jnp.int32), axis=1)
    starts = seq_ends - lengths_row
    match = doc_index[:, None] == jnp.arange(SEQS, dtype=jnp.int32)[None, :]
    doc_start = jnp.sum(jnp.where(match, starts[None, :], 0), axis=1)
    return (doc_index, positions - doc_start)


def rope_tables(offset):
    lane = jnp.arange(128, dtype=jnp.int32)
    frequency = rope_base ** (-(lane % 32).astype(F32) * 2.0 / HEAD_DIM)
    angles = offset.astype(F32)[:, None] * frequency[None, :]
    cosine, sine = jnp.cos(angles), jnp.sin(angles)
    sine = jnp.where(lane % 64 < 32, -sine, sine)
    key = lane < HEAD_DIM
    return (cosine, sine, jnp.where(key, cosine, 1.0), jnp.where(key, sine, 0.0))


def rms_parts(values, gain):
    inverse = lax.rsqrt(jnp.mean(values * values, axis=-1, keepdims=True) + eps_norm)
    unit = values * inverse
    return (unit * gain, unit, inverse)


def rms_back(grad_out, unit, inverse, gain):
    grad_unit = grad_out * gain
    return inverse * (grad_unit - unit * jnp.mean(grad_unit * unit, axis=-1, keepdims=True))


def per_device(
    inputs,
    lengths,
    routes,
    attn_gain,
    query_weight,
    key_weight,
    value_weight,
    output_weight,
    moe_gain,
    router_weight,
    gate_weight,
    up_weight,
    down_weight,
    cotangent,
):
    tp = lax.axis_index("tp")
    small = jnp.concatenate(
        [
            query_weight,
            key_weight,
            value_weight,
            output_weight.T,
            router_weight,
            attn_gain[:, None],
            moe_gain[:, None],
            jnp.zeros((BLOCK, 128 - EXPERTS - 2), BF16),
        ],
        axis=1,
    )
    x_all, weights, gate_all = exchange(
        "exchange_inputs",
        1,
        [GatherTp(ROWS, D), GatherFsdp(1, 512), GatherFsdp(LOCAL, HIDDEN)],
        [inputs, small[None], gate_weight],
    )
    weights = weights[0]
    gain_one = weights[:, 416].astype(F32)[None, :]
    gain_two = weights[:, 417].astype(F32)[None, :]
    router_all = weights[:, 384:416]

    doc_index, offset = doc_layout(lengths[0])
    tables = rope_tables(offset)
    doc_column, doc_row = doc_index[:, None], doc_index[None, :]
    normed, query, pair, lse, mixed, attended = attention(
        x_all, weights, gain_one, tables, doc_column, doc_row
    )
    attended, up_all = exchange(
        "exchange_attended",
        2,
        [SumTp(ROWS, D), GatherFsdp(LOCAL, HIDDEN)],
        [attended, up_weight],
    )
    middle = inputs.astype(F32) + attended
    normed_two, unit_two, inverse_two = rms_parts(middle, gain_two)
    normed_two = normed_two.astype(BF16)
    tokens, down_all = exchange(
        "exchange_tokens",
        3,
        [GatherTp(ROWS, D), GatherFsdp(LOCAL, HIDDEN)],
        [normed_two, down_weight.transpose(0, 2, 1)],
    )

    expert_ids = jnp.arange(128, dtype=jnp.int32)
    chosen = jnp.any(routes[:, :, None] == expert_ids[None, None, :], axis=1)
    positions = jnp.arange(GROUP, dtype=jnp.int32)
    until = (positions[:, None] >= positions[None, :]).astype(BF16)
    running = jnp.dot(until, chosen.astype(BF16), preferred_element_type=F32).astype(jnp.int32)
    rank = jnp.where(chosen, running - 1, -1)
    rank = lax.dynamic_slice_in_dim(rank, tp * LOCAL, LOCAL, 1).T
    dy_all = lax.all_gather(cotangent, "tp", axis=0, tiled=True)
    router_wide = jnp.pad(router_all, ((0, 0), (0, 128 - EXPERTS)))
    combined, grads, gate_grad, up_grad, down_grad = experts(
        tp[None],
        tokens,
        dy_all,
        router_wide,
        chosen.astype(jnp.int32),
        rank[:, None, :],
        rank[:, :, None],
        gate_all,
        up_all,
        down_all,
    )
    grads, gate_grad = exchange(
        "exchange_expert_grads",
        4,
        [SumTp(ROWS, WIDE), SumFsdp(LOCAL, HIDDEN)],
        [grads, gate_grad],
    )
    chosen_own = lax.dynamic_slice_in_dim(chosen, tp * ROWS, ROWS, 0)
    logits = jnp.dot(normed_two, router_wide, preferred_element_type=F32)
    gates = jax.nn.softmax(jnp.where(chosen_own, logits, -1e30), axis=-1)
    dgates = grads[:, D:]
    dlogits = gates * (dgates - jnp.sum(gates * dgates, axis=-1, keepdims=True))
    dlogits = dlogits.astype(BF16)
    dnormed_two = grads[:, :D] + jnp.einsum(
        "te,de->td", dlogits, router_wide, preferred_element_type=F32
    )
    router_grad = jnp.einsum("td,te->de", normed_two, dlogits, preferred_element_type=F32)
    moe_gain_grad = jnp.sum(dnormed_two * unit_two, axis=0)
    dmiddle = cotangent.astype(F32) + rms_back(dnormed_two, unit_two, inverse_two, gain_two)
    datt, up_grad, moe_out = exchange(
        "exchange_attended_grads",
        5,
        [GatherTp(ROWS, D), SumFsdp(LOCAL, HIDDEN), SumTp(ROWS, D)],
        [dmiddle.astype(BF16), up_grad, combined],
    )
    outputs = (middle + moe_out).astype(BF16)
    dnormed, attention_grads, attn_gain_grad = attention_back(
        datt, x_all, normed, weights, query, pair, lse, mixed, tables, doc_column, doc_row
    )
    small_grads = jnp.where(
        expert_ids[None, :] == EXPERTS,
        moe_gain_grad[:, None],
        jnp.where(expert_ids[None, :] == EXPERTS + 1, attn_gain_grad[0][:, None], router_grad),
    )
    dnormed, down_grad, attention_grads, small_grads = exchange(
        "exchange_input_grads",
        6,
        [SumTp(ROWS, D), SumFsdp(LOCAL, HIDDEN), SumFsdp(1, 384), SumAll(128)],
        [dnormed, down_grad, attention_grads[None], small_grads[None]],
    )
    _, unit_one, inverse_one = rms_parts(inputs.astype(F32), gain_one)
    input_grad = dmiddle + rms_back(dnormed, unit_one, inverse_one, gain_one)
    attention_grads = attention_grads[0]
    return (
        outputs,
        input_grad,
        small_grads[:, EXPERTS + 1],
        attention_grads[:, 0:128],
        attention_grads[:, 128:192],
        attention_grads[:, 192:256],
        attention_grads[:, 256:384].T,
        small_grads[:, EXPERTS],
        small_grads[:, :EXPERTS],
        gate_grad,
        up_grad,
        down_grad.transpose(0, 2, 1),
    )


def solution(mesh):
    return jax.shard_map(
        per_device,
        mesh=mesh,
        in_specs=(
            P(("fsdp", "tp"), None),
            P("fsdp", None),
            P("fsdp", None),
            P("fsdp"),
            P("fsdp", "tp"),
            P("fsdp", "tp"),
            P("fsdp", "tp"),
            P("tp", "fsdp"),
            P("fsdp"),
            P("fsdp", None),
            P("tp", "fsdp", None),
            P("tp", "fsdp", None),
            P("tp", None, "fsdp"),
            P(("fsdp", "tp"), None),
        ),
        out_specs=(
            P(("fsdp", "tp"), None),
            P(("fsdp", "tp"), None),
            P(("fsdp", "tp")),
            P("fsdp", "tp"),
            P("fsdp", "tp"),
            P("fsdp", "tp"),
            P("tp", "fsdp"),
            P(("fsdp", "tp")),
            P(("fsdp", "tp"), None),
            P("tp", "fsdp", None),
            P("tp", "fsdp", None),
            P("tp", None, "fsdp"),
        ),
        check_vma=False,
    )
```

```python
import functools

import jax
import jax.numpy as jnp
from jax import lax
from jax.experimental import pallas as pl
from jax.experimental.pallas import tpu as pltpu
from jax.sharding import PartitionSpec as P

MESH = pl.DeviceIdType.MESH
D = 1024
HEAD_DIM = 64
EXPERTS = 32
HIDDEN = 512
GROUP = 1024
SEQS = 3
ROWS = 128
SLOTS = 352
LOCAL = 4
BLOCK = 64
WIDE = D + 128

eps_norm = 1e-06
rope_base = 10000.0
score_scale = 1.0 / HEAD_DIM
F32 = jnp.float32
BF16 = jnp.bfloat16


def tp_at(along, across):
    tp = lax.axis_index("tp")
    return lax.rem(tp // 2 + along, 4) * 2 + lax.rem(tp + across, 2)


def fsdp_at(along, across):
    fsdp = lax.axis_index("fsdp")
    chip = lax.rem(fsdp // 8 + across, 2) * 4 + lax.rem(fsdp // 2 + along, 4)
    return chip * 2 + lax.rem(fsdp, 2)


def core_partner():
    fsdp = lax.axis_index("fsdp")
    return fsdp // 2 * 2 + 1 - lax.rem(fsdp, 2)


def send(src, dst, send_sem, recv_sem, device):
    copy = pltpu.make_async_remote_copy(
        src_ref=src,
        dst_ref=dst,
        send_sem=send_sem,
        recv_sem=recv_sem,
        device_id=device,
        device_id_type=MESH,
    )
    copy.start()
    return copy


def greet():
    barrier = pltpu.get_barrier_semaphore()
    for place in ((1, 0), (3, 0), (0, 1)):
        for device in ({"tp": tp_at(*place)}, {"fsdp": fsdp_at(*place)}):
            pl.semaphore_signal(barrier, inc=1, device_id=device, device_id_type=MESH)
    pl.semaphore_signal(barrier, inc=1, device_id={"fsdp": core_partner()}, device_id_type=MESH)
    pl.semaphore_wait(barrier, 7)


def dma(count):
    return pltpu.SemaphoreType.DMA((count,))


GATHER = (
    ((0, 0), (0, 1), None),
    ((0, 0), (1, 0), None),
    ((0, 0), (3, 0), None),
    ((0, 1), (1, 0), 0),
    ((0, 1), (3, 0), 0),
    ((3, 0), (1, 0), 1),
    ((1, 1), (3, 0), 4),
)
ARRIVES = ((0, 1), (3, 0), (1, 0), (3, 1), (1, 1), (2, 0), (2, 1))
SUM = (
    ((2, 0), (1, 0), ()),
    ((2, 1), (3, 0), ()),
    ((1, 1), (1, 0), ()),
    ((3, 0), (3, 0), ()),
    ((1, 0), (1, 0), (0,)),
    ((3, 1), (3, 0), (1,)),
    ((0, 1), (0, 1), (2, 5)),
)
LAST = (3, 4, 6)
CORE_ORDER = tuple(block for block, _, _ in SUM) + ((0, 0),)


class GatherTp:
    def __init__(self, rows, columns):
        self.rows = rows
        self.out = jax.ShapeDtypeStruct((8 * rows, columns), BF16)
        self.out_space = pltpu.VMEM
        self.scratch = [dma(7), dma(7), pltpu.SemaphoreType.DMA(())]

    def run(self, src, out, send_sem, recv_sem, own_sem):
        def block(place):
            return out.at[pl.ds(pl.multiple_of(tp_at(*place) * self.rows, self.rows), self.rows)]

        own = pltpu.make_async_copy(src, block((0, 0)), own_sem)
        own.start()
        copies, arrived = [], set()
        for k, (place, target, after) in enumerate(GATHER):
            if after is not None and after not in arrived:
                yield
                copies[after].wait_recv()
                arrived.add(after)
            copies.append(
                send(
                    src if place == (0, 0) else block(place),
                    block(place),
                    send_sem.at[k],
                    recv_sem.at[k],
                    {"tp": tp_at(*target)},
                )
            )
        yield
        for k, copy in enumerate(copies):
            if k not in arrived:
                copy.wait_recv()
            copy.wait_send()
        own.wait()


class SumTp:
    def __init__(self, rows, columns):
        self.rows = rows
        self.out = jax.ShapeDtypeStruct((rows, columns), F32)
        self.out_space = pltpu.VMEM
        self.scratch = [dma(7), dma(7), pltpu.VMEM((7, rows, columns), BF16)]

    def run(self, src, out, send_sem, recv_sem, landed):
        def first(place):
            return pl.multiple_of(tp_at(*place) * self.rows, self.rows)

        def total(place, others, dst):
            start = first(place)

            @pl.loop(0, self.rows // 16)
            def _(i):
                at = pl.multiple_of(i * 16, 16)
                value = src[pl.ds(pl.multiple_of(start + at, 16), 16), :].astype(F32)
                for k in others:
                    value = value + landed[k, pl.ds(at, 16), :].astype(F32)
                dst[pl.ds(at, 16), :] = value.astype(dst.dtype)

        copies, arrived = [], set()
        for k, (place, target, others) in enumerate(SUM):
            if others:
                yield
                for other in others:
                    copies[other].wait_recv()
                    arrived.add(other)
                part = landed.at[others[0]]
                total(place, others, part)
            else:
                part = src.at[pl.ds(first(place), self.rows)]
            copies.append(
                send(part, landed.at[k], send_sem.at[k], recv_sem.at[k], {"tp": tp_at(*target)})
            )
        yield
        for k in LAST:
            copies[k].wait_recv()
        total((0, 0), LAST, out)
        for copy in copies:
            copy.wait_send()


class GatherFsdp:
    def __init__(self, experts, columns):
        self.out = jax.ShapeDtypeStruct((experts, D, columns), BF16)
        self.out_space = pl.ANY
        self.scratch = [dma(7), dma(7), dma(8), dma(8), pltpu.SemaphoreType.DMA(())]

    def run(self, src, out, send_sem, recv_sem, core_send, core_recv, own_sem):
        def block(place):
            return out.at[:, pl.ds(pl.multiple_of(fsdp_at(*place) * BLOCK, BLOCK), BLOCK)]

        own = pltpu.make_async_copy(src, block((0, 0)), own_sem)
        own.start()
        copies, arrived, crossed = [], set(), []

        def arrive(k):
            copies[k].wait_recv()
            arrived.add(k)
            here = block(ARRIVES[k])
            crossed.append(
                send(here, here, core_send.at[k], core_recv.at[k], {"fsdp": core_partner()})
            )

        for k, (place, target, after) in enumerate(GATHER):
            if after is not None and after not in arrived:
                yield
                arrive(after)
            copies.append(
                send(
                    src if place == (0, 0) else block(place),
                    block(place),
                    send_sem.at[k],
                    recv_sem.at[k],
                    {"fsdp": fsdp_at(*target)},
                )
            )
        crossed.append(
            send(src, block((0, 0)), core_send.at[7], core_recv.at[7], {"fsdp": core_partner()})
        )
        yield
        for k in range(7):
            if k not in arrived:
                arrive(k)
        for copy in copies:
            copy.wait_send()
        for copy in crossed:
            copy.wait()
        own.wait()


class SumFsdp:
    def __init__(self, experts, columns, dtype=BF16):
        self.experts = experts
        self.out = jax.ShapeDtypeStruct((experts, BLOCK, columns), F32)
        self.out_space = pltpu.VMEM
        self.scratch = [
            dma(7),
            dma(7),
            dma(8),
            dma(8),
            pltpu.VMEM((8, experts, BLOCK, columns), dtype),
            pltpu.VMEM((7, experts, BLOCK, columns), dtype),
        ]

    def run(self, src, out, send_sem, recv_sem, core_send, core_recv, pair, landed):
        def over_rows(body):
            @pl.loop(0, self.experts * (BLOCK // 16))
            def _(i):
                body(i // (BLOCK // 16), pl.multiple_of(lax.rem(i, BLOCK // 16) * 16, 16))

        crossed, copies, arrived = [], [], set()
        mine = lax.rem(lax.axis_index("fsdp"), 2)
        for k, place in enumerate(CORE_ORDER):
            start = pl.multiple_of((fsdp_at(*place) + 1 - 2 * mine) * BLOCK, BLOCK)
            crossed.append(
                send(
                    src.at[:, pl.ds(start, BLOCK)],
                    pair.at[k],
                    core_send.at[k],
                    core_recv.at[k],
                    {"fsdp": core_partner()},
                )
            )
        for k, place in enumerate(CORE_ORDER):
            if k in (0, 4, 5, 6):
                yield
            others = SUM[k][2] if k < 7 else LAST
            crossed[k].wait_recv()
            for other in others:
                if other not in arrived:
                    copies[other].wait_recv()
                    arrived.add(other)
            start = fsdp_at(*place) * BLOCK
            if k == 7:
                for copy in copies + crossed:
                    copy.wait_send()
            dst = out if k == 7 else pair.at[k]

            def add(expert, at):
                rows = pl.ds(pl.multiple_of(start + at, 16), 16)
                value = src[expert, rows, :].astype(F32) + pair[k, expert, pl.ds(at, 16), :].astype(F32)
                for other in others:
                    value = value + landed[other, expert, pl.ds(at, 16), :].astype(F32)
                dst[expert, pl.ds(at, 16), :] = value.astype(dst.dtype)

            over_rows(add)
            if k < 7:
                copies.append(
                    send(
                        pair.at[k],
                        landed.at[k],
                        send_sem.at[k],
                        recv_sem.at[k],
                        {"fsdp": fsdp_at(*SUM[k][1])},
                    )
                )


class SumAll:
    def __init__(self, columns):
        self.over_fsdp = SumFsdp(1, columns, F32)
        self.out = jax.ShapeDtypeStruct((8, columns), F32)
        self.out_space = pltpu.VMEM
        self.scratch = self.over_fsdp.scratch + [
            pltpu.VMEM((1, BLOCK, columns), F32),
            dma(7),
            dma(7),
            pltpu.VMEM((7, 8, columns), F32),
        ]

    def run(self, src, out, *scratch):
        total, send_sem, recv_sem, landed = scratch[-4:]
        yield from self.over_fsdp.run(src, total, *scratch[:-4])

        def own(place):
            return total[0, pl.ds(pl.multiple_of(tp_at(*place) * 8, 8), 8), :]

        copies = []
        for k, (place, target, others) in enumerate(SUM):
            if others:
                yield
                value = own(place)
                for other in others:
                    copies[other].wait_recv()
                    value = value + landed[other]
                landed[others[0]] = value
                part = landed.at[others[0]]
            else:
                part = total.at[0, pl.ds(pl.multiple_of(tp_at(*place) * 8, 8), 8)]
            copies.append(
                send(part, landed.at[k], send_sem.at[k], recv_sem.at[k], {"tp": tp_at(*target)})
            )
        yield
        value = own((0, 0))
        for other in LAST:
            copies[other].wait_recv()
            value = value + landed[other]
        out[...] = value
        for copy in copies:
            copy.wait_send()


def together(runs):
    runs = list(runs)
    while runs:
        still = []
        for run in runs:
            try:
                next(run)
                still.append(run)
            except StopIteration:
                pass
        runs = still


def exchange(name, number, tasks, arrays):
    n = len(tasks)

    def body(*refs):
        sources, outs, scratch = refs[:n], refs[n : 2 * n], list(refs[2 * n :])
        greet()
        runs = []
        for task, source, out in zip(tasks, sources, outs):
            count = len(task.scratch)
            runs.append(task.run(source, out, *scratch[:count]))
            scratch = scratch[count:]
        together(runs)

    return pl.pallas_call(
        body,
        name=name,
        out_shape=[task.out for task in tasks],
        in_specs=[pl.BlockSpec(memory_space=pltpu.VMEM)] * n,
        out_specs=[pl.BlockSpec(memory_space=task.out_space) for task in tasks],
        scratch_shapes=[shape for task in tasks for shape in task.scratch],
        compiler_params=pltpu.CompilerParams(
            collective_id=number, has_side_effects=True, vmem_limit_bytes=48 * 2**20
        ),
    )(*arrays)


def dot(a, b, dims=((1,), (0,))):
    return lax.dot_general(a, b, (dims, ((), ())), preferred_element_type=F32)


def lanes(rows):
    return lax.broadcasted_iota(jnp.int32, (rows, 128), 1)


def turn(values):
    low_half = lax.rem(lanes(values.shape[0]), HEAD_DIM) < HEAD_DIM // 2
    return jnp.where(low_half, pltpu.roll(values, 96, 1), pltpu.roll(values, 32, 1))


def both_halves(pair):
    low = lanes(pair.shape[0]) < HEAD_DIM
    other = pltpu.roll(pair, HEAD_DIM, 1)
    return jnp.where(low, pair, other), jnp.where(low, other, pair)


def head_lanes(values, head):
    return jnp.where(lanes(values.shape[0]) // HEAD_DIM == head, values, 0.0)


def allowed(keys, first, queries, doc_column, doc_row):
    key_at = lax.broadcasted_iota(jnp.int32, (keys, queries), 0)
    query_at = first + lax.broadcasted_iota(jnp.int32, (keys, queries), 1)
    return (key_at <= query_at) & (doc_column[:keys, :] == doc_row[:, first : first + queries])


def unit_rows(values):
    return values * lax.rsqrt(jnp.mean(values * values, axis=-1, keepdims=True) + eps_norm)


QUERIES = 256


def attention_body(
    x_ref, w_ref, gain_ref, cos_q, sin_q, cos_k, sin_k, doc_column, doc_row,
    normed_ref, query_ref, pair_ref, lse_ref, mixed_ref, attended_ref, mixed_t,
):
    @pl.loop(0, GROUP // 128)
    def _(i):
        rows = pl.ds(pl.multiple_of(i * 128, 128), 128)
        normed = (unit_rows(x_ref[rows, :].astype(F32)) * gain_ref[...]).astype(BF16)
        normed_ref[rows, :] = normed
        raw = dot(normed, w_ref[:, 0:256])
        query, pair = raw[:, 0:128], raw[:, 128:256]
        query_ref[rows, :] = (query * cos_q[rows, :] + turn(query) * sin_q[rows, :]).astype(BF16)
        pair_ref[rows, :] = (pair * cos_k[rows, :] + turn(pair) * sin_k[rows, :]).astype(BF16)

    keys, values = both_halves(pair_ref[...].astype(F32))
    keys, values_t = keys.astype(BF16), values.T.astype(BF16)

    for first in range(0, GROUP, QUERIES):
        count = first + QUERIES
        mask = allowed(count, first, QUERIES, doc_column, doc_row)
        parts = []
        for head in range(2):
            query = head_lanes(query_ref[first : first + QUERIES, :].astype(F32), head).astype(BF16)
            scores = dot(keys[:count], query, ((1,), (1,))) * score_scale
            scores = jnp.where(mask, scores, -1e30)
            top = jnp.max(scores, axis=0, keepdims=True)
            raised = jnp.exp(scores - top)
            total = jnp.sum(raised, axis=0, keepdims=True)
            lse_ref[head : head + 1, first : first + QUERIES] = top + jnp.log(total)
            weights = (raised * (1.0 / total)).astype(BF16)
            parts.append(dot(values_t[HEAD_DIM * head : HEAD_DIM * (head + 1), :count], weights))
        for head in range(2):
            mixed_t[HEAD_DIM * head : HEAD_DIM * (head + 1), first : first + QUERIES] = parts[head]
    mixed_ref[...] = mixed_t[...].astype(BF16)

    @pl.loop(0, GROUP // 128)
    def _(i):
        at = pl.multiple_of(i * 128, 128)
        mixed = mixed_t[:, pl.ds(at, 128)].T.astype(BF16)
        attended_ref[pl.ds(at, 128), :] = dot(mixed, w_ref[:, 256:384], ((1,), (1,))).astype(BF16)


def attention(x, w, gain, tables, doc_column, doc_row):
    return pl.pallas_call(
        attention_body,
        name="attention",
        out_shape=[
            jax.ShapeDtypeStruct((GROUP, D), BF16),
            jax.ShapeDtypeStruct((GROUP, 128), BF16),
            jax.ShapeDtypeStruct((GROUP, 128), BF16),
            jax.ShapeDtypeStruct((2, GROUP), F32),
            jax.ShapeDtypeStruct((128, GROUP), BF16),
            jax.ShapeDtypeStruct((GROUP, D), BF16),
        ],
        scratch_shapes=[pltpu.VMEM((128, GROUP), F32)],
        compiler_params=pltpu.CompilerParams(vmem_limit_bytes=48 * 2**20),
    )(x, w, gain, *tables, doc_column, doc_row)


def attention_back_body(
    datt_ref, x_ref, normed_ref, w_ref, query_ref, pair_ref, lse_ref, mixed_ref,
    cos_q, sin_q, cos_k, sin_k, doc_column, doc_row,
    grad_ref, weights_ref, gain_ref, dmixed_ref, dquery_t, dpair_ref, raw_ref, raw_t,
):
    @pl.loop(0, GROUP // 128)
    def _(i):
        rows = pl.ds(pl.multiple_of(i * 128, 128), 128)
        dmixed_ref[rows, :] = dot(datt_ref[rows, :], w_ref[:, 256:384]).astype(BF16)

    keys, values = both_halves(pair_ref[...].astype(F32))
    keys_t = keys.T.astype(BF16)
    keys, values = keys.astype(BF16), values.astype(BF16)
    dpair_ref[...] = jnp.zeros_like(dpair_ref)

    for first in range(0, GROUP, QUERIES):
        count = first + QUERIES
        mask = allowed(count, first, QUERIES, doc_column, doc_row)
        for head in range(2):
            query = head_lanes(query_ref[first : first + QUERIES, :].astype(F32), head).astype(BF16)
            dmixed = head_lanes(dmixed_ref[first : first + QUERIES, :].astype(F32), head).astype(BF16)
            scores = dot(keys[:count], query, ((1,), (1,))) * score_scale
            scores = jnp.where(mask, scores, -1e30)
            weights = jnp.exp(scores - lse_ref[head : head + 1, first : first + QUERIES])
            dweights = dot(values[:count], dmixed, ((1,), (1,)))
            inner = jnp.sum(weights * dweights, axis=0, keepdims=True)
            dscores = (weights * (dweights - inner)).astype(BF16)
            dquery_t[HEAD_DIM * head : HEAD_DIM * (head + 1), first : first + QUERIES] = (
                dot(keys_t[HEAD_DIM * head : HEAD_DIM * (head + 1), :count], dscores) * score_scale
            )
            dpair_ref[0, :count, :] += dot(dscores, query) * score_scale
            dpair_ref[1, :count, :] += dot(weights.astype(BF16), dmixed)

    gain_ref[...] = jnp.zeros_like(gain_ref)

    @pl.loop(0, GROUP // 128)
    def _(i):
        at = pl.multiple_of(i * 128, 128)
        rows = pl.ds(at, 128)
        dquery = dquery_t[:, rows].T
        dkey, dvalue = dpair_ref[0, rows, :], dpair_ref[1, rows, :]
        dkey = dkey + pltpu.roll(dkey, HEAD_DIM, 1)
        dvalue = dvalue + pltpu.roll(dvalue, HEAD_DIM, 1)
        dpair = jnp.where(lanes(128) < HEAD_DIM, dkey, dvalue)
        dquery = dquery * cos_q[rows, :] + turn(dquery * sin_q[rows, :])
        dpair = dpair * cos_k[rows, :] + turn(dpair * sin_k[rows, :])
        raw_ref[rows, 0:128] = dquery.astype(BF16)
        raw_ref[rows, 128:256] = dpair.astype(BF16)
        raw_t[0:128, rows] = dquery.T.astype(BF16)
        raw_t[128:256, rows] = dpair.T.astype(BF16)
        dnormed = dot(raw_ref[rows, :], w_ref[:, 0:256], ((1,), (1,)))
        grad_ref[rows, :] = dnormed.astype(BF16)
        unit = unit_rows(x_ref[rows, :].astype(F32))
        gain_ref[...] += jnp.sum(dnormed * unit, axis=0, keepdims=True)

    @pl.loop(0, D // 256)
    def _(i):
        at = pl.ds(pl.multiple_of(i * 256, 256), 256)
        weights_ref[at, 0:256] = dot(raw_t[...], normed_ref[:, at]).T.astype(BF16)
        weights_ref[at, 256:384] = dot(mixed_ref[...], datt_ref[:, at]).T.astype(BF16)


def attention_back(datt, x, normed, w, query, pair, lse, mixed, tables, doc_column, doc_row):
    return pl.pallas_call(
        attention_back_body,
        name="attention_back",
        out_shape=[
            jax.ShapeDtypeStruct((GROUP, D), BF16),
            jax.ShapeDtypeStruct((D, 384), BF16),
            jax.ShapeDtypeStruct((1, D), F32),
        ],
        scratch_shapes=[
            pltpu.VMEM((GROUP, 128), BF16),
            pltpu.VMEM((128, GROUP), F32),
            pltpu.VMEM((2, GROUP, 128), F32),
            pltpu.VMEM((GROUP, 256), BF16),
            pltpu.VMEM((256, GROUP), BF16),
        ],
        compiler_params=pltpu.CompilerParams(vmem_limit_bytes=48 * 2**20),
    )(datt, x, normed, w, query, pair, lse, mixed, *tables, doc_column, doc_row)


def experts_body(
    tp_ref, tokens_ref, dy_ref, router_ref, chosen_ref, rank_row, rank_column,
    gate_ref, up_ref, down_ref,
    combined_ref, grad_ref, gate_grad, up_grad, down_grad, combined_sum, grad_sum, gate_sum, gates_ref,
):
    step = pl.program_id(0)
    lane = lax.broadcasted_iota(jnp.int32, (1, 128), 1)

    @pl.when(step == 0)
    def _():
        combined_sum[...] = jnp.zeros_like(combined_sum)
        grad_sum[...] = jnp.zeros_like(grad_sum)
        gate_sum[...] = jnp.zeros_like(gate_sum)
        logits = jnp.where(chosen_ref[...] > 0, dot(tokens_ref[...], router_ref[...]), -1e30)
        raised = jnp.exp(logits - jnp.max(logits, axis=-1, keepdims=True))
        gates = raised / jnp.sum(raised, axis=-1, keepdims=True)
        high = gates.astype(BF16)
        gates_ref[:, 0:128] = high
        gates_ref[:, 128:256] = (gates - high.astype(F32)).astype(BF16)

    expert_lane = lane == tp_ref[0] * LOCAL + step
    slot = lax.broadcasted_iota(jnp.int32, (SLOTS, GROUP), 0)
    take = jnp.where(slot == rank_row[0], 1.0, 0.0).astype(BF16)
    slot_gates = dot(take, gates_ref[...])
    slot_gates = slot_gates[:, 0:128] + slot_gates[:, 128:256]
    slot_gate = jnp.sum(jnp.where(expert_lane, slot_gates, 0.0), axis=1, keepdims=True)
    picked = dot(take, tokens_ref[...]).astype(BF16)
    dy = dot(take, dy_ref[...]).astype(BF16)

    gate_part = dot(picked, gate_ref[0])
    up_part = dot(picked, up_ref[0])
    sigmoid = 1.0 / (1.0 + jnp.exp(-gate_part))
    silu = gate_part * sigmoid
    hidden = silu * up_part
    dhidden = dot(dy, down_ref[0])
    dgate = jnp.sum(hidden * dhidden, axis=1, keepdims=True)
    weighted = (hidden * slot_gate).astype(BF16)
    dhidden = dhidden * slot_gate
    dgate_part = (dhidden * up_part * (sigmoid * (1.0 + gate_part * (1.0 - sigmoid)))).astype(BF16)
    dup_part = (dhidden * silu).astype(BF16)

    down_grad[0] = dot(dy, weighted, ((0,), (0,))).astype(BF16)
    gate_grad[0] = dot(picked, dgate_part, ((0,), (0,))).astype(BF16)
    up_grad[0] = dot(picked, dup_part, ((0,), (0,))).astype(BF16)

    out = dot(weighted, down_ref[0], ((1,), (1,))).astype(BF16)
    dpicked = dot(dgate_part, gate_ref[0], ((1,), (1,)))
    dpicked = (dpicked + dot(dup_part, up_ref[0], ((1,), (1,)))).astype(BF16)
    dgate = jnp.where(expert_lane, dgate, 0.0).astype(BF16)

    give = jnp.where(
        lax.broadcasted_iota(jnp.int32, (GROUP, SLOTS), 1) == rank_column[0], 1.0, 0.0
    ).astype(BF16)
    combined_sum[...] += dot(give, out)
    grad_sum[...] += dot(give, dpicked)
    gate_sum[...] += dot(give, dgate)

    @pl.when(step == LOCAL - 1)
    def _():
        combined_ref[...] = combined_sum[...].astype(BF16)
        grad_ref[:, 0:D] = grad_sum[...].astype(BF16)
        grad_ref[:, D:WIDE] = gate_sum[...].astype(BF16)


def experts(tp, tokens, dy, router, chosen, rank_row, rank_column, gate, up, down):
    def whole(*shape):
        return pl.BlockSpec(shape, lambda i, tp: (0,) * len(shape))

    def own(*shape):
        return pl.BlockSpec((1,) + shape, lambda i, tp: (i,) + (0,) * len(shape))

    weight = jax.ShapeDtypeStruct((LOCAL, D, HIDDEN), BF16)
    return pl.pallas_call(
        experts_body,
        name="experts",
        grid_spec=pltpu.PrefetchScalarGridSpec(
            num_scalar_prefetch=1,
            grid=(LOCAL,),
            in_specs=[
                whole(GROUP, D),
                whole(GROUP, D),
                whole(D, 128),
                whole(GROUP, 128),
                own(1, GROUP),
                own(GROUP, 1),
                own(D, HIDDEN),
                own(D, HIDDEN),
                own(D, HIDDEN),
            ],
            out_specs=[
                whole(GROUP, D),
                whole(GROUP, WIDE),
                own(D, HIDDEN),
                own(D, HIDDEN),
                own(D, HIDDEN),
            ],
            scratch_shapes=[
                pltpu.VMEM((GROUP, D), F32),
                pltpu.VMEM((GROUP, D), F32),
                pltpu.VMEM((GROUP, 128), F32),
                pltpu.VMEM((GROUP, 256), BF16),
            ],
        ),
        out_shape=[
            jax.ShapeDtypeStruct((GROUP, D), BF16),
            jax.ShapeDtypeStruct((GROUP, WIDE), BF16),
            weight,
            weight,
            weight,
        ],
        compiler_params=pltpu.CompilerParams(vmem_limit_bytes=60 * 2**20),
    )(tp, tokens, dy, router, chosen, rank_row, rank_column, gate, up, down)


def doc_layout(lengths_row):
    seq_ends = jnp.cumsum(lengths_row)
    positions = jnp.arange(GROUP, dtype=jnp.int32)
    doc_index = jnp.sum((positions[:, None] >= seq_ends[None, :]).astype(jnp.int32), axis=1)
    starts = seq_ends - lengths_row
    match = doc_index[:, None] == jnp.arange(SEQS, dtype=jnp.int32)[None, :]
    doc_start = jnp.sum(jnp.where(match, starts[None, :], 0), axis=1)
    return (doc_index, positions - doc_start)


def rope_tables(offset):
    lane = jnp.arange(128, dtype=jnp.int32)
    frequency = rope_base ** (-(lane % 32).astype(F32) * 2.0 / HEAD_DIM)
    angles = offset.astype(F32)[:, None] * frequency[None, :]
    cosine, sine = jnp.cos(angles), jnp.sin(angles)
    sine = jnp.where(lane % 64 < 32, -sine, sine)
    key = lane < HEAD_DIM
    return (cosine, sine, jnp.where(key, cosine, 1.0), jnp.where(key, sine, 0.0))


def rms_parts(values, gain):
    inverse = lax.rsqrt(jnp.mean(values * values, axis=-1, keepdims=True) + eps_norm)
    unit = values * inverse
    return (unit * gain, unit, inverse)


def rms_back(grad_out, unit, inverse, gain):
    grad_unit = grad_out * gain
    return inverse * (grad_unit - unit * jnp.mean(grad_unit * unit, axis=-1, keepdims=True))


def per_device(
    inputs,
    lengths,
    routes,
    attn_gain,
    query_weight,
    key_weight,
    value_weight,
    output_weight,
    moe_gain,
    router_weight,
    gate_weight,
    up_weight,
    down_weight,
    cotangent,
):
    tp = lax.axis_index("tp")
    small = jnp.concatenate(
        [
            query_weight,
            key_weight,
            value_weight,
            output_weight.T,
            router_weight,
            attn_gain[:, None],
            moe_gain[:, None],
            jnp.zeros((BLOCK, 128 - EXPERTS - 2), BF16),
        ],
        axis=1,
    )
    x_all, weights, gate_all = exchange(
        "exchange_inputs",
        1,
        [GatherTp(ROWS, D), GatherFsdp(1, 512), GatherFsdp(LOCAL, HIDDEN)],
        [inputs, small[None], gate_weight],
    )
    weights = weights[0]
    gain_one = weights[:, 416].astype(F32)[None, :]
    gain_two = weights[:, 417].astype(F32)[None, :]
    router_all = weights[:, 384:416]

    doc_index, offset = doc_layout(lengths[0])
    tables = rope_tables(offset)
    doc_column, doc_row = doc_index[:, None], doc_index[None, :]
    normed, query, pair, lse, mixed, attended = attention(
        x_all, weights, gain_one, tables, doc_column, doc_row
    )
    attended, up_all = exchange(
        "exchange_attended",
        2,
        [SumTp(ROWS, D), GatherFsdp(LOCAL, HIDDEN)],
        [attended, up_weight],
    )
    middle = inputs.astype(F32) + attended
    normed_two, unit_two, inverse_two = rms_parts(middle, gain_two)
    normed_two = normed_two.astype(BF16)
    tokens, down_all = exchange(
        "exchange_tokens",
        3,
        [GatherTp(ROWS, D), GatherFsdp(LOCAL, HIDDEN)],
        [normed_two, down_weight.transpose(0, 2, 1)],
    )

    expert_ids = jnp.arange(128, dtype=jnp.int32)
    chosen = jnp.any(routes[:, :, None] == expert_ids[None, None, :], axis=1)
    positions = jnp.arange(GROUP, dtype=jnp.int32)
    until = (positions[:, None] >= positions[None, :]).astype(BF16)
    running = jnp.dot(until, chosen.astype(BF16), preferred_element_type=F32).astype(jnp.int32)
    rank = jnp.where(chosen, running - 1, -1)
    rank = lax.dynamic_slice_in_dim(rank, tp * LOCAL, LOCAL, 1).T
    dy_all = lax.all_gather(cotangent, "tp", axis=0, tiled=True)
    router_wide = jnp.pad(router_all, ((0, 0), (0, 128 - EXPERTS)))
    combined, grads, gate_grad, up_grad, down_grad = experts(
        tp[None],
        tokens,
        dy_all,
        router_wide,
        chosen.astype(jnp.int32),
        rank[:, None, :],
        rank[:, :, None],
        gate_all,
        up_all,
        down_all,
    )
    grads, gate_grad = exchange(
        "exchange_expert_grads",
        4,
        [SumTp(ROWS, WIDE), SumFsdp(LOCAL, HIDDEN)],
        [grads, gate_grad],
    )
    chosen_own = lax.dynamic_slice_in_dim(chosen, tp * ROWS, ROWS, 0)
    logits = jnp.dot(normed_two, router_wide, preferred_element_type=F32)
    gates = jax.nn.softmax(jnp.where(chosen_own, logits, -1e30), axis=-1)
    dgates = grads[:, D:]
    dlogits = gates * (dgates - jnp.sum(gates * dgates, axis=-1, keepdims=True))
    dlogits = dlogits.astype(BF16)
    dnormed_two = grads[:, :D] + jnp.einsum(
        "te,de->td", dlogits, router_wide, preferred_element_type=F32
    )
    router_grad = jnp.einsum("td,te->de", normed_two, dlogits, preferred_element_type=F32)
    moe_gain_grad = jnp.sum(dnormed_two * unit_two, axis=0)
    dmiddle = cotangent.astype(F32) + rms_back(dnormed_two, unit_two, inverse_two, gain_two)
    datt, up_grad, moe_out = exchange(
        "exchange_attended_grads",
        5,
        [GatherTp(ROWS, D), SumFsdp(LOCAL, HIDDEN), SumTp(ROWS, D)],
        [dmiddle.astype(BF16), up_grad, combined],
    )
    outputs = (middle + moe_out).astype(BF16)
    dnormed, attention_grads, attn_gain_grad = attention_back(
        datt, x_all, normed, weights, query, pair, lse, mixed, tables, doc_column, doc_row
    )
    small_grads = jnp.where(
        expert_ids[None, :] == EXPERTS,
        moe_gain_grad[:, None],
        jnp.where(expert_ids[None, :] == EXPERTS + 1, attn_gain_grad[0][:, None], router_grad),
    )
    dnormed, down_grad, attention_grads, small_grads = exchange(
        "exchange_input_grads",
        6,
        [SumTp(ROWS, D), SumFsdp(LOCAL, HIDDEN), SumFsdp(1, 384), SumAll(128)],
        [dnormed, down_grad, attention_grads[None], small_grads[None]],
    )
    _, unit_one, inverse_one = rms_parts(inputs.astype(F32), gain_one)
    input_grad = dmiddle + rms_back(dnormed, unit_one, inverse_one, gain_one)
    attention_grads = attention_grads[0]
    return (
        outputs,
        input_grad,
        small_grads[:, EXPERTS + 1],
        attention_grads[:, 0:128],
        attention_grads[:, 128:192],
        attention_grads[:, 192:256],
        attention_grads[:, 256:384].T,
        small_grads[:, EXPERTS],
        small_grads[:, :EXPERTS],
        gate_grad,
        up_grad,
        down_grad.transpose(0, 2, 1),
    )


def solution(mesh):
    return jax.shard_map(
        per_device,
        mesh=mesh,
        in_specs=(
            P(("fsdp", "tp"), None),
            P("fsdp", None),
            P("fsdp", None),
            P("fsdp"),
            P("fsdp", "tp"),
            P("fsdp", "tp"),
            P("fsdp", "tp"),
            P("tp", "fsdp"),
            P("fsdp"),
            P("fsdp", None),
            P("tp", "fsdp", None),
            P("tp", "fsdp", None),
            P("tp", None, "fsdp"),
            P(("fsdp", "tp"), None),
        ),
        out_specs=(
            P(("fsdp", "tp"), None),
            P(("fsdp", "tp"), None),
            P(("fsdp", "tp")),
            P("fsdp", "tp"),
            P("fsdp", "tp"),
            P("fsdp", "tp"),
            P("tp", "fsdp"),
            P(("fsdp", "tp")),
            P(("fsdp", "tp"), None),
            P("tp", "fsdp", None),
            P("tp", "fsdp", None),
            P("tp", None, "fsdp"),
        ),
        check_vma=False,
    )
```

```python
import jax
import jax.numpy as jnp
from jax import lax
from jax.experimental import pallas as pl
from jax.experimental.pallas import tpu as pltpu
from jax.sharding import PartitionSpec as P

MESH = pl.DeviceIdType.MESH
D = 1024
HEAD_DIM = 64
EXPERTS = 32
HIDDEN = 512
GROUP = 1024
ROWS = 128
SLOTS = 352
LOCAL = 4
BLOCK = 64
WIDE = D + 128

eps_norm = 1e-06
rope_base = 10000.0
score_scale = 1.0 / HEAD_DIM
F32 = jnp.float32
BF16 = jnp.bfloat16


def tp_at(along, across):
    tp = lax.axis_index("tp")
    return lax.rem(tp // 2 + along, 4) * 2 + lax.rem(tp + across, 2)


def fsdp_at(along, across):
    fsdp = lax.axis_index("fsdp")
    chip = lax.rem(fsdp // 8 + across, 2) * 4 + lax.rem(fsdp // 2 + along, 4)
    return chip * 2 + lax.rem(fsdp, 2)


def core_partner():
    fsdp = lax.axis_index("fsdp")
    return fsdp // 2 * 2 + 1 - lax.rem(fsdp, 2)


def send(src, dst, send_sem, recv_sem, device):
    copy = pltpu.make_async_remote_copy(
        src_ref=src,
        dst_ref=dst,
        send_sem=send_sem,
        recv_sem=recv_sem,
        device_id=device,
        device_id_type=MESH,
    )
    copy.start()
    return copy


def greet():
    barrier = pltpu.get_barrier_semaphore()
    for place in ((1, 0), (3, 0), (0, 1)):
        for device in ({"tp": tp_at(*place)}, {"fsdp": fsdp_at(*place)}):
            pl.semaphore_signal(barrier, inc=1, device_id=device, device_id_type=MESH)
    pl.semaphore_signal(barrier, inc=1, device_id={"fsdp": core_partner()}, device_id_type=MESH)
    pl.semaphore_wait(barrier, 7)


def dma(count):
    return pltpu.SemaphoreType.DMA((count,))


GATHER = (
    ((0, 0), (0, 1), None),
    ((0, 0), (1, 0), None),
    ((0, 0), (3, 0), None),
    ((0, 1), (1, 0), 0),
    ((0, 1), (3, 0), 0),
    ((3, 0), (1, 0), 1),
    ((1, 1), (3, 0), 4),
)
ARRIVES = ((0, 1), (3, 0), (1, 0), (3, 1), (1, 1), (2, 0), (2, 1))
SUM = (
    ((2, 0), (1, 0), ()),
    ((2, 1), (3, 0), ()),
    ((1, 1), (1, 0), ()),
    ((3, 0), (3, 0), ()),
    ((1, 0), (1, 0), (0,)),
    ((3, 1), (3, 0), (1,)),
    ((0, 1), (0, 1), (2, 5)),
)
LAST = (3, 4, 6)
CORE_ORDER = tuple(block for block, _, _ in SUM) + ((0, 0),)


class GatherTp:
    def __init__(self, rows, columns):
        self.rows = rows
        self.scratch = [dma(7), dma(7), pltpu.SemaphoreType.DMA(())]

    def run(self, src, out, send_sem, recv_sem, own_sem):
        def block(place):
            return out.at[pl.ds(pl.multiple_of(tp_at(*place) * self.rows, self.rows), self.rows)]

        own = pltpu.make_async_copy(src, block((0, 0)), own_sem)
        own.start()
        copies, arrived = [], set()
        for k, (place, target, after) in enumerate(GATHER):
            if after is not None and after not in arrived:
                yield
                copies[after].wait_recv()
                arrived.add(after)
            copies.append(
                send(
                    src if place == (0, 0) else block(place),
                    block(place),
                    send_sem.at[k],
                    recv_sem.at[k],
                    {"tp": tp_at(*target)},
                )
            )
        yield
        for k, copy in enumerate(copies):
            if k not in arrived:
                copy.wait_recv()
            copy.wait_send()
        own.wait()


class SumTp:
    def __init__(self, rows, columns):
        self.rows = rows
        self.scratch = [dma(7), dma(7), pltpu.VMEM((7, rows, columns), BF16)]

    def run(self, src, out, send_sem, recv_sem, landed):
        def first(place):
            return pl.multiple_of(tp_at(*place) * self.rows, self.rows)

        def total(place, others, dst):
            start = first(place)

            @pl.loop(0, self.rows // 16)
            def _(i):
                at = pl.multiple_of(i * 16, 16)
                value = src[pl.ds(pl.multiple_of(start + at, 16), 16), :].astype(F32)
                for k in others:
                    value = value + landed[k, pl.ds(at, 16), :].astype(F32)
                dst[pl.ds(at, 16), :] = value.astype(dst.dtype)

        copies, arrived = [], set()
        for k, (place, target, others) in enumerate(SUM):
            if others:
                yield
                for other in others:
                    copies[other].wait_recv()
                    arrived.add(other)
                part = landed.at[others[0]]
                total(place, others, part)
            else:
                part = src.at[pl.ds(first(place), self.rows)]
            copies.append(
                send(part, landed.at[k], send_sem.at[k], recv_sem.at[k], {"tp": tp_at(*target)})
            )
        yield
        for k in LAST:
            copies[k].wait_recv()
        total((0, 0), LAST, out)
        for copy in copies:
            copy.wait_send()


class GatherFsdp:
    def __init__(self, experts, columns):
        self.scratch = [dma(7), dma(7), dma(8), dma(8), pltpu.SemaphoreType.DMA(())]

    def run(self, src, out, send_sem, recv_sem, core_send, core_recv, own_sem):
        def block(place):
            return out.at[:, pl.ds(pl.multiple_of(fsdp_at(*place) * BLOCK, BLOCK), BLOCK)]

        own = pltpu.make_async_copy(src, block((0, 0)), own_sem)
        own.start()
        copies, arrived, crossed = [], set(), []

        def arrive(k):
            copies[k].wait_recv()
            arrived.add(k)
            here = block(ARRIVES[k])
            crossed.append(
                send(here, here, core_send.at[k], core_recv.at[k], {"fsdp": core_partner()})
            )

        for k, (place, target, after) in enumerate(GATHER):
            if after is not None and after not in arrived:
                yield
                arrive(after)
            copies.append(
                send(
                    src if place == (0, 0) else block(place),
                    block(place),
                    send_sem.at[k],
                    recv_sem.at[k],
                    {"fsdp": fsdp_at(*target)},
                )
            )
        crossed.append(
            send(src, block((0, 0)), core_send.at[7], core_recv.at[7], {"fsdp": core_partner()})
        )
        for k in range(7):
            if k not in arrived:
                yield
                arrive(k)
        yield
        for copy in copies:
            copy.wait_send()
        for copy in crossed:
            copy.wait()
        own.wait()


class SumFsdp:
    def __init__(self, experts, columns, dtype=BF16):
        self.experts = experts
        self.scratch = [
            dma(7),
            dma(7),
            dma(8),
            dma(8),
            dma(8),
            pltpu.VMEM((8, experts, BLOCK, columns), dtype),
            pltpu.VMEM((8, experts, BLOCK, columns), dtype),
            pltpu.VMEM((7, experts, BLOCK, columns), dtype),
        ]

    def run(self, src, out, send_sem, recv_sem, core_send, core_recv, own_sem, own, pair, landed):
        def over_rows(body):
            @pl.loop(0, self.experts * (BLOCK // 16))
            def _(i):
                body(i // (BLOCK // 16), pl.multiple_of(lax.rem(i, BLOCK // 16) * 16, 16))

        crossed, copies, arrived, kept = [], [], set(), []
        mine = lax.rem(lax.axis_index("fsdp"), 2)
        for k, place in enumerate(CORE_ORDER):
            start = pl.multiple_of((fsdp_at(*place) + 1 - 2 * mine) * BLOCK, BLOCK)
            crossed.append(
                send(
                    src.at[:, pl.ds(start, BLOCK)],
                    pair.at[k],
                    core_send.at[k],
                    core_recv.at[k],
                    {"fsdp": core_partner()},
                )
            )
            start = pl.multiple_of(fsdp_at(*place) * BLOCK, BLOCK)
            kept.append(
                pltpu.make_async_copy(src.at[:, pl.ds(start, BLOCK)], own.at[k], own_sem.at[k])
            )
            kept[k].start()
        for k, place in enumerate(CORE_ORDER):
            yield
            others = SUM[k][2] if k < 7 else LAST
            crossed[k].wait_recv()
            for other in others:
                if other not in arrived:
                    copies[other].wait_recv()
                    arrived.add(other)
            kept[k].wait()
            dst = out if k == 7 else pair.at[k]

            def add(expert, at):
                rows = pl.ds(at, 16)
                value = own[k, expert, rows, :].astype(F32) + pair[k, expert, rows, :].astype(F32)
                for other in others:
                    value = value + landed[other, expert, pl.ds(at, 16), :].astype(F32)
                dst[expert, pl.ds(at, 16), :] = value.astype(dst.dtype)

            over_rows(add)
            if k < 7:
                copies.append(
                    send(
                        pair.at[k],
                        landed.at[k],
                        send_sem.at[k],
                        recv_sem.at[k],
                        {"fsdp": fsdp_at(*SUM[k][1])},
                    )
                )
        for copy in copies + crossed:
            copy.wait_send()


class SumAll:
    def __init__(self, columns):
        self.over_fsdp = SumFsdp(1, columns, F32)
        self.scratch = self.over_fsdp.scratch + [
            pltpu.VMEM((1, BLOCK, columns), F32),
            dma(7),
            dma(7),
            pltpu.VMEM((7, 8, columns), F32),
        ]

    def run(self, src, out, *scratch):
        total, send_sem, recv_sem, landed = scratch[-4:]
        yield from self.over_fsdp.run(src, total, *scratch[:-4])

        def own(place):
            return total[0, pl.ds(pl.multiple_of(tp_at(*place) * 8, 8), 8), :]

        copies = []
        for k, (place, target, others) in enumerate(SUM):
            if others:
                yield
                value = own(place)
                for other in others:
                    copies[other].wait_recv()
                    value = value + landed[other]
                landed[others[0]] = value
                part = landed.at[others[0]]
            else:
                part = total.at[0, pl.ds(pl.multiple_of(tp_at(*place) * 8, 8), 8)]
            copies.append(
                send(part, landed.at[k], send_sem.at[k], recv_sem.at[k], {"tp": tp_at(*target)})
            )
        yield
        value = own((0, 0))
        for other in LAST:
            copies[other].wait_recv()
            value = value + landed[other]
        out[...] = value
        for copy in copies:
            copy.wait_send()


def pump(runs):
    for run in list(runs):
        if next(run, "done") == "done":
            runs.remove(run)
    return bool(runs)


def drain(run, behind=(), steps=1):
    for _ in run:
        for _ in range(steps):
            pump(behind)


def run_task(task, scratch, src, out):
    count = len(task.scratch)
    mine, scratch[:] = scratch[:count], scratch[count:]
    return task.run(src, out, *mine)


def dot(a, b, dims=((1,), (0,))):
    return lax.dot_general(a, b, (dims, ((), ())), preferred_element_type=F32)


def lanes(rows):
    return lax.broadcasted_iota(jnp.int32, (rows, 128), 1)


def turn(values):
    low_half = lax.rem(lanes(values.shape[0]), HEAD_DIM) < HEAD_DIM // 2
    return jnp.where(low_half, pltpu.roll(values, 96, 1), pltpu.roll(values, 32, 1))


def both_halves(pair):
    low = lanes(pair.shape[0]) < HEAD_DIM
    other = pltpu.roll(pair, HEAD_DIM, 1)
    return jnp.where(low, pair, other), jnp.where(low, other, pair)


def head_lanes(values, head):
    return jnp.where(lanes(values.shape[0]) // HEAD_DIM == head, values, 0.0)


def doc_of(position, lengths):
    first = lengths[0, 0]
    return jnp.where(position >= first, 1, 0) + jnp.where(position >= first + lengths[0, 1], 1, 0)


def allowed(keys, first, lengths):
    key_at = lax.broadcasted_iota(jnp.int32, (keys, 1), 0)
    query_at = first + lax.broadcasted_iota(jnp.int32, (1, QUERIES), 1)
    return (key_at <= query_at) & (doc_of(key_at, lengths) == doc_of(query_at, lengths))


def inverse_root(values):
    return lax.rsqrt(jnp.mean(values * values, axis=-1, keepdims=True) + eps_norm)


def rms_back(grad_out, unit, inverse, gain):
    grad_unit = grad_out * gain
    return inverse * (grad_unit - unit * jnp.mean(grad_unit * unit, axis=-1, keepdims=True))


def key_tables(cosine, sine):
    key = lanes(cosine.shape[0]) < HEAD_DIM
    return jnp.where(key, cosine, 1.0), jnp.where(key, sine, 0.0)


QUERIES = 256


def attend(x_ref, w_ref, gain_ref, cos_ref, sin_ref, lengths, normed_ref, query_ref, pair_ref, lse_ref, mixed_ref, mixed_t, attended_ref, between):
    @pl.loop(0, GROUP // 128)
    def _(i):
        rows = pl.ds(pl.multiple_of(i * 128, 128), 128)
        x = x_ref[rows, :].astype(F32)
        normed = (x * inverse_root(x) * gain_ref[0:1, :]).astype(BF16)
        normed_ref[rows, :] = normed
        raw = dot(normed, w_ref[0, :, 0:256])
        query, pair = raw[:, 0:128], raw[:, 128:256]
        cosine, sine = cos_ref[rows, :], sin_ref[rows, :]
        query_ref[rows, :] = (query * cosine + turn(query) * sine).astype(BF16)
        cosine, sine = key_tables(cosine, sine)
        pair_ref[rows, :] = (pair * cosine + turn(pair) * sine).astype(BF16)

    between()
    keys, values = both_halves(pair_ref[...].astype(F32))
    keys, values_t = keys.astype(BF16), values.T.astype(BF16)

    for first in range(0, GROUP, QUERIES):
        count = first + QUERIES
        mask = allowed(count, first, lengths)
        for head in range(2):
            query = head_lanes(query_ref[first : first + QUERIES, :].astype(F32), head).astype(BF16)
            scores = dot(keys[:count], query, ((1,), (1,))) * score_scale
            scores = jnp.where(mask, scores, -1e30)
            top = jnp.max(scores, axis=0, keepdims=True)
            raised = jnp.exp(scores - top)
            total = jnp.sum(raised, axis=0, keepdims=True)
            lse_ref[head : head + 1, first : first + QUERIES] = top + jnp.log(total)
            weights = (raised * (1.0 / total)).astype(BF16)
            mixed_t[HEAD_DIM * head : HEAD_DIM * (head + 1), first : first + QUERIES] = dot(
                values_t[HEAD_DIM * head : HEAD_DIM * (head + 1), :count], weights
            )
        between()
    mixed_ref[...] = mixed_t[...].astype(BF16)

    @pl.loop(0, GROUP // 128)
    def _(i):
        at = pl.multiple_of(i * 128, 128)
        mixed = mixed_t[:, pl.ds(at, 128)].T.astype(BF16)
        attended_ref[pl.ds(at, 128), :] = dot(mixed, w_ref[0, :, 256:384], ((1,), (1,))).astype(BF16)


def attend_back(datt_ref, x_ref, w_ref, query_ref, pair_ref, lse_ref, cos_ref, sin_ref, lengths, grad_ref, gain_grad, dmixed_ref, dquery_t, dpair_ref, raw_ref, raw_t, between):
    @pl.loop(0, GROUP // 128)
    def _(i):
        rows = pl.ds(pl.multiple_of(i * 128, 128), 128)
        dmixed_ref[rows, :] = dot(datt_ref[rows, :], w_ref[0, :, 256:384]).astype(BF16)

    keys, values = both_halves(pair_ref[...].astype(F32))
    keys_t = keys.T.astype(BF16)
    keys, values = keys.astype(BF16), values.astype(BF16)
    dpair_ref[...] = jnp.zeros_like(dpair_ref)

    for first in range(0, GROUP, QUERIES):
        count = first + QUERIES
        mask = allowed(count, first, lengths)
        for head in range(2):
            query = head_lanes(query_ref[first : first + QUERIES, :].astype(F32), head).astype(BF16)
            dmixed = head_lanes(dmixed_ref[first : first + QUERIES, :].astype(F32), head).astype(BF16)
            scores = dot(keys[:count], query, ((1,), (1,))) * score_scale
            scores = jnp.where(mask, scores, -1e30)
            weights = jnp.exp(scores - lse_ref[head : head + 1, first : first + QUERIES])
            dweights = dot(values[:count], dmixed, ((1,), (1,)))
            inner = jnp.sum(weights * dweights, axis=0, keepdims=True)
            dscores = (weights * (dweights - inner)).astype(BF16)
            dquery_t[HEAD_DIM * head : HEAD_DIM * (head + 1), first : first + QUERIES] = (
                dot(keys_t[HEAD_DIM * head : HEAD_DIM * (head + 1), :count], dscores) * score_scale
            )
            dpair_ref[0, :count, :] += dot(dscores, query) * score_scale
            dpair_ref[1, :count, :] += dot(weights.astype(BF16), dmixed)
        between()

    gain_grad[...] = jnp.zeros_like(gain_grad)

    @pl.loop(0, GROUP // 128)
    def _(i):
        at = pl.multiple_of(i * 128, 128)
        rows = pl.ds(at, 128)
        dquery = dquery_t[:, rows].T
        dkey, dvalue = dpair_ref[0, rows, :], dpair_ref[1, rows, :]
        dkey = dkey + pltpu.roll(dkey, HEAD_DIM, 1)
        dvalue = dvalue + pltpu.roll(dvalue, HEAD_DIM, 1)
        dpair = jnp.where(lanes(128) < HEAD_DIM, dkey, dvalue)
        cosine, sine = cos_ref[rows, :], sin_ref[rows, :]
        dquery = dquery * cosine + turn(dquery * sine)
        cosine, sine = key_tables(cosine, sine)
        dpair = dpair * cosine + turn(dpair * sine)
        raw_ref[rows, 0:128] = dquery.astype(BF16)
        raw_ref[rows, 128:256] = dpair.astype(BF16)
        raw_t[0:128, rows] = dquery.T.astype(BF16)
        raw_t[128:256, rows] = dpair.T.astype(BF16)
        dnormed = dot(raw_ref[rows, :], w_ref[0, :, 0:256], ((1,), (1,)))
        grad_ref[rows, :] = dnormed.astype(BF16)
        x = x_ref[rows, :].astype(F32)
        gain_grad[...] += jnp.sum(dnormed * (x * inverse_root(x)), axis=0, keepdims=True)


HEAD_TASKS = (
    GatherTp(ROWS, D),
    GatherFsdp(1, 512),
    GatherFsdp(LOCAL, HIDDEN),
    GatherFsdp(LOCAL, HIDDEN),
    GatherFsdp(LOCAL, HIDDEN),
    GatherTp(ROWS, D),
    SumTp(ROWS, D),
    GatherTp(ROWS, D),
)


def head_body(
    lengths, x_ref, small_ref, gate_ref, up_ref, down_ref, dy_ref, routes_ref, cos_ref, sin_ref,
    x_all, w_all, gate_all, up_all, down_all, dy_all, tokens,
    normed_ref, query_ref, pair_ref, lse_ref, mixed_ref, middle_ref, own_ref, chosen_ref, rank_ref, rank_t, gains_ref,
    mixed_t, attended_ref, summed, *scratch,
):
    scratch = list(scratch)
    greet()
    pairs = (
        (x_ref, x_all), (small_ref, w_all), (gate_ref, gate_all), (up_ref, up_all), (down_ref, down_all),
        (dy_ref, dy_all), (attended_ref, summed), (own_ref, tokens),
    )
    x_run, w_run, gate_run, up_run, down_run, dy_run, sum_run, token_run = [
        run_task(task, scratch, *pair) for task, pair in zip(HEAD_TASKS, pairs)
    ]
    front = [x_run, w_run]
    pump(front)

    lane = lanes(GROUP)
    chosen = lane == routes_ref[:, 0:1]
    for k in range(1, 8):
        chosen = chosen | (lane == routes_ref[:, k : k + 1])
    chosen = jnp.where(chosen, 1.0, 0.0)
    chosen_ref[...] = chosen
    pump(front)
    chosen = chosen.astype(BF16)
    for i in range(4):
        rows = slice(256 * i, 256 * (i + 1))
        later = 256 * i + lax.broadcasted_iota(jnp.int32, (256, GROUP), 0)
        until = jnp.where(later >= lax.broadcasted_iota(jnp.int32, (256, GROUP), 1), 1.0, 0.0)
        running = dot(until.astype(BF16), chosen)
        rank = jnp.where(chosen_ref[rows, :] > 0.0, running - 1.0, -1.0)
        rank_ref[rows, :] = rank
        rank_t[:, rows] = rank.T
    drain(w_run)
    behind = [gate_run, up_run, down_run]
    pump(behind)
    gains_ref[...] = w_all[0, :, 384:512].astype(F32).T[32:40, :]
    drain(x_run)
    pump(behind)
    far = [dy_run]
    pump(far)
    calls = [0]

    def between():
        calls[0] += 1
        if calls[0] in (3, 4, 5):
            pump(far)
        if calls[0] in (2, 5):
            pump(behind)

    attend(
        x_all, w_all, gains_ref, cos_ref, sin_ref, lengths,
        normed_ref, query_ref, pair_ref, lse_ref, mixed_ref, mixed_t, attended_ref, between,
    )
    next(sum_run)
    while pump(far):
        pass
    drain(sum_run, behind)
    middle = x_ref[...].astype(F32) + summed[...]
    middle_ref[...] = middle
    own_ref[...] = (middle * inverse_root(middle) * gains_ref[1:2, :]).astype(BF16)
    drain(token_run, behind, 2)
    while pump(behind):
        pass


def head(lengths, x, small, gate, up, down, dy, routes, cosine, sine):
    def shape(*dims, dtype=BF16):
        return jax.ShapeDtypeStruct(dims, dtype)

    vmem = pl.BlockSpec(memory_space=pltpu.VMEM)
    far = pl.BlockSpec(memory_space=pl.ANY)
    weight = shape(LOCAL, D, HIDDEN)
    return pl.pallas_call(
        head_body,
        name="head",
        out_shape=[
            shape(GROUP, D),
            shape(1, D, 512),
            weight,
            weight,
            weight,
            shape(GROUP, D),
            shape(GROUP, D),
            shape(GROUP, D),
            shape(GROUP, 128),
            shape(GROUP, 128),
            shape(2, GROUP, dtype=F32),
            shape(128, GROUP),
            shape(ROWS, D, dtype=F32),
            shape(ROWS, D),
            shape(GROUP, 128, dtype=F32),
            shape(GROUP, 128, dtype=F32),
            shape(128, GROUP, dtype=F32),
            shape(8, D, dtype=F32),
        ],
        in_specs=[pl.BlockSpec(memory_space=pltpu.SMEM)] + [vmem] * 9,
        out_specs=[vmem] * 2 + [far] * 3 + [vmem] * 13,
        scratch_shapes=[
            pltpu.VMEM((128, GROUP), F32),
            pltpu.VMEM((GROUP, D), BF16),
            pltpu.VMEM((ROWS, D), F32),
        ]
        + [buffer for task in HEAD_TASKS for buffer in task.scratch],
        compiler_params=pltpu.CompilerParams(
            collective_id=1, has_side_effects=True, vmem_limit_bytes=56 * 2**20
        ),
    )(lengths, x, small, gate, up, down, dy, routes, cosine, sine)


TAIL_TASKS = (
    SumTp(ROWS, WIDE),
    SumFsdp(LOCAL, HIDDEN),
    SumFsdp(LOCAL, HIDDEN),
    SumFsdp(LOCAL, HIDDEN),
    GatherTp(ROWS, D),
    SumTp(ROWS, D),
    SumTp(ROWS, D),
    SumFsdp(1, 384),
    SumAll(128),
)


def tail_body(
    lengths, grads_ref, combined_ref, gate_part, up_part, down_part,
    x_ref, dy_ref, middle_ref, own_ref, chosen_ref, gains_ref,
    x_all, w_all, normed_ref, query_ref, pair_ref, lse_ref, mixed_ref, cos_ref, sin_ref,
    outputs_ref, input_grad, small_grad, attention_grad, gate_grad, up_grad, down_grad,
    grads_sum, moe_sum, datt_own, datt_all, dmiddle_ref, dnormed_part, dnormed_sum, weights_part, small_part, gain_grads,
    gain_row, dmixed_ref, dquery_t, dpair_ref, raw_ref, raw_t, *scratch,
):
    scratch = list(scratch)
    greet()
    pairs = (
        (grads_ref, grads_sum), (gate_part, gate_grad), (up_part, up_grad), (down_part, down_grad),
        (datt_own, datt_all), (combined_ref, moe_sum), (dnormed_part, dnormed_sum),
        (weights_part, attention_grad), (small_part, small_grad),
    )
    grads_run, gate_run, up_run, down_run, datt_run, moe_run, dnormed_run, weights_run, small_run = [
        run_task(task, scratch, *pair) for task, pair in zip(TAIL_TASKS, pairs)
    ]
    behind = [gate_run, up_run, down_run]
    next(grads_run)
    pump(behind)
    drain(grads_run, behind, 2)

    middle = middle_ref[...]
    inverse = inverse_root(middle)
    unit = middle * inverse
    router = w_all[0, :, 384:512]
    own_rows = pl.ds(pl.multiple_of(lax.axis_index("tp") * ROWS, ROWS), ROWS)
    logits = jnp.where(chosen_ref[own_rows, :] > 0.0, dot(own_ref[...], router), -1e30)
    raised = jnp.exp(logits - jnp.max(logits, axis=-1, keepdims=True))
    gates = raised / jnp.sum(raised, axis=-1, keepdims=True)
    dgates = grads_sum[:, D:WIDE]
    dlogits = gates * (dgates - jnp.sum(gates * dgates, axis=-1, keepdims=True))
    dlogits = dlogits.astype(BF16)
    dtokens = grads_sum[:, 0:D] + dot(dlogits, router, ((1,), (1,)))
    dmiddle = dy_ref[...].astype(F32) + rms_back(dtokens, unit, inverse, gains_ref[1:2, :])
    dmiddle_ref[...] = dmiddle
    datt_own[...] = dmiddle.astype(BF16)
    next(datt_run)
    small_part[0] = dot(own_ref[...], dlogits, ((0,), (0,)))
    gain_grads[...] = jnp.zeros_like(gain_grads)
    gain_grads[EXPERTS : EXPERTS + 1, :] = jnp.sum(dtokens * unit, axis=0, keepdims=True)
    drain(datt_run, behind)

    far = [moe_run]
    pump(far)
    calls = [0]

    def between():
        calls[0] += 1
        if calls[0] in (2, 4):
            pump(far)
        if calls[0] in (1, 3):
            pump(behind)

    attend_back(
        datt_all, x_all, w_all, query_ref, pair_ref, lse_ref, cos_ref, sin_ref, lengths,
        dnormed_part, gain_row, dmixed_ref, dquery_t, dpair_ref, raw_ref, raw_t, between,
    )
    next(dnormed_run)
    gain_grads[EXPERTS + 1 : EXPERTS + 2, :] = gain_row[...]
    small_part[0] += gain_grads[...].T
    next(small_run)

    @pl.loop(0, D // 256)
    def _(i):
        at = pl.ds(pl.multiple_of(i * 256, 256), 256)
        weights_part[0, at, 0:256] = dot(raw_t[...], normed_ref[:, at]).T.astype(BF16)
        weights_part[0, at, 256:384] = dot(mixed_ref[...], datt_all[:, at]).T.astype(BF16)

    last = [dnormed_run, weights_run, small_run] + far + behind
    while pump(last):
        pass
    outputs_ref[...] = (middle_ref[...] + moe_sum[...]).astype(BF16)
    x = x_ref[...].astype(F32)
    inverse = inverse_root(x)
    input_grad[...] = dmiddle_ref[...] + rms_back(dnormed_sum[...], x * inverse, inverse, gains_ref[0:1, :])


def tail(*arrays):
    def shape(*dims, dtype=F32):
        return jax.ShapeDtypeStruct(dims, dtype)

    vmem = pl.BlockSpec(memory_space=pltpu.VMEM)
    far = pl.BlockSpec(memory_space=pl.ANY)
    weight = shape(LOCAL, BLOCK, HIDDEN)
    return pl.pallas_call(
        tail_body,
        name="tail",
        out_shape=[
            shape(ROWS, D, dtype=BF16),
            shape(ROWS, D),
            shape(8, 128),
            shape(1, BLOCK, 384),
            weight,
            weight,
            weight,
        ],
        in_specs=[pl.BlockSpec(memory_space=pltpu.SMEM)] + [vmem] * 2 + [far] * 3 + [vmem] * 15,
        out_specs=[vmem] * 7,
        scratch_shapes=[
            pltpu.VMEM((ROWS, WIDE), F32),
            pltpu.VMEM((ROWS, D), F32),
            pltpu.VMEM((ROWS, D), BF16),
            pltpu.VMEM((GROUP, D), BF16),
            pltpu.VMEM((ROWS, D), F32),
            pltpu.VMEM((GROUP, D), BF16),
            pltpu.VMEM((ROWS, D), F32),
            pltpu.VMEM((1, D, 384), BF16),
            pltpu.VMEM((1, D, 128), F32),
            pltpu.VMEM((128, D), F32),
            pltpu.VMEM((1, D), F32),
            pltpu.VMEM((GROUP, 128), BF16),
            pltpu.VMEM((128, GROUP), F32),
            pltpu.VMEM((2, GROUP, 128), F32),
            pltpu.VMEM((GROUP, 256), BF16),
            pltpu.VMEM((256, GROUP), BF16),
        ]
        + [buffer for task in TAIL_TASKS for buffer in task.scratch],
        compiler_params=pltpu.CompilerParams(
            collective_id=2, has_side_effects=True, vmem_limit_bytes=62 * 2**20
        ),
    )(*arrays)


def experts_body(
    tp_ref, tokens_ref, dy_ref, router_ref, chosen_ref, rank_ref, rank_t,
    gate_ref, up_ref, down_ref,
    combined_ref, grad_ref, gate_grad, up_grad, down_grad, combined_sum, grad_sum, gate_sum, gates_ref,
):
    step = pl.program_id(0)
    lane = lax.broadcasted_iota(jnp.int32, (1, 128), 1)

    @pl.when(step == 0)
    def _():
        combined_sum[...] = jnp.zeros_like(combined_sum)
        grad_sum[...] = jnp.zeros_like(grad_sum)
        gate_sum[...] = jnp.zeros_like(gate_sum)
        logits = jnp.where(chosen_ref[...] > 0.0, dot(tokens_ref[...], router_ref[0]), -1e30)
        raised = jnp.exp(logits - jnp.max(logits, axis=-1, keepdims=True))
        gates = raised / jnp.sum(raised, axis=-1, keepdims=True)
        high = gates.astype(BF16)
        gates_ref[:, 0:128] = high
        gates_ref[:, 128:256] = (gates - high.astype(F32)).astype(BF16)

    expert = tp_ref[0] * LOCAL + step
    expert_lane = lane == expert
    slot = lax.broadcasted_iota(jnp.int32, (SLOTS, GROUP), 0)
    rank_row = rank_t[pl.ds(expert, 1), :].astype(jnp.int32)
    rank_column = jnp.sum(jnp.where(expert_lane, rank_ref[...], 0.0), axis=1, keepdims=True)
    take = jnp.where(slot == rank_row, 1.0, 0.0).astype(BF16)
    slot_gates = dot(take, gates_ref[...])
    slot_gates = slot_gates[:, 0:128] + slot_gates[:, 128:256]
    slot_gate = jnp.sum(jnp.where(expert_lane, slot_gates, 0.0), axis=1, keepdims=True)
    picked = dot(take, tokens_ref[...]).astype(BF16)
    dy = dot(take, dy_ref[...]).astype(BF16)

    gate_part = dot(picked, gate_ref[0])
    up_part = dot(picked, up_ref[0])
    sigmoid = 1.0 / (1.0 + jnp.exp(-gate_part))
    silu = gate_part * sigmoid
    hidden = silu * up_part
    dhidden = dot(dy, down_ref[0])
    dgate = jnp.sum(hidden * dhidden, axis=1, keepdims=True)
    weighted = (hidden * slot_gate).astype(BF16)
    dhidden = dhidden * slot_gate
    dgate_part = (dhidden * up_part * (sigmoid * (1.0 + gate_part * (1.0 - sigmoid)))).astype(BF16)
    dup_part = (dhidden * silu).astype(BF16)

    down_grad[0] = dot(dy, weighted, ((0,), (0,))).astype(BF16)
    gate_grad[0] = dot(picked, dgate_part, ((0,), (0,))).astype(BF16)
    up_grad[0] = dot(picked, dup_part, ((0,), (0,))).astype(BF16)

    out = dot(weighted, down_ref[0], ((1,), (1,))).astype(BF16)
    dpicked = dot(dgate_part, gate_ref[0], ((1,), (1,)))
    dpicked = (dpicked + dot(dup_part, up_ref[0], ((1,), (1,)))).astype(BF16)
    dgate = jnp.where(expert_lane, dgate, 0.0).astype(BF16)

    give = jnp.where(
        lax.broadcasted_iota(jnp.int32, (GROUP, SLOTS), 1) == rank_column.astype(jnp.int32), 1.0, 0.0
    ).astype(BF16)
    combined_sum[...] += dot(give, out)
    grad_sum[...] += dot(give, dpicked)
    gate_sum[...] += dot(give, dgate)

    @pl.when(step == LOCAL - 1)
    def _():
        combined_ref[...] = combined_sum[...].astype(BF16)
        grad_ref[:, 0:D] = grad_sum[...].astype(BF16)
        grad_ref[:, D:WIDE] = gate_sum[...].astype(BF16)


def experts(tp, tokens, dy, router, chosen, rank, rank_t, gate, up, down):
    def whole(*shape):
        return pl.BlockSpec(shape, lambda i, tp: (0,) * len(shape))

    def own(*shape):
        return pl.BlockSpec((1,) + shape, lambda i, tp: (i,) + (0,) * len(shape))

    weight = jax.ShapeDtypeStruct((LOCAL, D, HIDDEN), BF16)
    return pl.pallas_call(
        experts_body,
        name="experts",
        grid_spec=pltpu.PrefetchScalarGridSpec(
            num_scalar_prefetch=1,
            grid=(LOCAL,),
            in_specs=[
                whole(GROUP, D),
                whole(GROUP, D),
                pl.BlockSpec((1, D, 128), lambda i, tp: (0, 0, 3)),
                whole(GROUP, 128),
                whole(GROUP, 128),
                whole(128, GROUP),
                own(D, HIDDEN),
                own(D, HIDDEN),
                own(D, HIDDEN),
            ],
            out_specs=[
                whole(GROUP, D),
                whole(GROUP, WIDE),
                own(D, HIDDEN),
                own(D, HIDDEN),
                own(D, HIDDEN),
            ],
            scratch_shapes=[
                pltpu.VMEM((GROUP, D), F32),
                pltpu.VMEM((GROUP, D), F32),
                pltpu.VMEM((GROUP, 128), F32),
                pltpu.VMEM((GROUP, 256), BF16),
            ],
        ),
        out_shape=[
            jax.ShapeDtypeStruct((GROUP, D), BF16),
            jax.ShapeDtypeStruct((GROUP, WIDE), BF16),
            weight,
            weight,
            weight,
        ],
        compiler_params=pltpu.CompilerParams(vmem_limit_bytes=60 * 2**20),
    )(tp, tokens, dy, router, chosen, rank, rank_t, gate, up, down)


def rope_tables(lengths):
    ends = jnp.cumsum(lengths)
    positions = jnp.arange(GROUP, dtype=jnp.int32)
    starts = jnp.where(positions >= ends[1], ends[1], jnp.where(positions >= ends[0], ends[0], 0))
    lane = jnp.arange(128, dtype=jnp.int32)
    frequency = rope_base ** (-(lane % 32).astype(F32) * 2.0 / HEAD_DIM)
    angles = (positions - starts).astype(F32)[:, None] * frequency[None, :]
    sine = jnp.sin(angles)
    return jnp.cos(angles), jnp.where(lane % 64 < 32, -sine, sine)


def per_device(
    inputs,
    lengths,
    routes,
    attn_gain,
    query_weight,
    key_weight,
    value_weight,
    output_weight,
    moe_gain,
    router_weight,
    gate_weight,
    up_weight,
    down_weight,
    cotangent,
):
    tp = lax.axis_index("tp")
    small = jnp.concatenate(
        [
            query_weight,
            key_weight,
            value_weight,
            output_weight.T,
            router_weight,
            attn_gain[:, None],
            moe_gain[:, None],
            jnp.zeros((BLOCK, 128 - EXPERTS - 2), BF16),
        ],
        axis=1,
    )
    cosine, sine = rope_tables(lengths[0])
    (
        x_all, w_all, gate_all, up_all, down_all, dy_all, tokens,
        normed, query, pair, lse, mixed, middle, own, chosen, rank, rank_t, gains,
    ) = head(
        lengths, inputs, small[None], gate_weight, up_weight, down_weight.transpose(0, 2, 1),
        cotangent, routes, cosine, sine,
    )
    combined, grads, gate_part, up_part, down_part = experts(
        tp[None], tokens, dy_all, w_all, chosen, rank, rank_t, gate_all, up_all, down_all
    )
    outputs, input_grad, small_grad, attention_grad, gate_grad, up_grad, down_grad = tail(
        lengths, grads, combined, gate_part, up_part, down_part,
        inputs, cotangent, middle, own, chosen, gains,
        x_all, w_all, normed, query, pair, lse, mixed, cosine, sine,
    )
    attention_grad = attention_grad[0]
    return (
        outputs,
        input_grad,
        small_grad[:, EXPERTS + 1],
        attention_grad[:, 0:128],
        attention_grad[:, 128:192],
        attention_grad[:, 192:256],
        attention_grad[:, 256:384].T,
        small_grad[:, EXPERTS],
        small_grad[:, :EXPERTS],
        gate_grad,
        up_grad,
        down_grad.transpose(0, 2, 1),
    )


def solution(mesh):
    return jax.shard_map(
        per_device,
        mesh=mesh,
        in_specs=(
            P(("fsdp", "tp"), None),
            P("fsdp", None),
            P("fsdp", None),
            P("fsdp"),
            P("fsdp", "tp"),
            P("fsdp", "tp"),
            P("fsdp", "tp"),
            P("tp", "fsdp"),
            P("fsdp"),
            P("fsdp", None),
            P("tp", "fsdp", None),
            P("tp", "fsdp", None),
            P("tp", None, "fsdp"),
            P(("fsdp", "tp"), None),
        ),
        out_specs=(
            P(("fsdp", "tp"), None),
            P(("fsdp", "tp"), None),
            P(("fsdp", "tp")),
            P("fsdp", "tp"),
            P("fsdp", "tp"),
            P("fsdp", "tp"),
            P("tp", "fsdp"),
            P(("fsdp", "tp")),
            P(("fsdp", "tp"), None),
            P("tp", "fsdp", None),
            P("tp", "fsdp", None),
            P("tp", None, "fsdp"),
        ),
        check_vma=False,
    )
```

```python
import math

import jax
import jax.numpy as jnp
from jax import lax
from jax.experimental import pallas as pl
from jax.experimental.pallas import tpu as pltpu
from jax.sharding import PartitionSpec as P

MESH = pl.DeviceIdType.MESH
D = 1024
HEAD_DIM = 64
EXPERTS = 32
HIDDEN = 512
GROUP = 1024
ROWS = 128
SLOTS = 352
LOCAL = 4
BLOCK = 64
WIDE = D + 128

eps_norm = 1e-06
rope_base = 10000.0
score_scale = 1.0 / HEAD_DIM
F32 = jnp.float32
BF16 = jnp.bfloat16


def tp_at(along, across):
    tp = lax.axis_index("tp")
    return lax.rem(tp // 2 + along, 4) * 2 + lax.rem(tp + across, 2)


def fsdp_at(along, across):
    fsdp = lax.axis_index("fsdp")
    chip = lax.rem(fsdp // 8 + across, 2) * 4 + lax.rem(fsdp // 2 + along, 4)
    return chip * 2 + lax.rem(fsdp, 2)


def core_partner():
    fsdp = lax.axis_index("fsdp")
    return fsdp // 2 * 2 + 1 - lax.rem(fsdp, 2)


def send(src, dst, send_sem, recv_sem, device):
    copy = pltpu.make_async_remote_copy(
        src_ref=src,
        dst_ref=dst,
        send_sem=send_sem,
        recv_sem=recv_sem,
        device_id=device,
        device_id_type=MESH,
    )
    copy.start()
    return copy


def greet():
    barrier = pltpu.get_barrier_semaphore()
    for place in ((1, 0), (3, 0), (0, 1)):
        for device in ({"tp": tp_at(*place)}, {"fsdp": fsdp_at(*place)}):
            pl.semaphore_signal(barrier, inc=1, device_id=device, device_id_type=MESH)
    pl.semaphore_signal(barrier, inc=1, device_id={"fsdp": core_partner()}, device_id_type=MESH)
    pl.semaphore_wait(barrier, 7)


def dma(count):
    return pltpu.SemaphoreType.DMA((count,))


GATHER = (
    ((0, 0), (0, 1), None),
    ((0, 0), (1, 0), None),
    ((0, 0), (3, 0), None),
    ((0, 1), (1, 0), 0),
    ((0, 1), (3, 0), 0),
    ((3, 0), (1, 0), 1),
    ((1, 1), (3, 0), 4),
)
ARRIVES = ((0, 1), (3, 0), (1, 0), (3, 1), (1, 1), (2, 0), (2, 1))
SUM = (
    ((2, 0), (1, 0), ()),
    ((2, 1), (3, 0), ()),
    ((1, 1), (1, 0), ()),
    ((3, 0), (3, 0), ()),
    ((1, 0), (1, 0), (0,)),
    ((3, 1), (3, 0), (1,)),
    ((0, 1), (0, 1), (2, 5)),
)
LAST = (3, 4, 6)
CORE_ORDER = tuple(block for block, _, _ in SUM) + ((0, 0),)


class GatherTp:
    def __init__(self, rows, columns):
        self.rows = rows
        self.scratch = [dma(7), dma(7), pltpu.SemaphoreType.DMA(())]

    def run(self, src, out, send_sem, recv_sem, own_sem):
        def block(place):
            return out.at[pl.ds(pl.multiple_of(tp_at(*place) * self.rows, self.rows), self.rows)]

        own = pltpu.make_async_copy(src, block((0, 0)), own_sem)
        own.start()
        copies, arrived = [], set()
        for k, (place, target, after) in enumerate(GATHER):
            if after is not None and after not in arrived:
                yield
                copies[after].wait_recv()
                arrived.add(after)
            copies.append(
                send(
                    src if place == (0, 0) else block(place),
                    block(place),
                    send_sem.at[k],
                    recv_sem.at[k],
                    {"tp": tp_at(*target)},
                )
            )
        yield
        for k, copy in enumerate(copies):
            if k not in arrived:
                copy.wait_recv()
            copy.wait_send()
        own.wait()


class SumTp:
    def __init__(self, rows, columns):
        self.rows = rows
        self.scratch = [dma(7), dma(7), pltpu.VMEM((7, rows, columns), BF16)]

    def run(self, src, out, send_sem, recv_sem, landed):
        def first(place):
            return pl.multiple_of(tp_at(*place) * self.rows, self.rows)

        def total(place, others, dst):
            start = first(place)

            @pl.loop(0, self.rows // 16)
            def _(i):
                at = pl.multiple_of(i * 16, 16)
                value = src[pl.ds(pl.multiple_of(start + at, 16), 16), :].astype(F32)
                for k in others:
                    value = value + landed[k, pl.ds(at, 16), :].astype(F32)
                dst[pl.ds(at, 16), :] = value.astype(dst.dtype)

        copies, arrived = [], set()
        for k, (place, target, others) in enumerate(SUM):
            if others:
                yield
                for other in others:
                    copies[other].wait_recv()
                    arrived.add(other)
                part = landed.at[others[0]]
                total(place, others, part)
            else:
                part = src.at[pl.ds(first(place), self.rows)]
            copies.append(
                send(part, landed.at[k], send_sem.at[k], recv_sem.at[k], {"tp": tp_at(*target)})
            )
        yield
        for k in LAST:
            copies[k].wait_recv()
        total((0, 0), LAST, out)
        for copy in copies:
            copy.wait_send()


class GatherFsdp:
    def __init__(self, experts, columns):
        self.scratch = [dma(7), dma(7), dma(8), dma(8), pltpu.SemaphoreType.DMA(())]

    def run(self, src, out, send_sem, recv_sem, core_send, core_recv, own_sem):
        def block(place):
            return out.at[:, pl.ds(pl.multiple_of(fsdp_at(*place) * BLOCK, BLOCK), BLOCK)]

        own = pltpu.make_async_copy(src, block((0, 0)), own_sem)
        own.start()
        copies, arrived, crossed = [], set(), []

        def arrive(k):
            copies[k].wait_recv()
            arrived.add(k)
            here = block(ARRIVES[k])
            crossed.append(
                send(here, here, core_send.at[k], core_recv.at[k], {"fsdp": core_partner()})
            )

        for k, (place, target, after) in enumerate(GATHER):
            if after is not None and after not in arrived:
                yield
                arrive(after)
            copies.append(
                send(
                    src if place == (0, 0) else block(place),
                    block(place),
                    send_sem.at[k],
                    recv_sem.at[k],
                    {"fsdp": fsdp_at(*target)},
                )
            )
        crossed.append(
            send(src, block((0, 0)), core_send.at[7], core_recv.at[7], {"fsdp": core_partner()})
        )
        for k in range(7):
            if k not in arrived:
                yield
                arrive(k)
        yield
        for copy in copies:
            copy.wait_send()
        for copy in crossed:
            copy.wait()
        own.wait()


class SumFsdp:
    def __init__(self, experts, columns, dtype=BF16):
        self.experts = experts
        self.scratch = [
            dma(7),
            dma(7),
            dma(8),
            dma(8),
            dma(8),
            pltpu.VMEM((8, experts, BLOCK, columns), dtype),
            pltpu.VMEM((8, experts, BLOCK, columns), dtype),
            pltpu.VMEM((7, experts, BLOCK, columns), dtype),
        ]

    def run(self, src, out, send_sem, recv_sem, core_send, core_recv, own_sem, own, pair, landed):
        def over_rows(body):
            @pl.loop(0, self.experts * (BLOCK // 16))
            def _(i):
                body(i // (BLOCK // 16), pl.multiple_of(lax.rem(i, BLOCK // 16) * 16, 16))

        crossed, copies, arrived, kept = [], [], set(), []
        mine = lax.rem(lax.axis_index("fsdp"), 2)
        for k, place in enumerate(CORE_ORDER):
            start = pl.multiple_of((fsdp_at(*place) + 1 - 2 * mine) * BLOCK, BLOCK)
            crossed.append(
                send(
                    src.at[:, pl.ds(start, BLOCK)],
                    pair.at[k],
                    core_send.at[k],
                    core_recv.at[k],
                    {"fsdp": core_partner()},
                )
            )
            start = pl.multiple_of(fsdp_at(*place) * BLOCK, BLOCK)
            kept.append(
                pltpu.make_async_copy(src.at[:, pl.ds(start, BLOCK)], own.at[k], own_sem.at[k])
            )
            kept[k].start()
        for k, place in enumerate(CORE_ORDER):
            yield
            others = SUM[k][2] if k < 7 else LAST
            crossed[k].wait_recv()
            for other in others:
                if other not in arrived:
                    copies[other].wait_recv()
                    arrived.add(other)
            kept[k].wait()
            dst = out if k == 7 else pair.at[k]

            def add(expert, at):
                rows = pl.ds(at, 16)
                value = own[k, expert, rows, :].astype(F32) + pair[k, expert, rows, :].astype(F32)
                for other in others:
                    value = value + landed[other, expert, pl.ds(at, 16), :].astype(F32)
                dst[expert, pl.ds(at, 16), :] = value.astype(dst.dtype)

            over_rows(add)
            if k < 7:
                copies.append(
                    send(
                        pair.at[k],
                        landed.at[k],
                        send_sem.at[k],
                        recv_sem.at[k],
                        {"fsdp": fsdp_at(*SUM[k][1])},
                    )
                )
        for copy in copies + crossed:
            copy.wait_send()


class SumChips:
    def __init__(self, kind):
        self.kind = kind
        self.scratch = [
            dma(7),
            dma(7),
            dma(4),
            pltpu.VMEM((4, LOCAL, BLOCK, HIDDEN), BF16),
            pltpu.VMEM((7, LOCAL, BLOCK, HIDDEN), BF16),
        ]

    def run(self, src, out, send_sem, recv_sem, own_sem, own, landed):
        def block(place):
            return src.at[:, self.kind, fsdp_at(*place) // 2]

        def total(k, others, dst):
            @pl.loop(0, LOCAL * (BLOCK // 16))
            def _(i):
                expert, at = i // (BLOCK // 16), pl.multiple_of(lax.rem(i, BLOCK // 16) * 16, 16)
                value = own[k, expert, pl.ds(at, 16), :].astype(F32)
                for other in others:
                    value = value + landed[other, expert, pl.ds(at, 16), :].astype(F32)
                dst[expert, pl.ds(at, 16), :] = value.astype(dst.dtype)

        copies, arrived, kept = [], set(), []
        for k, (place, target, others) in enumerate(SUM):
            if others:
                yield
                for other in others:
                    copies[other].wait_recv()
                kept[k - 4].wait()
                part = landed.at[others[0]]
                total(k - 4, others, part)
            else:
                part = block(place)
            copies.append(
                send(part, landed.at[k], send_sem.at[k], recv_sem.at[k], {"fsdp": fsdp_at(*target)})
            )
            if k == 3:
                for place in [place for place, _, _ in SUM[4:]] + [(0, 0)]:
                    j = len(kept)
                    kept.append(pltpu.make_async_copy(block(place), own.at[j], own_sem.at[j]))
                    kept[j].start()
        yield
        for k in LAST:
            copies[k].wait_recv()
        kept[3].wait()
        total(3, LAST, out)
        for copy in copies:
            copy.wait_send()


class SumAll:
    def __init__(self, columns):
        self.over_fsdp = SumFsdp(1, columns, F32)
        self.scratch = self.over_fsdp.scratch + [
            pltpu.VMEM((1, BLOCK, columns), F32),
            dma(7),
            dma(7),
            pltpu.VMEM((7, 8, columns), F32),
        ]

    def run(self, src, out, *scratch):
        total, send_sem, recv_sem, landed = scratch[-4:]
        yield from self.over_fsdp.run(src, total, *scratch[:-4])

        def own(place):
            return total[0, pl.ds(pl.multiple_of(tp_at(*place) * 8, 8), 8), :]

        copies = []
        for k, (place, target, others) in enumerate(SUM):
            if others:
                yield
                value = own(place)
                for other in others:
                    copies[other].wait_recv()
                    value = value + landed[other]
                landed[others[0]] = value
                part = landed.at[others[0]]
            else:
                part = total.at[0, pl.ds(pl.multiple_of(tp_at(*place) * 8, 8), 8)]
            copies.append(
                send(part, landed.at[k], send_sem.at[k], recv_sem.at[k], {"tp": tp_at(*target)})
            )
        yield
        value = own((0, 0))
        for other in LAST:
            copies[other].wait_recv()
            value = value + landed[other]
        out[...] = value
        for copy in copies:
            copy.wait_send()


def pump(runs):
    for run in list(runs):
        if next(run, "done") == "done":
            runs.remove(run)
    return bool(runs)


def drain(run, behind=(), steps=1):
    for _ in run:
        for _ in range(steps):
            pump(behind)


def run_task(task, scratch, src, out):
    count = len(task.scratch)
    mine, scratch[:] = scratch[:count], scratch[count:]
    return task.run(src, out, *mine)


def dot(a, b, dims=((1,), (0,))):
    return lax.dot_general(a, b, (dims, ((), ())), preferred_element_type=F32)


def lanes(rows):
    return lax.broadcasted_iota(jnp.int32, (rows, 128), 1)


def turn(values):
    low_half = lax.rem(lanes(values.shape[0]), HEAD_DIM) < HEAD_DIM // 2
    return jnp.where(low_half, pltpu.roll(values, 96, 1), pltpu.roll(values, 32, 1))


def both_halves(pair):
    low = lanes(pair.shape[0]) < HEAD_DIM
    other = pltpu.roll(pair, HEAD_DIM, 1)
    return jnp.where(low, pair, other), jnp.where(low, other, pair)


def head_lanes(values, head):
    return jnp.where(lanes(values.shape[0]) // HEAD_DIM == head, values, 0.0)


def doc_of(position, lengths):
    first = lengths[0, 0]
    return jnp.where(position >= first, 1, 0) + jnp.where(position >= first + lengths[0, 1], 1, 0)


def allowed(keys, first, lengths):
    key_at = lax.broadcasted_iota(jnp.int32, (keys, 1), 0)
    query_at = first + lax.broadcasted_iota(jnp.int32, (1, QUERIES), 1)
    return (key_at <= query_at) & (doc_of(key_at, lengths) == doc_of(query_at, lengths))


def inverse_root(values):
    return lax.rsqrt(jnp.mean(values * values, axis=-1, keepdims=True) + eps_norm)


def rms_back(grad_out, unit, inverse, gain):
    grad_unit = grad_out * gain
    return inverse * (grad_unit - unit * jnp.mean(grad_unit * unit, axis=-1, keepdims=True))


def key_tables(cosine, sine):
    key = lanes(cosine.shape[0]) < HEAD_DIM
    return jnp.where(key, cosine, 1.0), jnp.where(key, sine, 0.0)


QUERIES = 256


def attend(x_ref, w_ref, gain_ref, cos_ref, sin_ref, lengths, normed_ref, query_ref, pair_ref, lse_ref, mixed_ref, mixed_t, attended_ref, between):
    @pl.loop(0, GROUP // 128)
    def _(i):
        rows = pl.ds(pl.multiple_of(i * 128, 128), 128)
        x = x_ref[rows, :].astype(F32)
        normed = (x * inverse_root(x) * gain_ref[0:1, :]).astype(BF16)
        normed_ref[rows, :] = normed
        raw = dot(normed, w_ref[0, :, 0:256])
        query, pair = raw[:, 0:128], raw[:, 128:256]
        cosine, sine = cos_ref[rows, :], sin_ref[rows, :]
        query_ref[rows, :] = (query * cosine + turn(query) * sine).astype(BF16)
        cosine, sine = key_tables(cosine, sine)
        pair_ref[rows, :] = (pair * cosine + turn(pair) * sine).astype(BF16)

    between()
    keys, values = both_halves(pair_ref[...].astype(F32))
    keys, values_t = keys.astype(BF16), values.T.astype(BF16)

    for first in range(0, GROUP, QUERIES):
        count = first + QUERIES
        mask = allowed(count, first, lengths)
        for head in range(2):
            query = head_lanes(query_ref[first : first + QUERIES, :].astype(F32), head).astype(BF16)
            scores = dot(keys[:count], query, ((1,), (1,))) * score_scale
            scores = jnp.where(mask, scores, -1e30)
            top = jnp.max(scores, axis=0, keepdims=True)
            raised = jnp.exp(scores - top)
            total = jnp.sum(raised, axis=0, keepdims=True)
            lse_ref[head : head + 1, first : first + QUERIES] = top + jnp.log(total)
            weights = (raised * (1.0 / total)).astype(BF16)
            mixed_t[HEAD_DIM * head : HEAD_DIM * (head + 1), first : first + QUERIES] = dot(
                values_t[HEAD_DIM * head : HEAD_DIM * (head + 1), :count], weights
            )
        between()
    mixed_ref[...] = mixed_t[...].astype(BF16)

    @pl.loop(0, GROUP // 128)
    def _(i):
        at = pl.multiple_of(i * 128, 128)
        mixed = mixed_t[:, pl.ds(at, 128)].T.astype(BF16)
        attended_ref[pl.ds(at, 128), :] = dot(mixed, w_ref[0, :, 256:384], ((1,), (1,))).astype(BF16)


def attend_back(datt_ref, x_ref, w_ref, query_ref, pair_ref, lse_ref, cos_ref, sin_ref, lengths, grad_ref, gain_grad, dmixed_ref, dquery_t, dpair_ref, raw_ref, raw_t, between):
    @pl.loop(0, GROUP // 128)
    def _(i):
        rows = pl.ds(pl.multiple_of(i * 128, 128), 128)
        dmixed_ref[rows, :] = dot(datt_ref[rows, :], w_ref[0, :, 256:384]).astype(BF16)

    keys, values = both_halves(pair_ref[...].astype(F32))
    keys_t = keys.T.astype(BF16)
    keys, values = keys.astype(BF16), values.astype(BF16)
    dpair_ref[...] = jnp.zeros_like(dpair_ref)

    for first in range(0, GROUP, QUERIES):
        count = first + QUERIES
        mask = allowed(count, first, lengths)
        for head in range(2):
            query = head_lanes(query_ref[first : first + QUERIES, :].astype(F32), head).astype(BF16)
            dmixed = head_lanes(dmixed_ref[first : first + QUERIES, :].astype(F32), head).astype(BF16)
            scores = dot(keys[:count], query, ((1,), (1,))) * score_scale
            scores = jnp.where(mask, scores, -1e30)
            weights = jnp.exp(scores - lse_ref[head : head + 1, first : first + QUERIES])
            dweights = dot(values[:count], dmixed, ((1,), (1,)))
            inner = jnp.sum(weights * dweights, axis=0, keepdims=True)
            dscores = (weights * (dweights - inner)).astype(BF16)
            dquery_t[HEAD_DIM * head : HEAD_DIM * (head + 1), first : first + QUERIES] = (
                dot(keys_t[HEAD_DIM * head : HEAD_DIM * (head + 1), :count], dscores) * score_scale
            )
            dpair_ref[0, :count, :] += dot(dscores, query) * score_scale
            dpair_ref[1, :count, :] += dot(weights.astype(BF16), dmixed)
        between()

    gain_grad[...] = jnp.zeros_like(gain_grad)

    @pl.loop(0, GROUP // 128)
    def _(i):
        at = pl.multiple_of(i * 128, 128)
        rows = pl.ds(at, 128)
        dquery = dquery_t[:, rows].T
        dkey, dvalue = dpair_ref[0, rows, :], dpair_ref[1, rows, :]
        dkey = dkey + pltpu.roll(dkey, HEAD_DIM, 1)
        dvalue = dvalue + pltpu.roll(dvalue, HEAD_DIM, 1)
        dpair = jnp.where(lanes(128) < HEAD_DIM, dkey, dvalue)
        cosine, sine = cos_ref[rows, :], sin_ref[rows, :]
        dquery = dquery * cosine + turn(dquery * sine)
        cosine, sine = key_tables(cosine, sine)
        dpair = dpair * cosine + turn(dpair * sine)
        raw_ref[rows, 0:128] = dquery.astype(BF16)
        raw_ref[rows, 128:256] = dpair.astype(BF16)
        raw_t[0:128, rows] = dquery.T.astype(BF16)
        raw_t[128:256, rows] = dpair.T.astype(BF16)
        dnormed = dot(raw_ref[rows, :], w_ref[0, :, 0:256], ((1,), (1,)))
        grad_ref[rows, :] = dnormed.astype(BF16)
        x = x_ref[rows, :].astype(F32)
        gain_grad[...] += jnp.sum(dnormed * (x * inverse_root(x)), axis=0, keepdims=True)


HEAD_TASKS = (
    GatherTp(ROWS, D),
    GatherFsdp(1, 512),
    GatherFsdp(LOCAL, HIDDEN),
    GatherFsdp(LOCAL, HIDDEN),
    GatherFsdp(LOCAL, HIDDEN),
    GatherTp(ROWS, D),
    SumTp(ROWS, D),
    GatherTp(ROWS, D),
)


def head_body(
    lengths, x_ref, small_ref, gate_ref, up_ref, down_ref, dy_ref, routes_ref,
    x_all, w_all, gate_all, up_all, down_all, dy_all, tokens,
    normed_ref, query_ref, pair_ref, lse_ref, mixed_ref, middle_ref, own_ref, chosen_ref, rank_ref, rank_t, gains_ref, cos_ref, sin_ref,
    mixed_t, attended_ref, summed, *scratch,
):
    scratch = list(scratch)
    greet()
    pairs = (
        (x_ref, x_all), (small_ref, w_all), (gate_ref, gate_all), (up_ref, up_all), (down_ref, down_all),
        (dy_ref, dy_all), (attended_ref, summed), (own_ref, tokens),
    )
    x_run, w_run, gate_run, up_run, down_run, dy_run, sum_run, token_run = [
        run_task(task, scratch, *pair) for task, pair in zip(HEAD_TASKS, pairs)
    ]
    front = [x_run, w_run]
    pump(front)

    lane = lanes(GROUP)
    routes = routes_ref[...].astype(F32).T.astype(jnp.int32)
    chosen = lane == routes[:, 0:1]
    for k in range(1, 8):
        chosen = chosen | (lane == routes[:, k : k + 1])
    chosen = jnp.where(chosen, 1.0, 0.0)
    chosen_ref[...] = chosen
    pump(front)
    chosen = chosen.astype(BF16)
    for i in range(4):
        rows = slice(256 * i, 256 * (i + 1))
        later = 256 * i + lax.broadcasted_iota(jnp.int32, (256, GROUP), 0)
        until = jnp.where(later >= lax.broadcasted_iota(jnp.int32, (256, GROUP), 1), 1.0, 0.0)
        running = dot(until.astype(BF16), chosen)
        rank = jnp.where(chosen_ref[rows, :] > 0.0, running - 1.0, -1.0)
        rank_ref[rows, :] = rank
        rank_t[:, rows] = rank.T
    pump(front)
    position = lax.broadcasted_iota(jnp.int32, (GROUP, 1), 0)
    ends = (lengths[0, 0], lengths[0, 0] + lengths[0, 1])
    start = jnp.where(position >= ends[1], ends[1], jnp.where(position >= ends[0], ends[0], 0))
    half = lax.rem(lane[0:1], HEAD_DIM // 2).astype(F32)
    frequency = jnp.exp(half * (-2.0 / HEAD_DIM * math.log(rope_base)))
    angles = (position - start).astype(F32) * frequency
    cos_ref[...] = jnp.cos(angles)
    sine = jnp.sin(angles)
    sin_ref[...] = jnp.where(lax.rem(lane, HEAD_DIM) < HEAD_DIM // 2, -sine, sine)
    drain(w_run)
    behind = [gate_run, up_run, down_run]
    pump(behind)
    gains_ref[...] = w_all[0, :, 384:512].astype(F32).T[32:40, :]
    drain(x_run)
    pump(behind)
    far = [dy_run]
    pump(far)
    calls = [0]

    def between():
        calls[0] += 1
        if calls[0] in (3, 4, 5):
            pump(far)
        if calls[0] in (2, 5):
            pump(behind)

    attend(
        x_all, w_all, gains_ref, cos_ref, sin_ref, lengths,
        normed_ref, query_ref, pair_ref, lse_ref, mixed_ref, mixed_t, attended_ref, between,
    )
    next(sum_run)
    while pump(far):
        pass
    drain(sum_run)
    pump(behind)
    pump(behind)
    middle = x_ref[...].astype(F32) + summed[...]
    middle_ref[...] = middle
    own_ref[...] = (middle * inverse_root(middle) * gains_ref[1:2, :]).astype(BF16)
    drain(token_run, behind, 2)
    while pump(behind):
        pass


def head(lengths, x, small, gate, up, down, dy, routes):
    def shape(*dims, dtype=BF16):
        return jax.ShapeDtypeStruct(dims, dtype)

    vmem = pl.BlockSpec(memory_space=pltpu.VMEM)
    far = pl.BlockSpec(memory_space=pl.ANY)
    weight = shape(LOCAL, D, HIDDEN)
    return pl.pallas_call(
        head_body,
        name="head",
        out_shape=[
            shape(GROUP, D),
            shape(1, D, 512),
            weight,
            weight,
            weight,
            shape(GROUP, D),
            shape(GROUP, D),
            shape(GROUP, D),
            shape(GROUP, 128),
            shape(GROUP, 128),
            shape(2, GROUP, dtype=F32),
            shape(128, GROUP),
            shape(ROWS, D, dtype=F32),
            shape(ROWS, D),
            shape(GROUP, 128, dtype=F32),
            shape(GROUP, 128, dtype=F32),
            shape(128, GROUP, dtype=F32),
            shape(8, D, dtype=F32),
            shape(GROUP, 128, dtype=F32),
            shape(GROUP, 128, dtype=F32),
        ],
        in_specs=[pl.BlockSpec(memory_space=pltpu.SMEM)] + [vmem] * 7,
        out_specs=[vmem] * 2 + [far] * 3 + [vmem] * 15,
        scratch_shapes=[
            pltpu.VMEM((128, GROUP), F32),
            pltpu.VMEM((GROUP, D), BF16),
            pltpu.VMEM((ROWS, D), F32),
        ]
        + [buffer for task in HEAD_TASKS for buffer in task.scratch],
        compiler_params=pltpu.CompilerParams(
            collective_id=1, has_side_effects=True, vmem_limit_bytes=56 * 2**20
        ),
    )(lengths, x, small, gate, up, down, dy, routes)


TAIL_TASKS = (
    SumTp(ROWS, WIDE),
    SumChips(0),
    SumChips(1),
    SumChips(2),
    GatherTp(ROWS, D),
    SumTp(ROWS, D),
    SumTp(ROWS, D),
    SumFsdp(1, 384),
    SumAll(128),
)


def tail_body(
    lengths, grads_ref, combined_ref, pairs_ref,
    x_ref, dy_ref, middle_ref, own_ref, chosen_ref, gains_ref,
    x_all, w_all, normed_ref, query_ref, pair_ref, lse_ref, mixed_ref, cos_ref, sin_ref,
    outputs_ref, input_grad, small_grad, attention_grad, gate_grad, up_grad, down_grad,
    grads_sum, moe_sum, datt_own, datt_all, dmiddle_ref, dnormed_part, dnormed_sum, weights_part, small_part, gain_grads,
    gain_row, dmixed_ref, dquery_t, dpair_ref, raw_ref, raw_t, *scratch,
):
    scratch = list(scratch)
    greet()
    pairs = (
        (grads_ref, grads_sum), (pairs_ref, gate_grad), (pairs_ref, up_grad), (pairs_ref, down_grad),
        (datt_own, datt_all), (combined_ref, moe_sum), (dnormed_part, dnormed_sum),
        (weights_part, attention_grad), (small_part, small_grad),
    )
    grads_run, gate_run, up_run, down_run, datt_run, moe_run, dnormed_run, weights_run, small_run = [
        run_task(task, scratch, *pair) for task, pair in zip(TAIL_TASKS, pairs)
    ]
    behind = [gate_run, up_run, down_run]
    next(grads_run)
    pump(behind)
    drain(grads_run)

    middle = middle_ref[...]
    inverse = inverse_root(middle)
    unit = middle * inverse
    router = w_all[0, :, 384:512]
    own_rows = pl.ds(pl.multiple_of(lax.axis_index("tp") * ROWS, ROWS), ROWS)
    logits = jnp.where(chosen_ref[own_rows, :] > 0.0, dot(own_ref[...], router), -1e30)
    raised = jnp.exp(logits - jnp.max(logits, axis=-1, keepdims=True))
    gates = raised / jnp.sum(raised, axis=-1, keepdims=True)
    dgates = grads_sum[:, D:WIDE]
    dlogits = gates * (dgates - jnp.sum(gates * dgates, axis=-1, keepdims=True))
    dlogits = dlogits.astype(BF16)
    dtokens = grads_sum[:, 0:D] + dot(dlogits, router, ((1,), (1,)))
    dmiddle = dy_ref[...].astype(F32) + rms_back(dtokens, unit, inverse, gains_ref[1:2, :])
    dmiddle_ref[...] = dmiddle
    datt_own[...] = dmiddle.astype(BF16)
    next(datt_run)
    pump(behind)
    pump(behind)
    small_part[0] = dot(own_ref[...], dlogits, ((0,), (0,)))
    gain_grads[...] = jnp.zeros_like(gain_grads)
    gain_grads[EXPERTS : EXPERTS + 1, :] = jnp.sum(dtokens * unit, axis=0, keepdims=True)
    drain(datt_run)

    far = [moe_run]
    pump(far)
    calls = [0]

    def between():
        calls[0] += 1
        if calls[0] in (2, 4):
            pump(far)
        if calls[0] == 2:
            pump(behind)

    attend_back(
        datt_all, x_all, w_all, query_ref, pair_ref, lse_ref, cos_ref, sin_ref, lengths,
        dnormed_part, gain_row, dmixed_ref, dquery_t, dpair_ref, raw_ref, raw_t, between,
    )
    next(dnormed_run)
    gain_grads[EXPERTS + 1 : EXPERTS + 2, :] = gain_row[...]
    small_part[0] += gain_grads[...].T
    next(small_run)

    @pl.loop(0, D // 256)
    def _(i):
        at = pl.ds(pl.multiple_of(i * 256, 256), 256)
        weights_part[0, at, 0:256] = dot(raw_t[...], normed_ref[:, at]).T.astype(BF16)
        weights_part[0, at, 256:384] = dot(mixed_ref[...], datt_all[:, at]).T.astype(BF16)

    last = [dnormed_run, weights_run, small_run] + far + behind
    while pump(last):
        pass
    outputs_ref[...] = (middle_ref[...] + moe_sum[...]).astype(BF16)
    x = x_ref[...].astype(F32)
    inverse = inverse_root(x)
    input_grad[...] = dmiddle_ref[...] + rms_back(dnormed_sum[...], x * inverse, inverse, gains_ref[0:1, :])


def tail(*arrays):
    def shape(*dims, dtype=F32):
        return jax.ShapeDtypeStruct(dims, dtype)

    vmem = pl.BlockSpec(memory_space=pltpu.VMEM)
    far = pl.BlockSpec(memory_space=pl.ANY)
    weight = shape(LOCAL, BLOCK, HIDDEN)
    return pl.pallas_call(
        tail_body,
        name="tail",
        out_shape=[
            shape(ROWS, D, dtype=BF16),
            shape(ROWS, D),
            shape(8, 128),
            shape(1, BLOCK, 384),
            weight,
            weight,
            weight,
        ],
        in_specs=[pl.BlockSpec(memory_space=pltpu.SMEM)] + [vmem] * 2 + [far] + [vmem] * 15,
        out_specs=[vmem] * 7,
        scratch_shapes=[
            pltpu.VMEM((ROWS, WIDE), F32),
            pltpu.VMEM((ROWS, D), F32),
            pltpu.VMEM((ROWS, D), BF16),
            pltpu.VMEM((GROUP, D), BF16),
            pltpu.VMEM((ROWS, D), F32),
            pltpu.VMEM((GROUP, D), BF16),
            pltpu.VMEM((ROWS, D), F32),
            pltpu.VMEM((1, D, 384), BF16),
            pltpu.VMEM((1, D, 128), F32),
            pltpu.VMEM((128, D), F32),
            pltpu.VMEM((1, D), F32),
            pltpu.VMEM((GROUP, 128), BF16),
            pltpu.VMEM((128, GROUP), F32),
            pltpu.VMEM((2, GROUP, 128), F32),
            pltpu.VMEM((GROUP, 256), BF16),
            pltpu.VMEM((256, GROUP), BF16),
        ]
        + [buffer for task in TAIL_TASKS for buffer in task.scratch],
        compiler_params=pltpu.CompilerParams(
            collective_id=2, has_side_effects=True, vmem_limit_bytes=62 * 2**20
        ),
    )(*arrays)


def experts_body(
    tokens_ref, dy_ref, router_ref, chosen_ref, rank_ref, rank_t,
    gate_ref, up_ref, down_ref,
    combined_ref, grad_ref, pair_ref,
    combined_sum, grad_sum, gate_sum, gates_ref, parts, got, send_sem, recv_sem,
):
    step = pl.program_id(0)
    lane = lax.broadcasted_iota(jnp.int32, (1, 128), 1)
    core = lax.rem(lax.axis_index("fsdp"), 2)

    def across(expert):
        slot = lax.rem(expert, 2)
        return pltpu.make_async_remote_copy(
            src_ref=parts.at[slot, :, :, 1 - core],
            dst_ref=got.at[expert],
            send_sem=send_sem.at[slot],
            recv_sem=recv_sem.at[expert],
            device_id={"fsdp": core_partner()},
            device_id_type=MESH,
        )

    @pl.when(step == 0)
    def _():
        barrier = pltpu.get_barrier_semaphore()
        pl.semaphore_signal(barrier, inc=1, device_id={"fsdp": core_partner()}, device_id_type=MESH)
        pl.semaphore_wait(barrier, 1)
        combined_sum[...] = jnp.zeros_like(combined_sum)
        grad_sum[...] = jnp.zeros_like(grad_sum)
        gate_sum[...] = jnp.zeros_like(gate_sum)
        logits = jnp.where(chosen_ref[...] > 0.0, dot(tokens_ref[...], router_ref[0]), -1e30)
        raised = jnp.exp(logits - jnp.max(logits, axis=-1, keepdims=True))
        gates = raised / jnp.sum(raised, axis=-1, keepdims=True)
        high = gates.astype(BF16)
        gates_ref[:, 0:128] = high
        gates_ref[:, 128:256] = (gates - high.astype(F32)).astype(BF16)

    @pl.when(step < LOCAL)
    def _():
        expert = lax.axis_index("tp") * LOCAL + step
        expert_lane = lane == expert
        slot = lax.broadcasted_iota(jnp.int32, (SLOTS, GROUP), 0)
        rank_row = rank_t[pl.ds(expert, 1), :].astype(jnp.int32)
        rank_column = jnp.sum(jnp.where(expert_lane, rank_ref[...], 0.0), axis=1, keepdims=True)
        take = jnp.where(slot == rank_row, 1.0, 0.0).astype(BF16)
        slot_gates = dot(take, gates_ref[...])
        slot_gates = slot_gates[:, 0:128] + slot_gates[:, 128:256]
        slot_gate = jnp.sum(jnp.where(expert_lane, slot_gates, 0.0), axis=1, keepdims=True)
        picked = dot(take, tokens_ref[...]).astype(BF16)
        dy = dot(take, dy_ref[...]).astype(BF16)

        gate_part = dot(picked, gate_ref[0])
        up_part = dot(picked, up_ref[0])
        sigmoid = 1.0 / (1.0 + jnp.exp(-gate_part))
        silu = gate_part * sigmoid
        hidden = silu * up_part
        dhidden = dot(dy, down_ref[0])
        dgate = jnp.sum(hidden * dhidden, axis=1, keepdims=True)
        weighted = (hidden * slot_gate).astype(BF16)
        dhidden = dhidden * slot_gate
        dgate_part = (dhidden * up_part * (sigmoid * (1.0 + gate_part * (1.0 - sigmoid)))).astype(BF16)
        dup_part = (dhidden * silu).astype(BF16)

        @pl.when(step >= 2)
        def _():
            across(step - 2).wait_send()

        slot_now = lax.rem(step, 2)
        for k, (left, right) in enumerate(((picked, dgate_part), (picked, dup_part), (dy, weighted))):
            grad = dot(left, right, ((0,), (0,))).astype(BF16)
            parts[slot_now, k] = grad.reshape(8, 2, BLOCK, HIDDEN)
        across(step).start()

        out = dot(weighted, down_ref[0], ((1,), (1,))).astype(BF16)
        dpicked = dot(dgate_part, gate_ref[0], ((1,), (1,)))
        dpicked = (dpicked + dot(dup_part, up_ref[0], ((1,), (1,)))).astype(BF16)
        dgate = jnp.where(expert_lane, dgate, 0.0).astype(BF16)

        give = jnp.where(
            lax.broadcasted_iota(jnp.int32, (GROUP, SLOTS), 1) == rank_column.astype(jnp.int32), 1.0, 0.0
        ).astype(BF16)
        combined_sum[...] += dot(give, out)
        grad_sum[...] += dot(give, dpicked)
        gate_sum[...] += dot(give, dgate)

    @pl.when(step == LOCAL)
    def _():
        combined_ref[...] = combined_sum[...].astype(BF16)
        grad_ref[:, 0:D] = grad_sum[...].astype(BF16)
        grad_ref[:, D:WIDE] = gate_sum[...].astype(BF16)

    @pl.when(step >= 1)
    def _():
        across(step - 1).wait_recv()
        slot_before = lax.rem(step - 1, 2)

        @pl.loop(0, 24)
        def _(i):
            kind, chip = i // 8, lax.rem(i, 8)
            total = parts[slot_before, kind, chip, core].astype(F32) + got[step - 1, kind, chip].astype(F32)
            pair_ref[0, kind, chip] = total.astype(BF16)

    @pl.when(step == LOCAL)
    def _():
        for expert in (LOCAL - 2, LOCAL - 1):
            across(expert).wait_send()


def experts(tokens, dy, router, chosen, rank, rank_t, gate, up, down):
    def whole(*shape):
        return pl.BlockSpec(shape, lambda i: (0,) * len(shape))

    def own(*shape):
        return pl.BlockSpec((1,) + shape, lambda i: (jnp.minimum(i, LOCAL - 1),) + (0,) * len(shape))

    return pl.pallas_call(
        experts_body,
        name="experts",
        grid=(LOCAL + 1,),
        in_specs=[
            whole(GROUP, D),
            whole(GROUP, D),
            pl.BlockSpec((1, D, 128), lambda i: (0, 0, 3)),
            whole(GROUP, 128),
            whole(GROUP, 128),
            whole(128, GROUP),
            own(D, HIDDEN),
            own(D, HIDDEN),
            own(D, HIDDEN),
        ],
        out_specs=[
            whole(GROUP, D),
            whole(GROUP, WIDE),
            pl.BlockSpec((1, 3, 8, BLOCK, HIDDEN), lambda i: (jnp.maximum(i - 1, 0), 0, 0, 0, 0)),
        ],
        scratch_shapes=[
            pltpu.VMEM((GROUP, D), F32),
            pltpu.VMEM((GROUP, D), F32),
            pltpu.VMEM((GROUP, 128), F32),
            pltpu.VMEM((GROUP, 256), BF16),
            pltpu.VMEM((2, 3, 8, 2, BLOCK, HIDDEN), BF16),
            pltpu.VMEM((LOCAL, 3, 8, BLOCK, HIDDEN), BF16),
            dma(2),
            dma(LOCAL),
        ],
        out_shape=[
            jax.ShapeDtypeStruct((GROUP, D), BF16),
            jax.ShapeDtypeStruct((GROUP, WIDE), BF16),
            jax.ShapeDtypeStruct((LOCAL, 3, 8, BLOCK, HIDDEN), BF16),
        ],
        compiler_params=pltpu.CompilerParams(
            collective_id=3, has_side_effects=True, vmem_limit_bytes=60 * 2**20
        ),
    )(tokens, dy, router, chosen, rank, rank_t, gate, up, down)


def finish_body(*refs):
    outputs, input_grad, small, attention, gate, up, down = refs[:7]
    outs = refs[7:]
    outs[0][...] = outputs[...]
    outs[1][...] = input_grad[...]
    outs[2][...] = attention[0, :, 0:128]
    outs[3][...] = attention[0, :, 128:192]
    outs[4][...] = attention[0, :, 192:256]
    outs[5][...] = attention[0, :, 256:384].T
    outs[6][...] = small[:, 0:EXPERTS]
    columns = small[...].T
    outs[7][...] = columns[EXPERTS + 1 : EXPERTS + 2, :]
    outs[8][...] = columns[EXPERTS : EXPERTS + 1, :]
    outs[9][...] = gate[...]
    outs[10][...] = up[...]
    outs[11][...] = down[...]


def finish(*arrays):
    def shape(*dims, dtype=F32):
        return jax.ShapeDtypeStruct(dims, dtype)

    vmem = pl.BlockSpec(memory_space=pltpu.VMEM)
    return pl.pallas_call(
        finish_body,
        name="finish",
        out_shape=[
            shape(ROWS, D, dtype=BF16),
            shape(ROWS, D),
            shape(BLOCK, 128),
            shape(BLOCK, BLOCK),
            shape(BLOCK, BLOCK),
            shape(128, BLOCK),
            shape(8, EXPERTS),
            shape(1, 8),
            shape(1, 8),
        ]
        + [shape(LOCAL, BLOCK, HIDDEN)] * 3,
        in_specs=[vmem] * 7,
        out_specs=[vmem] * 12,
        compiler_params=pltpu.CompilerParams(vmem_limit_bytes=32 * 2**20),
    )(*arrays)


def per_device(
    inputs,
    lengths,
    routes,
    attn_gain,
    query_weight,
    key_weight,
    value_weight,
    output_weight,
    moe_gain,
    router_weight,
    gate_weight,
    up_weight,
    down_weight,
    cotangent,
):
    small = jnp.concatenate(
        [
            query_weight,
            key_weight,
            value_weight,
            output_weight.T,
            router_weight,
            attn_gain[:, None],
            moe_gain[:, None],
            jnp.zeros((BLOCK, 128 - EXPERTS - 2), BF16),
        ],
        axis=1,
    )
    (
        x_all, w_all, gate_all, up_all, down_all, dy_all, tokens,
        normed, query, pair, lse, mixed, middle, own, chosen, rank, rank_t, gains, cosine, sine,
    ) = head(
        lengths, inputs, small[None], gate_weight, up_weight, down_weight.transpose(0, 2, 1),
        cotangent, routes.T,
    )
    combined, grads, pairs = experts(
        tokens, dy_all, w_all, chosen, rank, rank_t, gate_all, up_all, down_all
    )
    results = tail(
        lengths, grads, combined, pairs,
        inputs, cotangent, middle, own, chosen, gains,
        x_all, w_all, normed, query, pair, lse, mixed, cosine, sine,
    )
    (
        outputs, input_grad, query_grad, key_grad, value_grad, output_grad, router_grad, attn_gain_grad, moe_gain_grad,
        gate_grad, up_grad, down_grad,
    ) = finish(*results)
    return (
        outputs,
        input_grad,
        attn_gain_grad.reshape(8),
        query_grad,
        key_grad,
        value_grad,
        output_grad,
        moe_gain_grad.reshape(8),
        router_grad,
        gate_grad,
        up_grad,
        down_grad.transpose(0, 2, 1),
    )


def solution(mesh):
    return jax.shard_map(
        per_device,
        mesh=mesh,
        in_specs=(
            P(("fsdp", "tp"), None),
            P("fsdp", None),
            P("fsdp", None),
            P("fsdp"),
            P("fsdp", "tp"),
            P("fsdp", "tp"),
            P("fsdp", "tp"),
            P("tp", "fsdp"),
            P("fsdp"),
            P("fsdp", None),
            P("tp", "fsdp", None),
            P("tp", "fsdp", None),
            P("tp", None, "fsdp"),
            P(("fsdp", "tp"), None),
        ),
        out_specs=(
            P(("fsdp", "tp"), None),
            P(("fsdp", "tp"), None),
            P(("fsdp", "tp")),
            P("fsdp", "tp"),
            P("fsdp", "tp"),
            P("fsdp", "tp"),
            P("tp", "fsdp"),
            P(("fsdp", "tp")),
            P(("fsdp", "tp"), None),
            P("tp", "fsdp", None),
            P("tp", "fsdp", None),
            P("tp", None, "fsdp"),
        ),
        check_vma=False,
    )
```

```python
import functools
import math

import jax
import jax.numpy as jnp
from jax import lax
from jax.experimental import pallas as pl
from jax.experimental.pallas import tpu as pltpu
from jax.sharding import PartitionSpec as P

MESH = pl.DeviceIdType.MESH
D = 1024
HEAD_DIM = 64
EXPERTS = 32
HIDDEN = 512
GROUP = 1024
ROWS = 128
SLOTS = 352
PLACES = 384
LOCAL = 4
BLOCK = 64
WIDE = D + 128

eps_norm = 1e-06
rope_base = 10000.0
score_scale = 1.0 / HEAD_DIM
F32 = jnp.float32
BF16 = jnp.bfloat16


def tp_at(along, across):
    tp = lax.axis_index("tp")
    return lax.rem(tp // 2 + along, 4) * 2 + lax.rem(tp + across, 2)


def fsdp_at(along, across):
    fsdp = lax.axis_index("fsdp")
    chip = lax.rem(fsdp // 8 + across, 2) * 4 + lax.rem(fsdp // 2 + along, 4)
    return chip * 2 + lax.rem(fsdp, 2)


def core_partner():
    fsdp = lax.axis_index("fsdp")
    return fsdp // 2 * 2 + 1 - lax.rem(fsdp, 2)


def send(src, dst, send_sem, recv_sem, device):
    copy = pltpu.make_async_remote_copy(
        src_ref=src,
        dst_ref=dst,
        send_sem=send_sem,
        recv_sem=recv_sem,
        device_id=device,
        device_id_type=MESH,
    )
    copy.start()
    return copy


def greet():
    barrier = pltpu.get_barrier_semaphore()
    for place in EVERY:
        for device in ({"tp": tp_at(*place)}, {"fsdp": fsdp_at(*place)}):
            pl.semaphore_signal(barrier, inc=1, device_id=device, device_id_type=MESH)
    pl.semaphore_signal(barrier, inc=1, device_id={"fsdp": core_partner()}, device_id_type=MESH)
    pl.semaphore_wait(barrier, 15)


def dma(count):
    return pltpu.SemaphoreType.DMA((count,))


EVERY = ((2, 0), (2, 1), (1, 1), (3, 1), (1, 0), (3, 0), (0, 1))
GATHER = (
    ((0, 0), (0, 1), None),
    ((0, 0), (1, 0), None),
    ((0, 0), (3, 0), None),
    ((0, 1), (1, 0), 0),
    ((0, 1), (3, 0), 0),
    ((3, 0), (1, 0), 1),
    ((1, 1), (3, 0), 4),
)
ARRIVES = ((0, 1), (3, 0), (1, 0), (3, 1), (1, 1), (2, 0), (2, 1))
SUM = (
    ((2, 0), (1, 0), ()),
    ((2, 1), (3, 0), ()),
    ((1, 1), (1, 0), ()),
    ((3, 0), (3, 0), ()),
    ((1, 0), (1, 0), (0,)),
    ((3, 1), (3, 0), (1,)),
    ((0, 1), (0, 1), (2, 5)),
)
LAST = (3, 4, 6)


class GatherTp:
    def __init__(self, rows, columns):
        self.rows = rows
        self.scratch = [dma(7), dma(7), pltpu.SemaphoreType.DMA(())]

    def run(self, src, out, send_sem, recv_sem, own_sem):
        def block(place):
            return out.at[pl.ds(pl.multiple_of(tp_at(*place) * self.rows, self.rows), self.rows)]

        own = pltpu.make_async_copy(src, block((0, 0)), own_sem)
        own.start()
        copies, arrived = [], set()
        for k, (place, target, after) in enumerate(GATHER):
            if after is not None and after not in arrived:
                yield
                copies[after].wait_recv()
                arrived.add(after)
            copies.append(
                send(
                    src if place == (0, 0) else block(place),
                    block(place),
                    send_sem.at[k],
                    recv_sem.at[k],
                    {"tp": tp_at(*target)},
                )
            )
        yield
        for k, copy in enumerate(copies):
            if k not in arrived:
                copy.wait_recv()
            copy.wait_send()
        own.wait()


class SumTp:
    def __init__(self, rows, columns):
        self.rows = rows
        self.scratch = [dma(7), dma(7), pltpu.VMEM((7, rows, columns), BF16)]

    def run(self, src, out, send_sem, recv_sem, landed):
        def first(place):
            return pl.multiple_of(tp_at(*place) * self.rows, self.rows)

        def total(place, others, dst):
            start = first(place)

            @pl.loop(0, self.rows // 16)
            def _(i):
                at = pl.multiple_of(i * 16, 16)
                value = src[pl.ds(pl.multiple_of(start + at, 16), 16), :].astype(F32)
                for k in others:
                    value = value + landed[k, pl.ds(at, 16), :].astype(F32)
                dst[pl.ds(at, 16), :] = value.astype(dst.dtype)

        copies, arrived = [], set()
        for k, (place, target, others) in enumerate(SUM):
            if others:
                yield
                for other in others:
                    copies[other].wait_recv()
                    arrived.add(other)
                part = landed.at[others[0]]
                total(place, others, part)
            else:
                part = src.at[pl.ds(first(place), self.rows)]
            copies.append(
                send(part, landed.at[k], send_sem.at[k], recv_sem.at[k], {"tp": tp_at(*target)})
            )
        yield
        for k in LAST:
            copies[k].wait_recv()
        total((0, 0), LAST, out)
        for copy in copies:
            copy.wait_send()


class ExchangeTp:
    def __init__(self):
        self.scratch = [dma(7), dma(7), pltpu.SemaphoreType.DMA(())]

    def run(self, block, place, send_sem, recv_sem, own_sem):
        here = lax.axis_index("tp")
        copies = [
            send(block(peer), place(here), send_sem.at[k], recv_sem.at[k], {"tp": peer})
            for k, peer in enumerate(tp_at(*step) for step in EVERY)
        ]
        own = pltpu.make_async_copy(block(here), place(here), own_sem)
        own.start()
        yield
        for copy in copies:
            copy.wait()
        own.wait()


class GatherFsdp:
    def __init__(self, experts, columns):
        self.scratch = [dma(7), dma(7), dma(8), dma(8), pltpu.SemaphoreType.DMA(())]

    def run(self, src, out, send_sem, recv_sem, core_send, core_recv, own_sem):
        def block(place):
            return out.at[:, pl.ds(pl.multiple_of(fsdp_at(*place) * BLOCK, BLOCK), BLOCK)]

        own = pltpu.make_async_copy(src, block((0, 0)), own_sem)
        own.start()
        copies, arrived, crossed = [], set(), []

        def arrive(k):
            copies[k].wait_recv()
            arrived.add(k)
            here = block(ARRIVES[k])
            crossed.append(
                send(here, here, core_send.at[k], core_recv.at[k], {"fsdp": core_partner()})
            )

        for k, (place, target, after) in enumerate(GATHER):
            if after is not None and after not in arrived:
                yield
                arrive(after)
            copies.append(
                send(
                    src if place == (0, 0) else block(place),
                    block(place),
                    send_sem.at[k],
                    recv_sem.at[k],
                    {"fsdp": fsdp_at(*target)},
                )
            )
        crossed.append(
            send(src, block((0, 0)), core_send.at[7], core_recv.at[7], {"fsdp": core_partner()})
        )
        for k in range(7):
            if k not in arrived:
                yield
                arrive(k)
        yield
        for copy in copies:
            copy.wait_send()
        for copy in crossed:
            copy.wait()
        own.wait()


class SumFsdp:
    def __init__(self, columns, dtype):
        blocks = pltpu.VMEM((8, BLOCK, columns), dtype)
        self.scratch = [dma(7), dma(7), dma(2), blocks, blocks]

    def run(self, src, out, send_sem, recv_sem, core_sem, pair, landed):
        core = lax.rem(lax.axis_index("fsdp"), 2)
        across = send(
            src.at[:, 1 - core], pair, core_sem.at[0], core_sem.at[1], {"fsdp": core_partner()}
        )
        yield
        across.wait_recv()

        @pl.loop(0, 8)
        def _(chip):
            pair[chip] = (src[chip, core].astype(F32) + pair[chip].astype(F32)).astype(pair.dtype)

        copies = []
        for k, place in enumerate(EVERY):
            device = fsdp_at(*place)
            copies.append(
                send(pair.at[device // 2], landed.at[k], send_sem.at[k], recv_sem.at[k], {"fsdp": device})
            )
        yield
        value = pair[lax.axis_index("fsdp") // 2].astype(F32)
        for k, copy in enumerate(copies):
            copy.wait_recv()
            value = value + landed[k].astype(F32)
        out[...] = value
        across.wait_send()
        for copy in copies:
            copy.wait_send()


class SumChips:
    def __init__(self, kind):
        self.kind = kind
        self.scratch = [
            dma(7),
            dma(7),
            dma(4),
            pltpu.VMEM((4, LOCAL, BLOCK, HIDDEN), BF16),
            pltpu.VMEM((7, LOCAL, BLOCK, HIDDEN), BF16),
        ]

    def run(self, src, out, send_sem, recv_sem, own_sem, own, landed):
        def block(place):
            return src.at[:, self.kind, fsdp_at(*place) // 2]

        def total(k, others, dst):
            @pl.loop(0, LOCAL * (BLOCK // 16))
            def _(i):
                expert, at = i // (BLOCK // 16), pl.multiple_of(lax.rem(i, BLOCK // 16) * 16, 16)
                value = own[k, expert, pl.ds(at, 16), :].astype(F32)
                for other in others:
                    value = value + landed[other, expert, pl.ds(at, 16), :].astype(F32)
                dst[expert, pl.ds(at, 16), :] = value.astype(dst.dtype)

        copies, arrived, kept = [], set(), []
        for k, (place, target, others) in enumerate(SUM):
            if others:
                yield
                for other in others:
                    copies[other].wait_recv()
                kept[k - 4].wait()
                part = landed.at[others[0]]
                total(k - 4, others, part)
            else:
                part = block(place)
            copies.append(
                send(part, landed.at[k], send_sem.at[k], recv_sem.at[k], {"fsdp": fsdp_at(*target)})
            )
            if k == 3:
                for place in [place for place, _, _ in SUM[4:]] + [(0, 0)]:
                    j = len(kept)
                    kept.append(pltpu.make_async_copy(block(place), own.at[j], own_sem.at[j]))
                    kept[j].start()
        yield
        for k in LAST:
            copies[k].wait_recv()
        kept[3].wait()
        total(3, LAST, out)
        for copy in copies:
            copy.wait_send()


class SumAll:
    def __init__(self, columns):
        self.over_fsdp = SumFsdp(columns, F32)
        self.scratch = self.over_fsdp.scratch + [
            pltpu.VMEM((BLOCK, columns), F32),
            dma(7),
            dma(7),
            pltpu.VMEM((7, 8, columns), F32),
        ]

    def run(self, src, out, *scratch):
        total, send_sem, recv_sem, landed = scratch[-4:]
        yield from self.over_fsdp.run(src, total, *scratch[:-4])

        def rows(tp):
            return pl.ds(pl.multiple_of(tp * 8, 8), 8)

        copies = []
        for k, place in enumerate(EVERY):
            peer = tp_at(*place)
            copies.append(
                send(total.at[rows(peer)], landed.at[k], send_sem.at[k], recv_sem.at[k], {"tp": peer})
            )
        yield
        value = total[rows(lax.axis_index("tp")), :]
        for k, copy in enumerate(copies):
            copy.wait()
            value = value + landed[k]
        out[...] = value


def pump(runs):
    for run in list(runs):
        if next(run, "done") == "done":
            runs.remove(run)
    return bool(runs)


def drain(run, behind=(), steps=1):
    for _ in run:
        for _ in range(steps):
            pump(behind)


def part(ref, index):
    return ref.at[pl.ds(pl.multiple_of(index * ROWS, ROWS), ROWS)]


def run_task(task, scratch, src, out):
    count = len(task.scratch)
    mine, scratch[:] = scratch[:count], scratch[count:]
    return task.run(src, out, *mine)


def dot(a, b, dims=((1,), (0,))):
    return lax.dot_general(a, b, (dims, ((), ())), preferred_element_type=F32)


def lanes(rows):
    return lax.broadcasted_iota(jnp.int32, (rows, 128), 1)


def turn(values):
    low_half = lax.rem(lanes(values.shape[0]), HEAD_DIM) < HEAD_DIM // 2
    return jnp.where(low_half, pltpu.roll(values, 96, 1), pltpu.roll(values, 32, 1))


def both_halves(pair):
    low = lanes(pair.shape[0]) < HEAD_DIM
    other = pltpu.roll(pair, HEAD_DIM, 1)
    return jnp.where(low, pair, other), jnp.where(low, other, pair)


def head_lanes(values, head):
    return jnp.where(lanes(values.shape[0]) // HEAD_DIM == head, values, 0.0)


def doc_of(position, lengths):
    first = lengths[0, 0]
    return jnp.where(position >= first, 1, 0) + jnp.where(position >= first + lengths[0, 1], 1, 0)


def allowed(keys, first, lengths):
    key_at = lax.broadcasted_iota(jnp.int32, (keys, 1), 0)
    query_at = first + lax.broadcasted_iota(jnp.int32, (1, QUERIES), 1)
    return (key_at <= query_at) & (doc_of(key_at, lengths) == doc_of(query_at, lengths))


def inverse_root(values):
    return lax.rsqrt(jnp.mean(values * values, axis=-1, keepdims=True) + eps_norm)


def rms_back(grad_out, unit, inverse, gain):
    grad_unit = grad_out * gain
    return inverse * (grad_unit - unit * jnp.mean(grad_unit * unit, axis=-1, keepdims=True))


def key_tables(cosine, sine):
    key = lanes(cosine.shape[0]) < HEAD_DIM
    return jnp.where(key, cosine, 1.0), jnp.where(key, sine, 0.0)


QUERIES = 256


def attend(x_ref, w_ref, gain_ref, cos_ref, sin_ref, lengths, normed_ref, query_ref, pair_ref, lse_ref, mixed_ref, mixed_t, mixed_rows, between):
    @pl.loop(0, GROUP // 128)
    def _(i):
        rows = pl.ds(pl.multiple_of(i * 128, 128), 128)
        x = x_ref[rows, :].astype(F32)
        normed = (x * inverse_root(x) * gain_ref[0:1, :]).astype(BF16)
        normed_ref[rows, :] = normed
        raw = dot(normed, w_ref[0, :, 0:256])
        query, pair = raw[:, 0:128], raw[:, 128:256]
        cosine, sine = cos_ref[rows, :], sin_ref[rows, :]
        query_ref[rows, :] = (query * cosine + turn(query) * sine).astype(BF16)
        cosine, sine = key_tables(cosine, sine)
        pair_ref[rows, :] = (pair * cosine + turn(pair) * sine).astype(BF16)

    between()
    keys, values = both_halves(pair_ref[...].astype(F32))
    keys, values_t = keys.astype(BF16), values.T.astype(BF16)

    for first in range(0, GROUP, QUERIES):
        count = first + QUERIES
        mask = allowed(count, first, lengths)
        for head in range(2):
            query = head_lanes(query_ref[first : first + QUERIES, :].astype(F32), head).astype(BF16)
            scores = dot(keys[:count], query, ((1,), (1,))) * score_scale
            scores = jnp.where(mask, scores, -1e30)
            top = jnp.max(scores, axis=0, keepdims=True)
            raised = jnp.exp(scores - top)
            total = jnp.sum(raised, axis=0, keepdims=True)
            lse_ref[head : head + 1, first : first + QUERIES] = top + jnp.log(total)
            weights = (raised * (1.0 / total)).astype(BF16)
            mixed_t[HEAD_DIM * head : HEAD_DIM * (head + 1), first : first + QUERIES] = dot(
                values_t[HEAD_DIM * head : HEAD_DIM * (head + 1), :count], weights
            )
        between()
    mixed_ref[...] = mixed_t[...].astype(BF16)
    mixed_rows[...] = mixed_t[...].T.astype(BF16)


def attend_back(x_ref, w_ref, query_ref, pair_ref, lse_ref, cos_ref, sin_ref, lengths, grad_ref, gain_grad, dmixed_ref, dquery_t, dpair_ref, raw_ref, raw_t, between):
    keys, values = both_halves(pair_ref[...].astype(F32))
    keys_t = keys.T.astype(BF16)
    keys, values = keys.astype(BF16), values.astype(BF16)
    dpair_ref[...] = jnp.zeros_like(dpair_ref)

    for first in range(0, GROUP, QUERIES):
        count = first + QUERIES
        mask = allowed(count, first, lengths)
        for head in range(2):
            query = head_lanes(query_ref[first : first + QUERIES, :].astype(F32), head).astype(BF16)
            dmixed = head_lanes(dmixed_ref[first : first + QUERIES, :].astype(F32), head).astype(BF16)
            scores = dot(keys[:count], query, ((1,), (1,))) * score_scale
            scores = jnp.where(mask, scores, -1e30)
            weights = jnp.exp(scores - lse_ref[head : head + 1, first : first + QUERIES])
            dweights = dot(values[:count], dmixed, ((1,), (1,)))
            inner = jnp.sum(weights * dweights, axis=0, keepdims=True)
            dscores = (weights * (dweights - inner)).astype(BF16)
            dquery_t[HEAD_DIM * head : HEAD_DIM * (head + 1), first : first + QUERIES] = (
                dot(keys_t[HEAD_DIM * head : HEAD_DIM * (head + 1), :count], dscores) * score_scale
            )
            dpair_ref[0, :count, :] += dot(dscores, query) * score_scale
            dpair_ref[1, :count, :] += dot(weights.astype(BF16), dmixed)
        between()

    gain_grad[...] = jnp.zeros_like(gain_grad)

    @pl.loop(0, GROUP // 128)
    def _(i):
        at = pl.multiple_of(i * 128, 128)
        rows = pl.ds(at, 128)
        dquery = dquery_t[:, rows].T
        dkey, dvalue = dpair_ref[0, rows, :], dpair_ref[1, rows, :]
        dkey = dkey + pltpu.roll(dkey, HEAD_DIM, 1)
        dvalue = dvalue + pltpu.roll(dvalue, HEAD_DIM, 1)
        dpair = jnp.where(lanes(128) < HEAD_DIM, dkey, dvalue)
        cosine, sine = cos_ref[rows, :], sin_ref[rows, :]
        dquery = dquery * cosine + turn(dquery * sine)
        cosine, sine = key_tables(cosine, sine)
        dpair = dpair * cosine + turn(dpair * sine)
        raw_ref[rows, 0:128] = dquery.astype(BF16)
        raw_ref[rows, 128:256] = dpair.astype(BF16)
        raw_t[0:128, rows] = dquery.T.astype(BF16)
        raw_t[128:256, rows] = dpair.T.astype(BF16)
        dnormed = dot(raw_ref[rows, :], w_ref[0, :, 0:256], ((1,), (1,)))
        grad_ref[rows, :] = dnormed.astype(BF16)
        x = x_ref[rows, :].astype(F32)
        gain_grad[...] += jnp.sum(dnormed * (x * inverse_root(x)), axis=0, keepdims=True)


HEAD_TASKS = (
    GatherTp(ROWS, D),
    GatherFsdp(1, 512),
    GatherFsdp(LOCAL, HIDDEN),
    GatherFsdp(LOCAL, HIDDEN),
    GatherFsdp(LOCAL, HIDDEN),
    GatherTp(ROWS, D),
    GatherTp(D, ROWS),
    ExchangeTp(),
    GatherTp(ROWS, D),
)


def head_body(
    lengths, x_ref, small_ref, gate_ref, up_ref, down_ref, dy_ref, routes_ref,
    x_out, w_out, gate_all, up_all, down_all, dy_out, tokens,
    normed_out, query_out, pair_out, lse_ref, mixed_ref, middle_ref, own_ref, chosen_out, rank_out, rank_t_out, gains_ref, cos_out, sin_out, output_out,
    x_all, w_all, dy_all, normed_ref, query_ref, pair_ref, chosen_ref, rank_ref, rank_t, cos_ref, sin_ref, store_sem,
    mixed_t, mixed_rows, mixed_own, output_all, *scratch,
):
    scratch = list(scratch)
    stores = []

    def store(src, dst):
        stores.append(pltpu.make_async_copy(src, dst, store_sem.at[len(stores)]))
        stores[-1].start()

    greet()
    pairs = (
        (x_ref, x_all), (small_ref, w_all), (gate_ref, gate_all), (up_ref, up_all), (down_ref, down_all),
        (dy_ref, dy_all), (w_all.at[0, :, 256:384], output_all),
        (functools.partial(part, mixed_rows), lambda tp: mixed_own.at[tp]), (own_ref, tokens),
    )
    x_run, w_run, gate_run, up_run, down_run, dy_run, output_run, mixed_run, token_run = [
        run_task(task, scratch, *pair) for task, pair in zip(HEAD_TASKS, pairs)
    ]
    front = [x_run, w_run]
    pump(front)

    lane = lanes(GROUP)
    routes = routes_ref[...].astype(F32).T.astype(jnp.int32)
    chosen = lane == routes[:, 0:1]
    for k in range(1, 8):
        chosen = chosen | (lane == routes[:, k : k + 1])
    chosen = jnp.where(chosen, 1.0, 0.0)
    chosen_ref[...] = chosen
    pump(front)
    chosen = chosen.astype(BF16)
    for i in range(4):
        rows = slice(256 * i, 256 * (i + 1))
        later = 256 * i + lax.broadcasted_iota(jnp.int32, (256, GROUP), 0)
        until = jnp.where(later >= lax.broadcasted_iota(jnp.int32, (256, GROUP), 1), 1.0, 0.0)
        running = dot(until.astype(BF16), chosen)
        rank = jnp.where(chosen_ref[rows, :] > 0.0, running - 1.0, -1.0)
        rank_ref[rows, :] = rank
        rank_t[:, rows] = rank.T
    pump(front)
    position = lax.broadcasted_iota(jnp.int32, (GROUP, 1), 0)
    ends = (lengths[0, 0], lengths[0, 0] + lengths[0, 1])
    start = jnp.where(position >= ends[1], ends[1], jnp.where(position >= ends[0], ends[0], 0))
    half = lax.rem(lane[0:1], HEAD_DIM // 2).astype(F32)
    frequency = jnp.exp(half * (-2.0 / HEAD_DIM * math.log(rope_base)))
    angles = (position - start).astype(F32) * frequency
    cos_ref[...] = jnp.cos(angles)
    sine = jnp.sin(angles)
    sin_ref[...] = jnp.where(lax.rem(lane, HEAD_DIM) < HEAD_DIM // 2, -sine, sine)
    for pair in ((chosen_ref, chosen_out), (rank_ref, rank_out), (rank_t, rank_t_out), (cos_ref, cos_out), (sin_ref, sin_out)):
        store(*pair)
    drain(w_run)
    behind = [gate_run, up_run, down_run]
    pump(behind)
    store(w_all, w_out)
    gains_ref[...] = w_all[0, :, 384:512].astype(F32).T[32:40, :]
    drain(x_run)
    pump(behind)
    store(x_all, x_out)
    far = [output_run, dy_run]
    pump(far)
    calls = [0]

    def between():
        calls[0] += 1
        if calls[0] in (3, 4, 5):
            pump(far[:1])
        if calls[0] in (2, 5):
            pump(behind)

    attend(
        x_all, w_all, gains_ref, cos_ref, sin_ref, lengths,
        normed_ref, query_ref, pair_ref, lse_ref, mixed_ref, mixed_t, mixed_rows, between,
    )
    next(mixed_run)
    store(normed_ref, normed_out)
    store(query_ref, query_out)
    store(pair_ref, pair_out)
    drain(output_run)
    store(output_all, output_out)
    drain(mixed_run)
    middle = x_ref[...].astype(F32)
    for tp in range(8):
        middle = middle + dot(mixed_own[tp], output_all[tp * D : (tp + 1) * D, :], ((1,), (1,)))
    middle_ref[...] = middle
    own_ref[...] = (middle * inverse_root(middle) * gains_ref[1:2, :]).astype(BF16)
    next(token_run)
    far = [dy_run]
    pump(behind)
    pump(far)
    pump(behind)
    pump(far)
    drain(token_run, far + behind)
    while pump(far):
        pass
    store(dy_all, dy_out)
    while pump(behind):
        pass
    for copy in stores:
        copy.wait()


def head(lengths, x, small, gate, up, down, dy, routes):
    def shape(*dims, dtype=BF16):
        return jax.ShapeDtypeStruct(dims, dtype)

    vmem = pl.BlockSpec(memory_space=pltpu.VMEM)
    far = pl.BlockSpec(memory_space=pl.ANY)
    weight = shape(LOCAL, D, HIDDEN)
    return pl.pallas_call(
        head_body,
        name="head",
        out_shape=[
            shape(GROUP, D),
            shape(1, D, 512),
            weight,
            weight,
            weight,
            shape(GROUP, D),
            shape(GROUP, D),
            shape(GROUP, D),
            shape(GROUP, 128),
            shape(GROUP, 128),
            shape(2, GROUP, dtype=F32),
            shape(128, GROUP),
            shape(ROWS, D, dtype=F32),
            shape(ROWS, D),
            shape(GROUP, 128, dtype=F32),
            shape(GROUP, 128, dtype=F32),
            shape(128, GROUP, dtype=F32),
            shape(8, D, dtype=F32),
            shape(GROUP, 128, dtype=F32),
            shape(GROUP, 128, dtype=F32),
            shape(8 * D, ROWS),
        ],
        in_specs=[pl.BlockSpec(memory_space=pltpu.SMEM)] + [vmem] * 7,
        out_specs=[far] * 6 + [vmem] + [far] * 3 + [vmem] * 4 + [far] * 3 + [vmem] + [far] * 3,
        scratch_shapes=[
            pltpu.VMEM((GROUP, D), BF16),
            pltpu.VMEM((1, D, 512), BF16),
            pltpu.VMEM((GROUP, D), BF16),
            pltpu.VMEM((GROUP, D), BF16),
            pltpu.VMEM((GROUP, 128), BF16),
            pltpu.VMEM((GROUP, 128), BF16),
            pltpu.VMEM((GROUP, 128), F32),
            pltpu.VMEM((GROUP, 128), F32),
            pltpu.VMEM((128, GROUP), F32),
            pltpu.VMEM((GROUP, 128), F32),
            pltpu.VMEM((GROUP, 128), F32),
            dma(12),
            pltpu.VMEM((128, GROUP), F32),
            pltpu.VMEM((GROUP, 128), BF16),
            pltpu.VMEM((8, ROWS, 128), BF16),
            pltpu.VMEM((8 * D, ROWS), BF16),
        ]
        + [buffer for task in HEAD_TASKS for buffer in task.scratch],
        compiler_params=pltpu.CompilerParams(
            collective_id=1, has_side_effects=True, vmem_limit_bytes=56 * 2**20
        ),
    )(lengths, x, small, gate, up, down, dy, routes)


TAIL_TASKS = (
    SumTp(ROWS, WIDE),
    SumChips(0),
    SumChips(1),
    SumChips(2),
    ExchangeTp(),
    GatherTp(ROWS, D),
    SumTp(ROWS, D),
    SumTp(ROWS, D),
    SumFsdp(384, BF16),
    SumAll(128),
)


def tail_body(
    lengths, grads_ref, combined_in, pairs_ref,
    x_ref, dy_ref, middle_ref, own_ref, chosen_ref, gains_ref, lse_ref, mixed_ref,
    x_in, w_in, normed_in, query_in, pair_in, cos_in, sin_in, output_in,
    outputs_ref, input_grad, small_grad, attention_grad, gate_grad, up_grad, down_grad,
    x_all, w_all, normed_ref, query_ref, pair_ref, cos_ref, sin_ref, output_all, combined_ref, dmixed_own, load_sem,
    grads_sum, moe_sum, datt_own, datt_all, dmiddle_ref, dnormed_part, dnormed_sum, weights_part, small_part, gain_grads,
    gain_row, dmixed_ref, dquery_t, dpair_ref, raw_ref, raw_t, *scratch,
):
    scratch = list(scratch)
    greet()
    pairs = (
        (grads_ref, grads_sum), (pairs_ref, gate_grad), (pairs_ref, up_grad), (pairs_ref, down_grad),
        (lambda tp: dmixed_own.at[tp], functools.partial(part, dmixed_ref)),
        (datt_own, datt_all), (combined_ref, moe_sum), (dnormed_part, dnormed_sum),
        (weights_part, attention_grad), (small_part, small_grad),
    )
    grads_run, gate_run, up_run, down_run, dmixed_run, datt_run, moe_run, dnormed_run, weights_run, small_run = [
        run_task(task, scratch, *pair) for task, pair in zip(TAIL_TASKS, pairs)
    ]
    behind = [gate_run, up_run, down_run]
    next(grads_run)
    pump(behind)
    loads = []
    for k, (src, dst) in enumerate(
        (
            (w_in, w_all), (x_in, x_all), (normed_in, normed_ref), (query_in, query_ref),
            (pair_in, pair_ref), (cos_in, cos_ref), (sin_in, sin_ref), (output_in, output_all),
            (combined_in, combined_ref),
        )
    ):
        loads.append(pltpu.make_async_copy(src, dst, load_sem.at[k]))
        loads[k].start()
    drain(grads_run)

    for copy in loads:
        copy.wait()
    middle = middle_ref[...]
    inverse = inverse_root(middle)
    unit = middle * inverse
    router = w_all[0, :, 384:512]
    own_rows = pl.ds(pl.multiple_of(lax.axis_index("tp") * ROWS, ROWS), ROWS)
    logits = jnp.where(chosen_ref[own_rows, :] > 0.0, dot(own_ref[...], router), -1e30)
    raised = jnp.exp(logits - jnp.max(logits, axis=-1, keepdims=True))
    gates = raised / jnp.sum(raised, axis=-1, keepdims=True)
    dgates = grads_sum[:, D:WIDE]
    dlogits = gates * (dgates - jnp.sum(gates * dgates, axis=-1, keepdims=True))
    dlogits = dlogits.astype(BF16)
    dtokens = grads_sum[:, 0:D] + dot(dlogits, router, ((1,), (1,)))
    dmiddle = dy_ref[...].astype(F32) + rms_back(dtokens, unit, inverse, gains_ref[1:2, :])
    dmiddle_ref[...] = dmiddle
    datt_own[...] = dmiddle.astype(BF16)
    for tp in range(8):
        dmixed_own[tp] = dot(datt_own[...], output_all[tp * D : (tp + 1) * D, :]).astype(BF16)
    next(dmixed_run)
    next(datt_run)
    pump(behind)
    pump(behind)
    small_part[...] = dot(own_ref[...], dlogits, ((0,), (0,))).reshape(small_part.shape)
    gain_grads[...] = jnp.zeros_like(gain_grads)
    gain_grads[EXPERTS : EXPERTS + 1, :] = jnp.sum(dtokens * unit, axis=0, keepdims=True)
    drain(dmixed_run)
    far = [datt_run, moe_run]
    pump(far)
    calls = [0]

    def between():
        calls[0] += 1
        if calls[0] in (2, 3, 4):
            pump(far[:1])
        if calls[0] == 2:
            pump(behind)

    attend_back(
        x_all, w_all, query_ref, pair_ref, lse_ref, cos_ref, sin_ref, lengths,
        dnormed_part, gain_row, dmixed_ref, dquery_t, dpair_ref, raw_ref, raw_t, between,
    )
    next(dnormed_run)
    gain_grads[EXPERTS + 1 : EXPERTS + 2, :] = gain_row[...]
    small_part[...] += gain_grads[...].T.reshape(small_part.shape)
    next(small_run)
    drain(datt_run)

    @pl.loop(0, 4)
    def _(i):
        at = pl.ds(pl.multiple_of(i * 256, 256), 256)
        chips = pl.ds(i * 2, 2)
        into_qkv = dot(raw_t[...], normed_ref[:, at]).T.astype(BF16)
        weights_part[chips, :, :, 0:256] = into_qkv.reshape(2, 2, BLOCK, 256)
        into_output = dot(mixed_ref[...], datt_all[:, at]).T.astype(BF16)
        weights_part[chips, :, :, 256:384] = into_output.reshape(2, 2, BLOCK, 128)

    last = [dnormed_run, weights_run, small_run, moe_run] + behind
    while pump(last):
        pass
    outputs_ref[...] = (middle_ref[...] + moe_sum[...]).astype(BF16)
    x = x_ref[...].astype(F32)
    inverse = inverse_root(x)
    input_grad[...] = dmiddle_ref[...] + rms_back(dnormed_sum[...], x * inverse, inverse, gains_ref[0:1, :])


def tail(*arrays):
    def shape(*dims, dtype=F32):
        return jax.ShapeDtypeStruct(dims, dtype)

    vmem = pl.BlockSpec(memory_space=pltpu.VMEM)
    far = pl.BlockSpec(memory_space=pl.ANY)
    weight = shape(LOCAL, BLOCK, HIDDEN)
    return pl.pallas_call(
        tail_body,
        name="tail",
        out_shape=[
            shape(ROWS, D, dtype=BF16),
            shape(ROWS, D),
            shape(8, 128),
            shape(BLOCK, 384),
            weight,
            weight,
            weight,
        ],
        in_specs=[pl.BlockSpec(memory_space=pltpu.SMEM)] + [vmem] + [far] * 2 + [vmem] * 8 + [far] * 8,
        out_specs=[vmem] * 7,
        scratch_shapes=[
            pltpu.VMEM((GROUP, D), BF16),
            pltpu.VMEM((1, D, 512), BF16),
            pltpu.VMEM((GROUP, D), BF16),
            pltpu.VMEM((GROUP, 128), BF16),
            pltpu.VMEM((GROUP, 128), BF16),
            pltpu.VMEM((GROUP, 128), F32),
            pltpu.VMEM((GROUP, 128), F32),
            pltpu.VMEM((8 * D, ROWS), BF16),
            pltpu.VMEM((GROUP, D), BF16),
            pltpu.VMEM((8, ROWS, 128), BF16),
            dma(9),
            pltpu.VMEM((ROWS, WIDE), F32),
            pltpu.VMEM((ROWS, D), F32),
            pltpu.VMEM((ROWS, D), BF16),
            pltpu.VMEM((GROUP, D), BF16),
            pltpu.VMEM((ROWS, D), F32),
            pltpu.VMEM((GROUP, D), BF16),
            pltpu.VMEM((ROWS, D), F32),
            pltpu.VMEM((8, 2, BLOCK, 384), BF16),
            pltpu.VMEM((8, 2, BLOCK, 128), F32),
            pltpu.VMEM((128, D), F32),
            pltpu.VMEM((1, D), F32),
            pltpu.VMEM((GROUP, 128), BF16),
            pltpu.VMEM((128, GROUP), F32),
            pltpu.VMEM((2, GROUP, 128), F32),
            pltpu.VMEM((GROUP, 256), BF16),
            pltpu.VMEM((256, GROUP), BF16),
        ]
        + [buffer for task in TAIL_TASKS for buffer in task.scratch],
        compiler_params=pltpu.CompilerParams(
            collective_id=2, has_side_effects=True, vmem_limit_bytes=62 * 2**20
        ),
    )(*arrays)


def experts_body(
    tokens_ref, dy_ref, router_ref, chosen_ref, rank_ref, rank_t,
    gate_ref, up_ref, down_ref,
    combined_ref, grad_ref, pair_ref,
    give_all, out_all, dpicked_all, dgate_all, gates_ref, parts, got, send_sem, recv_sem,
):
    step = pl.program_id(0)
    lane = lax.broadcasted_iota(jnp.int32, (1, 128), 1)
    core = lax.rem(lax.axis_index("fsdp"), 2)

    def across(expert):
        slot = lax.rem(expert, 2)
        return pltpu.make_async_remote_copy(
            src_ref=parts.at[slot, :, :, 1 - core],
            dst_ref=got.at[expert],
            send_sem=send_sem.at[slot],
            recv_sem=recv_sem.at[expert],
            device_id={"fsdp": core_partner()},
            device_id_type=MESH,
        )

    @pl.when(step == 0)
    def _():
        barrier = pltpu.get_barrier_semaphore()
        pl.semaphore_signal(barrier, inc=1, device_id={"fsdp": core_partner()}, device_id_type=MESH)
        pl.semaphore_wait(barrier, 1)
        out_all[...] = jnp.zeros_like(out_all)
        dpicked_all[...] = jnp.zeros_like(dpicked_all)
        dgate_all[...] = jnp.zeros_like(dgate_all)
        logits = jnp.where(chosen_ref[...] > 0.0, dot(tokens_ref[...], router_ref[0]), -1e30)
        raised = jnp.exp(logits - jnp.max(logits, axis=-1, keepdims=True))
        gates = raised / jnp.sum(raised, axis=-1, keepdims=True)
        high = gates.astype(BF16)
        gates_ref[:, 0:128] = high
        gates_ref[:, 128:256] = (gates - high.astype(F32)).astype(BF16)

    @pl.when(step < LOCAL)
    def _():
        expert = lax.axis_index("tp") * LOCAL + step
        expert_lane = lane == expert
        slot = lax.broadcasted_iota(jnp.int32, (SLOTS, GROUP), 0)
        rank_row = rank_t[pl.ds(expert, 1), :].astype(jnp.int32)
        rank_column = jnp.sum(jnp.where(expert_lane, rank_ref[...], 0.0), axis=1, keepdims=True)
        take = jnp.where(slot == rank_row, 1.0, 0.0).astype(BF16)
        slot_gates = dot(take, gates_ref[...])
        slot_gates = slot_gates[:, 0:128] + slot_gates[:, 128:256]
        slot_gate = jnp.sum(jnp.where(expert_lane, slot_gates, 0.0), axis=1, keepdims=True)
        picked = dot(take, tokens_ref[...]).astype(BF16)
        dy = dot(take, dy_ref[...]).astype(BF16)

        gate_part = dot(picked, gate_ref[0])
        up_part = dot(picked, up_ref[0])
        sigmoid = 1.0 / (1.0 + jnp.exp(-gate_part))
        silu = gate_part * sigmoid
        hidden = silu * up_part
        dhidden = dot(dy, down_ref[0])
        dgate = jnp.sum(hidden * dhidden, axis=1, keepdims=True)
        weighted = (hidden * slot_gate).astype(BF16)
        dhidden = dhidden * slot_gate
        dgate_part = (dhidden * up_part * (sigmoid * (1.0 + gate_part * (1.0 - sigmoid)))).astype(BF16)
        dup_part = (dhidden * silu).astype(BF16)

        @pl.when(step >= 2)
        def _():
            across(step - 2).wait_send()

        slot_now = lax.rem(step, 2)
        picked_t, dy_t = picked.T, dy.T
        for k, (left, right) in enumerate(
            ((picked_t, dgate_part), (picked_t, dup_part), (dy_t, weighted))
        ):
            parts[slot_now, k] = dot(left, right).astype(BF16).reshape(8, 2, BLOCK, HIDDEN)
        across(step).start()

        rows = pl.ds(pl.multiple_of(step * PLACES, PLACES), SLOTS)
        out_all[rows, :] = dot(weighted, down_ref[0], ((1,), (1,))).astype(BF16)
        dpicked = dot(dgate_part, gate_ref[0], ((1,), (1,)))
        dpicked_all[rows, :] = (dpicked + dot(dup_part, up_ref[0], ((1,), (1,)))).astype(BF16)
        dgate_all[rows, :] = jnp.where(expert_lane, dgate, 0.0).astype(BF16)
        place = lax.broadcasted_iota(jnp.int32, (GROUP, PLACES), 1)
        give = jnp.where(place == rank_column.astype(jnp.int32), 1.0, 0.0)
        give_all[:, pl.ds(pl.multiple_of(step * PLACES, PLACES), PLACES)] = give.astype(BF16)

    @pl.when(step == LOCAL)
    def _():
        for i in range(4):
            columns = slice(256 * i, 256 * (i + 1))
            combined_ref[:, columns] = dot(give_all[...], out_all[:, columns]).astype(BF16)
            grad_ref[:, columns] = dot(give_all[...], dpicked_all[:, columns]).astype(BF16)
        grad_ref[:, D:WIDE] = dot(give_all[...], dgate_all[...]).astype(BF16)

    @pl.when(step >= 1)
    def _():
        across(step - 1).wait_recv()
        slot_before = lax.rem(step - 1, 2)

        @pl.loop(0, 24)
        def _(i):
            kind, chip = i // 8, lax.rem(i, 8)
            total = parts[slot_before, kind, chip, core].astype(F32) + got[step - 1, kind, chip].astype(F32)
            pair_ref[0, kind, chip] = total.astype(BF16)

    @pl.when(step == LOCAL)
    def _():
        for expert in (LOCAL - 2, LOCAL - 1):
            across(expert).wait_send()


def experts(tokens, dy, router, chosen, rank, rank_t, gate, up, down):
    def whole(*shape):
        return pl.BlockSpec(shape, lambda i: (0,) * len(shape))

    def own(*shape):
        return pl.BlockSpec((1,) + shape, lambda i: (jnp.minimum(i, LOCAL - 1),) + (0,) * len(shape))

    return pl.pallas_call(
        experts_body,
        name="experts",
        grid=(LOCAL + 1,),
        in_specs=[
            whole(GROUP, D),
            whole(GROUP, D),
            pl.BlockSpec((1, D, 128), lambda i: (0, 0, 3)),
            whole(GROUP, 128),
            whole(GROUP, 128),
            whole(128, GROUP),
            own(D, HIDDEN),
            own(D, HIDDEN),
            own(D, HIDDEN),
        ],
        out_specs=[
            whole(GROUP, D),
            whole(GROUP, WIDE),
            pl.BlockSpec((1, 3, 8, BLOCK, HIDDEN), lambda i: (jnp.maximum(i - 1, 0), 0, 0, 0, 0)),
        ],
        scratch_shapes=[
            pltpu.VMEM((GROUP, LOCAL * PLACES), BF16),
            pltpu.VMEM((LOCAL * PLACES, D), BF16),
            pltpu.VMEM((LOCAL * PLACES, D), BF16),
            pltpu.VMEM((LOCAL * PLACES, 128), BF16),
            pltpu.VMEM((GROUP, 256), BF16),
            pltpu.VMEM((2, 3, 8, 2, BLOCK, HIDDEN), BF16),
            pltpu.VMEM((LOCAL, 3, 8, BLOCK, HIDDEN), BF16),
            dma(2),
            dma(LOCAL),
        ],
        out_shape=[
            jax.ShapeDtypeStruct((GROUP, D), BF16),
            jax.ShapeDtypeStruct((GROUP, WIDE), BF16),
            jax.ShapeDtypeStruct((LOCAL, 3, 8, BLOCK, HIDDEN), BF16),
        ],
        compiler_params=pltpu.CompilerParams(
            collective_id=3, has_side_effects=True, vmem_limit_bytes=60 * 2**20
        ),
    )(tokens, dy, router, chosen, rank, rank_t, gate, up, down)


def finish_body(*refs):
    sources, outs = refs[:7], refs[7:19]
    small, attention, sems = refs[19:]
    copies = []
    for k, (source, target) in enumerate(
        zip(sources, (outs[0], outs[1], small, attention, outs[9], outs[10], outs[11]))
    ):
        copies.append(pltpu.make_async_copy(source, target, sems.at[k]))
        copies[k].start()
    for copy in copies:
        copy.wait()
    outs[2][...] = attention[:, 0:128]
    outs[3][...] = attention[:, 128:192]
    outs[4][...] = attention[:, 192:256]
    outs[5][...] = attention[:, 256:384].T
    outs[6][...] = small[:, 0:EXPERTS]
    columns = small[...].T
    outs[7][...] = columns[EXPERTS + 1 : EXPERTS + 2, :]
    outs[8][...] = columns[EXPERTS : EXPERTS + 1, :]


def finish(*arrays):
    def shape(*dims, dtype=F32):
        return jax.ShapeDtypeStruct(dims, dtype)

    vmem = pl.BlockSpec(memory_space=pltpu.VMEM)
    far = pl.BlockSpec(memory_space=pl.ANY)
    return pl.pallas_call(
        finish_body,
        name="finish",
        out_shape=[
            shape(ROWS, D, dtype=BF16),
            shape(ROWS, D),
            shape(BLOCK, 128),
            shape(BLOCK, BLOCK),
            shape(BLOCK, BLOCK),
            shape(128, BLOCK),
            shape(8, EXPERTS),
            shape(1, 8),
            shape(1, 8),
        ]
        + [shape(LOCAL, BLOCK, HIDDEN)] * 3,
        in_specs=[far] * 7,
        out_specs=[vmem] * 12,
        scratch_shapes=[pltpu.VMEM((8, 128), F32), pltpu.VMEM((BLOCK, 384), F32), dma(7)],
        compiler_params=pltpu.CompilerParams(vmem_limit_bytes=60 * 2**20),
    )(*arrays)


def per_device(
    inputs,
    lengths,
    routes,
    attn_gain,
    query_weight,
    key_weight,
    value_weight,
    output_weight,
    moe_gain,
    router_weight,
    gate_weight,
    up_weight,
    down_weight,
    cotangent,
):
    small = jnp.concatenate(
        [
            query_weight,
            key_weight,
            value_weight,
            output_weight.T,
            router_weight,
            attn_gain[:, None],
            moe_gain[:, None],
            jnp.zeros((BLOCK, 128 - EXPERTS - 2), BF16),
        ],
        axis=1,
    )
    (
        x_all, w_all, gate_all, up_all, down_all, dy_all, tokens,
        normed, query, pair, lse, mixed, middle, own, chosen, rank, rank_t, gains, cosine, sine, output_all,
    ) = head(
        lengths, inputs, small[None], gate_weight, up_weight, down_weight.transpose(0, 2, 1),
        cotangent, routes.T,
    )
    combined, grads, pairs = experts(
        tokens, dy_all, w_all, chosen, rank, rank_t, gate_all, up_all, down_all
    )
    results = tail(
        lengths, grads, combined, pairs,
        inputs, cotangent, middle, own, chosen, gains, lse, mixed,
        x_all, w_all, normed, query, pair, cosine, sine, output_all,
    )
    (
        outputs, input_grad, query_grad, key_grad, value_grad, output_grad, router_grad, attn_gain_grad, moe_gain_grad,
        gate_grad, up_grad, down_grad,
    ) = finish(*results)
    return (
        outputs,
        input_grad,
        attn_gain_grad.reshape(8),
        query_grad,
        key_grad,
        value_grad,
        output_grad,
        moe_gain_grad.reshape(8),
        router_grad,
        gate_grad,
        up_grad,
        down_grad.transpose(0, 2, 1),
    )


def solution(mesh):
    return jax.shard_map(
        per_device,
        mesh=mesh,
        in_specs=(
            P(("fsdp", "tp"), None),
            P("fsdp", None),
            P("fsdp", None),
            P("fsdp"),
            P("fsdp", "tp"),
            P("fsdp", "tp"),
            P("fsdp", "tp"),
            P("tp", "fsdp"),
            P("fsdp"),
            P("fsdp", None),
            P("tp", "fsdp", None),
            P("tp", "fsdp", None),
            P("tp", None, "fsdp"),
            P(("fsdp", "tp"), None),
        ),
        out_specs=(
            P(("fsdp", "tp"), None),
            P(("fsdp", "tp"), None),
            P(("fsdp", "tp")),
            P("fsdp", "tp"),
            P("fsdp", "tp"),
            P("fsdp", "tp"),
            P("tp", "fsdp"),
            P(("fsdp", "tp")),
            P(("fsdp", "tp"), None),
            P("tp", "fsdp", None),
            P("tp", "fsdp", None),
            P("tp", None, "fsdp"),
        ),
        check_vma=False,
    )
```

```python
import functools
import math

import jax
import jax.numpy as jnp
from jax import lax
from jax.experimental import pallas as pl
from jax.experimental.pallas import tpu as pltpu
from jax.sharding import PartitionSpec as P

MESH = pl.DeviceIdType.MESH
D = 1024
HEAD_DIM = 64
EXPERTS = 32
HIDDEN = 512
GROUP = 1024
ROWS = 128
SLOTS = 352
PLACES = 384
LOCAL = 4
BLOCK = 64
WIDE = D + 128

eps_norm = 1e-06
rope_base = 10000.0
score_scale = 1.0 / HEAD_DIM
F32 = jnp.float32
BF16 = jnp.bfloat16


def tp_at(along, across):
    tp = lax.axis_index("tp")
    return lax.rem(tp // 2 + along, 4) * 2 + lax.rem(tp + across, 2)


def fsdp_at(along, across):
    fsdp = lax.axis_index("fsdp")
    chip = lax.rem(fsdp // 8 + across, 2) * 4 + lax.rem(fsdp // 2 + along, 4)
    return chip * 2 + lax.rem(fsdp, 2)


def core_partner():
    fsdp = lax.axis_index("fsdp")
    return fsdp // 2 * 2 + 1 - lax.rem(fsdp, 2)


def send(src, dst, send_sem, recv_sem, device):
    copy = pltpu.make_async_remote_copy(
        src_ref=src,
        dst_ref=dst,
        send_sem=send_sem,
        recv_sem=recv_sem,
        device_id=device,
        device_id_type=MESH,
    )
    copy.start()
    return copy


def greet():
    barrier = pltpu.get_barrier_semaphore()
    for place in EVERY:
        for device in ({"tp": tp_at(*place)}, {"fsdp": fsdp_at(*place)}):
            pl.semaphore_signal(barrier, inc=1, device_id=device, device_id_type=MESH)
    pl.semaphore_signal(barrier, inc=1, device_id={"fsdp": core_partner()}, device_id_type=MESH)
    pl.semaphore_wait(barrier, 15)


def dma(count):
    return pltpu.SemaphoreType.DMA((count,))


EVERY = ((2, 0), (2, 1), (1, 1), (3, 1), (1, 0), (3, 0), (0, 1))
GATHER = (
    ((0, 0), (0, 1), None),
    ((0, 0), (1, 0), None),
    ((0, 0), (3, 0), None),
    ((0, 1), (1, 0), 0),
    ((0, 1), (3, 0), 0),
    ((3, 0), (1, 0), 1),
    ((1, 1), (3, 0), 4),
)
ARRIVES = ((0, 1), (3, 0), (1, 0), (3, 1), (1, 1), (2, 0), (2, 1))
SUM = (
    ((2, 0), (1, 0), ()),
    ((2, 1), (3, 0), ()),
    ((1, 1), (1, 0), ()),
    ((3, 0), (3, 0), ()),
    ((1, 0), (1, 0), (0,)),
    ((3, 1), (3, 0), (1,)),
    ((0, 1), (0, 1), (2, 5)),
)
LAST = (3, 4, 6)


class GatherTp:
    def __init__(self, rows, columns):
        self.rows = rows
        self.scratch = [dma(7), dma(7), pltpu.SemaphoreType.DMA(())]

    def run(self, src, out, send_sem, recv_sem, own_sem):
        def block(place):
            return out.at[pl.ds(pl.multiple_of(tp_at(*place) * self.rows, self.rows), self.rows)]

        own = pltpu.make_async_copy(src, block((0, 0)), own_sem)
        own.start()
        copies, arrived = [], set()
        for k, (place, target, after) in enumerate(GATHER):
            if after is not None and after not in arrived:
                yield
                copies[after].wait_recv()
                arrived.add(after)
            copies.append(
                send(
                    src if place == (0, 0) else block(place),
                    block(place),
                    send_sem.at[k],
                    recv_sem.at[k],
                    {"tp": tp_at(*target)},
                )
            )
        yield
        for k, copy in enumerate(copies):
            if k not in arrived:
                copy.wait_recv()
            copy.wait_send()
        own.wait()


class SumTp:
    def __init__(self, rows, columns):
        self.rows = rows
        self.scratch = [dma(7), dma(7), pltpu.VMEM((7, rows, columns), BF16)]

    def run(self, src, out, send_sem, recv_sem, landed):
        def first(place):
            return pl.multiple_of(tp_at(*place) * self.rows, self.rows)

        def total(place, others, dst):
            start = first(place)

            @pl.loop(0, self.rows // 16)
            def _(i):
                at = pl.multiple_of(i * 16, 16)
                value = src[pl.ds(pl.multiple_of(start + at, 16), 16), :].astype(F32)
                for k in others:
                    value = value + landed[k, pl.ds(at, 16), :].astype(F32)
                dst[pl.ds(at, 16), :] = value.astype(dst.dtype)

        copies, arrived = [], set()
        for k, (place, target, others) in enumerate(SUM):
            if others:
                yield
                for other in others:
                    copies[other].wait_recv()
                    arrived.add(other)
                part = landed.at[others[0]]
                total(place, others, part)
            else:
                part = src.at[pl.ds(first(place), self.rows)]
            copies.append(
                send(part, landed.at[k], send_sem.at[k], recv_sem.at[k], {"tp": tp_at(*target)})
            )
        yield
        for k in LAST:
            copies[k].wait_recv()
        total((0, 0), LAST, out)
        for copy in copies:
            copy.wait_send()


class ExchangeTp:
    def __init__(self):
        self.scratch = [dma(7), dma(7), pltpu.SemaphoreType.DMA(())]

    def run(self, block, place, send_sem, recv_sem, own_sem):
        here = lax.axis_index("tp")
        copies = [
            send(block(peer), place(here), send_sem.at[k], recv_sem.at[k], {"tp": peer})
            for k, peer in enumerate(tp_at(*step) for step in EVERY)
        ]
        own = pltpu.make_async_copy(block(here), place(here), own_sem)
        own.start()
        yield
        for copy in copies:
            copy.wait()
        own.wait()


class GatherFsdp:
    def __init__(self, experts, columns):
        self.scratch = [dma(7), dma(7), dma(8), dma(8), pltpu.SemaphoreType.DMA(())]

    def run(self, src, out, send_sem, recv_sem, core_send, core_recv, own_sem):
        def block(place):
            return out.at[:, pl.ds(pl.multiple_of(fsdp_at(*place) * BLOCK, BLOCK), BLOCK)]

        own = pltpu.make_async_copy(src, block((0, 0)), own_sem)
        own.start()
        copies, arrived, crossed = [], set(), []

        def arrive(k):
            copies[k].wait_recv()
            arrived.add(k)
            here = block(ARRIVES[k])
            crossed.append(
                send(here, here, core_send.at[k], core_recv.at[k], {"fsdp": core_partner()})
            )

        for k, (place, target, after) in enumerate(GATHER):
            if after is not None and after not in arrived:
                yield
                arrive(after)
            copies.append(
                send(
                    src if place == (0, 0) else block(place),
                    block(place),
                    send_sem.at[k],
                    recv_sem.at[k],
                    {"fsdp": fsdp_at(*target)},
                )
            )
        crossed.append(
            send(src, block((0, 0)), core_send.at[7], core_recv.at[7], {"fsdp": core_partner()})
        )
        for k in range(7):
            if k not in arrived:
                yield
                arrive(k)
        yield
        for copy in copies:
            copy.wait_send()
        for copy in crossed:
            copy.wait()
        own.wait()


class SumFsdp:
    def __init__(self, columns, dtype):
        blocks = pltpu.VMEM((8, BLOCK, columns), dtype)
        self.scratch = [dma(7), dma(7), dma(2), blocks, blocks]

    def run(self, src, out, send_sem, recv_sem, core_sem, pair, landed):
        core = lax.rem(lax.axis_index("fsdp"), 2)
        across = send(
            src.at[:, 1 - core], pair, core_sem.at[0], core_sem.at[1], {"fsdp": core_partner()}
        )
        yield
        across.wait_recv()

        @pl.loop(0, 8)
        def _(chip):
            pair[chip] = (src[chip, core].astype(F32) + pair[chip].astype(F32)).astype(pair.dtype)

        copies = []
        for k, place in enumerate(EVERY):
            device = fsdp_at(*place)
            copies.append(
                send(pair.at[device // 2], landed.at[k], send_sem.at[k], recv_sem.at[k], {"fsdp": device})
            )
        yield
        value = pair[lax.axis_index("fsdp") // 2].astype(F32)
        for k, copy in enumerate(copies):
            copy.wait_recv()
            value = value + landed[k].astype(F32)
        out[...] = value
        across.wait_send()
        for copy in copies:
            copy.wait_send()


class SumChips:
    def __init__(self, kind):
        self.kind = kind
        self.scratch = [
            dma(7),
            dma(7),
            dma(4),
            pltpu.VMEM((4, LOCAL, BLOCK, HIDDEN), BF16),
            pltpu.VMEM((7, LOCAL, BLOCK, HIDDEN), BF16),
        ]

    def run(self, src, out, send_sem, recv_sem, own_sem, own, landed):
        def block(place):
            return src.at[:, self.kind, fsdp_at(*place) // 2]

        def total(k, others, dst):
            @pl.loop(0, LOCAL * (BLOCK // 16))
            def _(i):
                expert, at = i // (BLOCK // 16), pl.multiple_of(lax.rem(i, BLOCK // 16) * 16, 16)
                value = own[k, expert, pl.ds(at, 16), :].astype(F32)
                for other in others:
                    value = value + landed[other, expert, pl.ds(at, 16), :].astype(F32)
                dst[expert, pl.ds(at, 16), :] = value.astype(dst.dtype)

        copies, arrived, kept = [], set(), []
        for k, (place, target, others) in enumerate(SUM):
            if others:
                yield
                for other in others:
                    copies[other].wait_recv()
                kept[k - 4].wait()
                part = landed.at[others[0]]
                total(k - 4, others, part)
            else:
                part = block(place)
            copies.append(
                send(part, landed.at[k], send_sem.at[k], recv_sem.at[k], {"fsdp": fsdp_at(*target)})
            )
            if k == 3:
                for place in [place for place, _, _ in SUM[4:]] + [(0, 0)]:
                    j = len(kept)
                    kept.append(pltpu.make_async_copy(block(place), own.at[j], own_sem.at[j]))
                    kept[j].start()
        yield
        for k in LAST:
            copies[k].wait_recv()
        kept[3].wait()
        total(3, LAST, out)
        for copy in copies:
            copy.wait_send()


class SumAll:
    def __init__(self, columns):
        self.over_fsdp = SumFsdp(columns, F32)
        self.scratch = self.over_fsdp.scratch + [
            pltpu.VMEM((BLOCK, columns), F32),
            dma(7),
            dma(7),
            pltpu.VMEM((7, 8, columns), F32),
        ]

    def run(self, src, out, *scratch):
        total, send_sem, recv_sem, landed = scratch[-4:]
        yield from self.over_fsdp.run(src, total, *scratch[:-4])

        def rows(tp):
            return pl.ds(pl.multiple_of(tp * 8, 8), 8)

        copies = []
        for k, place in enumerate(EVERY):
            peer = tp_at(*place)
            copies.append(
                send(total.at[rows(peer)], landed.at[k], send_sem.at[k], recv_sem.at[k], {"tp": peer})
            )
        yield
        value = total[rows(lax.axis_index("tp")), :]
        for k, copy in enumerate(copies):
            copy.wait()
            value = value + landed[k]
        out[...] = value


def pump(runs):
    for run in list(runs):
        if next(run, "done") == "done":
            runs.remove(run)
    return bool(runs)


def drain(run, behind=(), steps=1):
    for _ in run:
        for _ in range(steps):
            pump(behind)


def part(ref, index):
    return ref.at[pl.ds(pl.multiple_of(index * ROWS, ROWS), ROWS)]


def run_task(task, scratch, src, out):
    count = len(task.scratch)
    mine, scratch[:] = scratch[:count], scratch[count:]
    return task.run(src, out, *mine)


def dot(a, b, dims=((1,), (0,))):
    return lax.dot_general(a, b, (dims, ((), ())), preferred_element_type=F32)


def lanes(rows):
    return lax.broadcasted_iota(jnp.int32, (rows, 128), 1)


def turn(values):
    low_half = lax.rem(lanes(values.shape[0]), HEAD_DIM) < HEAD_DIM // 2
    return jnp.where(low_half, pltpu.roll(values, 96, 1), pltpu.roll(values, 32, 1))


def both_halves(pair):
    low = lanes(pair.shape[0]) < HEAD_DIM
    other = pltpu.roll(pair, HEAD_DIM, 1)
    return jnp.where(low, pair, other), jnp.where(low, other, pair)


def head_lanes(values, head):
    return jnp.where(lanes(values.shape[0]) // HEAD_DIM == head, values, 0.0)


def doc_of(position, lengths):
    first = lengths[0, 0]
    return jnp.where(position >= first, 1, 0) + jnp.where(position >= first + lengths[0, 1], 1, 0)


def allowed(keys, first, lengths):
    key_at = lax.broadcasted_iota(jnp.int32, (keys, 1), 0)
    query_at = first + lax.broadcasted_iota(jnp.int32, (1, QUERIES), 1)
    return (key_at <= query_at) & (doc_of(key_at, lengths) == doc_of(query_at, lengths))


def inverse_root(values):
    return lax.rsqrt(jnp.mean(values * values, axis=-1, keepdims=True) + eps_norm)


def rms_back(grad_out, unit, inverse, gain):
    grad_unit = grad_out * gain
    return inverse * (grad_unit - unit * jnp.mean(grad_unit * unit, axis=-1, keepdims=True))


def key_tables(cosine, sine):
    key = lanes(cosine.shape[0]) < HEAD_DIM
    return jnp.where(key, cosine, 1.0), jnp.where(key, sine, 0.0)


QUERIES = 256


def attend(x_ref, w_ref, gain_ref, cos_ref, sin_ref, lengths, normed_ref, query_ref, pair_ref, lse_ref, mixed_ref, mixed_t, mixed_rows, between):
    @pl.loop(0, GROUP // 128)
    def _(i):
        rows = pl.ds(pl.multiple_of(i * 128, 128), 128)
        x = x_ref[rows, :].astype(F32)
        normed = (x * inverse_root(x) * gain_ref[0:1, :]).astype(BF16)
        normed_ref[rows, :] = normed
        raw = dot(normed, w_ref[0, :, 0:256])
        query, pair = raw[:, 0:128], raw[:, 128:256]
        cosine, sine = cos_ref[rows, :], sin_ref[rows, :]
        query_ref[rows, :] = (query * cosine + turn(query) * sine).astype(BF16)
        cosine, sine = key_tables(cosine, sine)
        pair_ref[rows, :] = (pair * cosine + turn(pair) * sine).astype(BF16)

    between()
    keys, values = both_halves(pair_ref[...].astype(F32))
    keys, values_t = keys.astype(BF16), values.T.astype(BF16)

    for first in range(0, GROUP, QUERIES):
        count = first + QUERIES
        mask = allowed(count, first, lengths)
        for head in range(2):
            query = head_lanes(query_ref[first : first + QUERIES, :].astype(F32), head).astype(BF16)
            scores = dot(keys[:count], query, ((1,), (1,))) * score_scale
            scores = jnp.where(mask, scores, -1e30)
            top = jnp.max(scores, axis=0, keepdims=True)
            raised = jnp.exp(scores - top)
            total = jnp.sum(raised, axis=0, keepdims=True)
            lse_ref[head : head + 1, first : first + QUERIES] = top + jnp.log(total)
            weights = (raised * (1.0 / total)).astype(BF16)
            mixed_t[HEAD_DIM * head : HEAD_DIM * (head + 1), first : first + QUERIES] = dot(
                values_t[HEAD_DIM * head : HEAD_DIM * (head + 1), :count], weights
            )
        between()
    mixed_ref[...] = mixed_t[...].astype(BF16)
    mixed_rows[...] = mixed_t[...].T.astype(BF16)


def attend_back(x_ref, w_ref, query_ref, pair_ref, lse_ref, cos_ref, sin_ref, lengths, grad_ref, gain_grad, dmixed_ref, dquery_t, dpair_ref, raw_ref, raw_t, between):
    keys, values = both_halves(pair_ref[...].astype(F32))
    keys_t = keys.T.astype(BF16)
    keys, values = keys.astype(BF16), values.astype(BF16)
    dpair_ref[...] = jnp.zeros_like(dpair_ref)

    for first in range(0, GROUP, QUERIES):
        count = first + QUERIES
        mask = allowed(count, first, lengths)
        for head in range(2):
            query = head_lanes(query_ref[first : first + QUERIES, :].astype(F32), head).astype(BF16)
            dmixed = head_lanes(dmixed_ref[first : first + QUERIES, :].astype(F32), head).astype(BF16)
            scores = dot(keys[:count], query, ((1,), (1,))) * score_scale
            scores = jnp.where(mask, scores, -1e30)
            weights = jnp.exp(scores - lse_ref[head : head + 1, first : first + QUERIES])
            dweights = dot(values[:count], dmixed, ((1,), (1,)))
            inner = jnp.sum(weights * dweights, axis=0, keepdims=True)
            dscores = (weights * (dweights - inner)).astype(BF16)
            dquery_t[HEAD_DIM * head : HEAD_DIM * (head + 1), first : first + QUERIES] = (
                dot(keys_t[HEAD_DIM * head : HEAD_DIM * (head + 1), :count], dscores) * score_scale
            )
            dpair_ref[0, :count, :] += dot(dscores, query) * score_scale
            dpair_ref[1, :count, :] += dot(weights.astype(BF16), dmixed)
        between()

    gain_grad[...] = jnp.zeros_like(gain_grad)

    @pl.loop(0, GROUP // 128)
    def _(i):
        at = pl.multiple_of(i * 128, 128)
        rows = pl.ds(at, 128)
        dquery = dquery_t[:, rows].T
        dkey, dvalue = dpair_ref[0, rows, :], dpair_ref[1, rows, :]
        dkey = dkey + pltpu.roll(dkey, HEAD_DIM, 1)
        dvalue = dvalue + pltpu.roll(dvalue, HEAD_DIM, 1)
        dpair = jnp.where(lanes(128) < HEAD_DIM, dkey, dvalue)
        cosine, sine = cos_ref[rows, :], sin_ref[rows, :]
        dquery = dquery * cosine + turn(dquery * sine)
        cosine, sine = key_tables(cosine, sine)
        dpair = dpair * cosine + turn(dpair * sine)
        raw_ref[rows, 0:128] = dquery.astype(BF16)
        raw_ref[rows, 128:256] = dpair.astype(BF16)
        raw_t[0:128, rows] = dquery.T.astype(BF16)
        raw_t[128:256, rows] = dpair.T.astype(BF16)
        dnormed = dot(raw_ref[rows, :], w_ref[0, :, 0:256], ((1,), (1,)))
        grad_ref[rows, :] = dnormed.astype(BF16)
        x = x_ref[rows, :].astype(F32)
        gain_grad[...] += jnp.sum(dnormed * (x * inverse_root(x)), axis=0, keepdims=True)


HEAD_TASKS = (
    GatherTp(ROWS, D),
    GatherFsdp(1, 512),
    GatherFsdp(LOCAL, HIDDEN),
    GatherFsdp(LOCAL, HIDDEN),
    GatherFsdp(LOCAL, HIDDEN),
    GatherTp(D, ROWS),
    ExchangeTp(),
    GatherTp(ROWS, D),
)


def head_body(
    lengths, x_ref, small_ref, gate_ref, up_ref, down_ref, routes_ref,
    x_out, w_out, gate_all, up_all, down_all, tokens,
    normed_out, query_out, pair_out, lse_ref, mixed_ref, middle_ref, own_ref, chosen_out, rank_out, rank_t_out, gains_ref, cos_out, sin_out, output_out,
    x_all, w_all, normed_ref, query_ref, pair_ref, chosen_ref, rank_ref, rank_t, cos_ref, sin_ref, store_sem,
    mixed_t, mixed_rows, mixed_own, output_all, *scratch,
):
    scratch = list(scratch)
    stores = []

    def store(src, dst):
        stores.append(pltpu.make_async_copy(src, dst, store_sem.at[len(stores)]))
        stores[-1].start()

    greet()
    pairs = (
        (x_ref, x_all), (small_ref, w_all), (gate_ref, gate_all), (up_ref, up_all), (down_ref, down_all),
        (w_all.at[0, :, 256:384], output_all),
        (functools.partial(part, mixed_rows), lambda tp: mixed_own.at[tp]), (own_ref, tokens),
    )
    x_run, w_run, gate_run, up_run, down_run, output_run, mixed_run, token_run = [
        run_task(task, scratch, *pair) for task, pair in zip(HEAD_TASKS, pairs)
    ]
    front = [x_run, w_run]
    pump(front)

    lane = lanes(GROUP)
    routes = routes_ref[...].astype(F32).T.astype(jnp.int32)
    chosen = lane == routes[:, 0:1]
    for k in range(1, 8):
        chosen = chosen | (lane == routes[:, k : k + 1])
    chosen = jnp.where(chosen, 1.0, 0.0)
    chosen_ref[...] = chosen
    pump(front)
    chosen = chosen.astype(BF16)
    for i in range(4):
        rows = slice(256 * i, 256 * (i + 1))
        later = 256 * i + lax.broadcasted_iota(jnp.int32, (256, GROUP), 0)
        until = jnp.where(later >= lax.broadcasted_iota(jnp.int32, (256, GROUP), 1), 1.0, 0.0)
        running = dot(until.astype(BF16), chosen)
        rank = jnp.where(chosen_ref[rows, :] > 0.0, running - 1.0, -1.0)
        rank_ref[rows, :] = rank
        rank_t[:, rows] = rank.T
    pump(front)
    position = lax.broadcasted_iota(jnp.int32, (GROUP, 1), 0)
    ends = (lengths[0, 0], lengths[0, 0] + lengths[0, 1])
    start = jnp.where(position >= ends[1], ends[1], jnp.where(position >= ends[0], ends[0], 0))
    half = lax.rem(lane[0:1], HEAD_DIM // 2).astype(F32)
    frequency = jnp.exp(half * (-2.0 / HEAD_DIM * math.log(rope_base)))
    angles = (position - start).astype(F32) * frequency
    cos_ref[...] = jnp.cos(angles)
    sine = jnp.sin(angles)
    sin_ref[...] = jnp.where(lax.rem(lane, HEAD_DIM) < HEAD_DIM // 2, -sine, sine)
    for pair in ((chosen_ref, chosen_out), (rank_ref, rank_out), (rank_t, rank_t_out), (cos_ref, cos_out), (sin_ref, sin_out)):
        store(*pair)
    drain(w_run)
    behind = [gate_run, up_run, down_run]
    pump(behind)
    store(w_all, w_out)
    gains_ref[...] = w_all[0, :, 384:512].astype(F32).T[32:40, :]
    drain(x_run)
    pump(behind)
    store(x_all, x_out)
    far = [output_run]
    pump(far)
    calls = [0]

    def between():
        calls[0] += 1
        if calls[0] in (3, 4, 5):
            pump(far)
        if calls[0] in (2, 5):
            pump(behind)

    attend(
        x_all, w_all, gains_ref, cos_ref, sin_ref, lengths,
        normed_ref, query_ref, pair_ref, lse_ref, mixed_ref, mixed_t, mixed_rows, between,
    )
    next(mixed_run)
    store(normed_ref, normed_out)
    store(query_ref, query_out)
    store(pair_ref, pair_out)
    drain(output_run)
    store(output_all, output_out)
    drain(mixed_run)
    middle = x_ref[...].astype(F32)
    for tp in range(8):
        middle = middle + dot(mixed_own[tp], output_all[tp * D : (tp + 1) * D, :], ((1,), (1,)))
    middle_ref[...] = middle
    own_ref[...] = (middle * inverse_root(middle) * gains_ref[1:2, :]).astype(BF16)
    next(token_run)
    pump(behind)
    pump(behind)
    drain(token_run, behind)
    while pump(behind):
        pass
    for copy in stores:
        copy.wait()


def head(lengths, x, small, gate, up, down, routes):
    def shape(*dims, dtype=BF16):
        return jax.ShapeDtypeStruct(dims, dtype)

    vmem = pl.BlockSpec(memory_space=pltpu.VMEM)
    far = pl.BlockSpec(memory_space=pl.ANY)
    weight = shape(LOCAL, D, HIDDEN)
    return pl.pallas_call(
        head_body,
        name="head",
        out_shape=[
            shape(GROUP, D),
            shape(1, D, 512),
            weight,
            weight,
            weight,
            shape(GROUP, D),
            shape(GROUP, D),
            shape(GROUP, 128),
            shape(GROUP, 128),
            shape(2, GROUP, dtype=F32),
            shape(128, GROUP),
            shape(ROWS, D, dtype=F32),
            shape(ROWS, D),
            shape(GROUP, 128, dtype=F32),
            shape(GROUP, 128, dtype=F32),
            shape(128, GROUP, dtype=F32),
            shape(8, D, dtype=F32),
            shape(GROUP, 128, dtype=F32),
            shape(GROUP, 128, dtype=F32),
            shape(8 * D, ROWS),
        ],
        in_specs=[pl.BlockSpec(memory_space=pltpu.SMEM)] + [vmem] * 6,
        out_specs=[far] * 5 + [vmem] + [far] * 3 + [vmem] * 4 + [far] * 3 + [vmem] + [far] * 3,
        scratch_shapes=[
            pltpu.VMEM((GROUP, D), BF16),
            pltpu.VMEM((1, D, 512), BF16),
            pltpu.VMEM((GROUP, D), BF16),
            pltpu.VMEM((GROUP, 128), BF16),
            pltpu.VMEM((GROUP, 128), BF16),
            pltpu.VMEM((GROUP, 128), F32),
            pltpu.VMEM((GROUP, 128), F32),
            pltpu.VMEM((128, GROUP), F32),
            pltpu.VMEM((GROUP, 128), F32),
            pltpu.VMEM((GROUP, 128), F32),
            dma(12),
            pltpu.VMEM((128, GROUP), F32),
            pltpu.VMEM((GROUP, 128), BF16),
            pltpu.VMEM((8, ROWS, 128), BF16),
            pltpu.VMEM((8 * D, ROWS), BF16),
        ]
        + [buffer for task in HEAD_TASKS for buffer in task.scratch],
        compiler_params=pltpu.CompilerParams(
            collective_id=1, has_side_effects=True, vmem_limit_bytes=56 * 2**20
        ),
    )(lengths, x, small, gate, up, down, routes)


TAIL_TASKS = (
    SumTp(ROWS, WIDE),
    SumChips(0),
    SumChips(1),
    SumChips(2),
    ExchangeTp(),
    GatherTp(ROWS, D),
    SumTp(ROWS, D),
    SumFsdp(384, BF16),
    SumAll(128),
)


def tail_body(
    lengths, grads_ref, moe_sum, pairs_ref,
    x_ref, dy_ref, middle_ref, own_ref, chosen_ref, gains_ref, lse_ref, mixed_ref,
    x_in, w_in, normed_in, query_in, pair_in, cos_in, sin_in, output_in,
    outputs_ref, input_grad, small_grad, attention_grad, gate_grad, up_grad, down_grad,
    x_all, w_all, normed_ref, query_ref, pair_ref, cos_ref, sin_ref, output_all, dmixed_own, load_sem,
    grads_sum, datt_own, datt_all, dmiddle_ref, dnormed_part, dnormed_sum, weights_part, small_part, gain_grads,
    gain_row, dmixed_ref, dquery_t, dpair_ref, raw_ref, raw_t, *scratch,
):
    scratch = list(scratch)
    greet()
    pairs = (
        (grads_ref, grads_sum), (pairs_ref, gate_grad), (pairs_ref, up_grad), (pairs_ref, down_grad),
        (lambda tp: dmixed_own.at[tp], functools.partial(part, dmixed_ref)),
        (datt_own, datt_all), (dnormed_part, dnormed_sum),
        (weights_part, attention_grad), (small_part, small_grad),
    )
    grads_run, gate_run, up_run, down_run, dmixed_run, datt_run, dnormed_run, weights_run, small_run = [
        run_task(task, scratch, *pair) for task, pair in zip(TAIL_TASKS, pairs)
    ]
    behind = [gate_run, up_run, down_run]
    next(grads_run)
    pump(behind)
    loads = []
    for k, (src, dst) in enumerate(
        (
            (w_in, w_all), (x_in, x_all), (normed_in, normed_ref), (query_in, query_ref),
            (pair_in, pair_ref), (cos_in, cos_ref), (sin_in, sin_ref), (output_in, output_all),
        )
    ):
        loads.append(pltpu.make_async_copy(src, dst, load_sem.at[k]))
        loads[k].start()
    drain(grads_run)

    for copy in loads:
        copy.wait()
    middle = middle_ref[...]
    inverse = inverse_root(middle)
    unit = middle * inverse
    router = w_all[0, :, 384:512]
    own_rows = pl.ds(pl.multiple_of(lax.axis_index("tp") * ROWS, ROWS), ROWS)
    logits = jnp.where(chosen_ref[own_rows, :] > 0.0, dot(own_ref[...], router), -1e30)
    raised = jnp.exp(logits - jnp.max(logits, axis=-1, keepdims=True))
    gates = raised / jnp.sum(raised, axis=-1, keepdims=True)
    dgates = grads_sum[:, D:WIDE]
    dlogits = gates * (dgates - jnp.sum(gates * dgates, axis=-1, keepdims=True))
    dlogits = dlogits.astype(BF16)
    dtokens = grads_sum[:, 0:D] + dot(dlogits, router, ((1,), (1,)))
    dmiddle = dy_ref[...].astype(F32) + rms_back(dtokens, unit, inverse, gains_ref[1:2, :])
    dmiddle_ref[...] = dmiddle
    datt_own[...] = dmiddle.astype(BF16)
    for tp in range(8):
        dmixed_own[tp] = dot(datt_own[...], output_all[tp * D : (tp + 1) * D, :]).astype(BF16)
    next(dmixed_run)
    next(datt_run)
    pump(behind)
    pump(behind)
    small_part[...] = dot(own_ref[...], dlogits, ((0,), (0,))).reshape(small_part.shape)
    gain_grads[...] = jnp.zeros_like(gain_grads)
    gain_grads[EXPERTS : EXPERTS + 1, :] = jnp.sum(dtokens * unit, axis=0, keepdims=True)
    drain(dmixed_run)
    far = [datt_run]
    pump(far)
    calls = [0]

    def between():
        calls[0] += 1
        if calls[0] in (2, 3, 4):
            pump(far)
        if calls[0] == 2:
            pump(behind)

    attend_back(
        x_all, w_all, query_ref, pair_ref, lse_ref, cos_ref, sin_ref, lengths,
        dnormed_part, gain_row, dmixed_ref, dquery_t, dpair_ref, raw_ref, raw_t, between,
    )
    next(dnormed_run)
    gain_grads[EXPERTS + 1 : EXPERTS + 2, :] = gain_row[...]
    small_part[...] += gain_grads[...].T.reshape(small_part.shape)
    next(small_run)
    drain(datt_run)

    @pl.loop(0, 4)
    def _(i):
        at = pl.ds(pl.multiple_of(i * 256, 256), 256)
        chips = pl.ds(i * 2, 2)
        into_qkv = dot(raw_t[...], normed_ref[:, at]).T.astype(BF16)
        weights_part[chips, :, :, 0:256] = into_qkv.reshape(2, 2, BLOCK, 256)
        into_output = dot(mixed_ref[...], datt_all[:, at]).T.astype(BF16)
        weights_part[chips, :, :, 256:384] = into_output.reshape(2, 2, BLOCK, 128)

    last = [dnormed_run, weights_run, small_run] + behind
    while pump(last):
        pass
    outputs_ref[...] = (middle_ref[...] + moe_sum[...]).astype(BF16)
    x = x_ref[...].astype(F32)
    inverse = inverse_root(x)
    input_grad[...] = dmiddle_ref[...] + rms_back(dnormed_sum[...], x * inverse, inverse, gains_ref[0:1, :])


def tail(*arrays):
    def shape(*dims, dtype=F32):
        return jax.ShapeDtypeStruct(dims, dtype)

    vmem = pl.BlockSpec(memory_space=pltpu.VMEM)
    far = pl.BlockSpec(memory_space=pl.ANY)
    weight = shape(LOCAL, BLOCK, HIDDEN)
    return pl.pallas_call(
        tail_body,
        name="tail",
        out_shape=[
            shape(ROWS, D, dtype=BF16),
            shape(ROWS, D),
            shape(8, 128),
            shape(BLOCK, 384),
            weight,
            weight,
            weight,
        ],
        in_specs=[pl.BlockSpec(memory_space=pltpu.SMEM)] + [vmem] * 2 + [far] + [vmem] * 8 + [far] * 8,
        out_specs=[vmem] * 7,
        scratch_shapes=[
            pltpu.VMEM((GROUP, D), BF16),
            pltpu.VMEM((1, D, 512), BF16),
            pltpu.VMEM((GROUP, D), BF16),
            pltpu.VMEM((GROUP, 128), BF16),
            pltpu.VMEM((GROUP, 128), BF16),
            pltpu.VMEM((GROUP, 128), F32),
            pltpu.VMEM((GROUP, 128), F32),
            pltpu.VMEM((8 * D, ROWS), BF16),
            pltpu.VMEM((8, ROWS, 128), BF16),
            dma(9),
            pltpu.VMEM((ROWS, WIDE), F32),
            pltpu.VMEM((ROWS, D), BF16),
            pltpu.VMEM((GROUP, D), BF16),
            pltpu.VMEM((ROWS, D), F32),
            pltpu.VMEM((GROUP, D), BF16),
            pltpu.VMEM((ROWS, D), F32),
            pltpu.VMEM((8, 2, BLOCK, 384), BF16),
            pltpu.VMEM((8, 2, BLOCK, 128), F32),
            pltpu.VMEM((128, D), F32),
            pltpu.VMEM((1, D), F32),
            pltpu.VMEM((GROUP, 128), BF16),
            pltpu.VMEM((128, GROUP), F32),
            pltpu.VMEM((2, GROUP, 128), F32),
            pltpu.VMEM((GROUP, 256), BF16),
            pltpu.VMEM((256, GROUP), BF16),
        ]
        + [buffer for task in TAIL_TASKS for buffer in task.scratch],
        compiler_params=pltpu.CompilerParams(
            collective_id=2, has_side_effects=True, vmem_limit_bytes=62 * 2**20
        ),
    )(*arrays)


class StepGather:
    scratch = [dma(7), dma(7), pltpu.SemaphoreType.DMA(())]

    def __init__(self, src, out, send_sem, recv_sem, own_sem):
        self.src, self.out, self.send_sem, self.recv_sem = src, out, send_sem, recv_sem
        self.own = pltpu.make_async_copy(src, part(out, lax.axis_index("tp")), own_sem)

    def copy(self, k):
        place, target, _ = GATHER[k]
        block = part(self.out, tp_at(*place))
        return pltpu.make_async_remote_copy(
            src_ref=self.src if place == (0, 0) else block,
            dst_ref=block,
            send_sem=self.send_sem.at[k],
            recv_sem=self.recv_sem.at[k],
            device_id={"tp": tp_at(*target)},
            device_id_type=MESH,
        )

    def stage(self, number):
        if number == 0:
            self.own.start()
            for k in (0, 1, 2):
                self.copy(k).start()
        elif number == 1:
            self.copy(0).wait_recv()
            self.copy(3).start()
            self.copy(4).start()
        elif number == 2:
            self.copy(1).wait_recv()
            self.copy(5).start()
            self.copy(4).wait_recv()
            self.copy(6).start()
        else:
            for k in (2, 3, 5, 6):
                self.copy(k).wait_recv()
            for k in range(7):
                self.copy(k).wait_send()
            self.own.wait()


class StepSum:
    scratch = [dma(7), dma(7), pltpu.VMEM((7, ROWS, D), BF16)]

    def __init__(self, src, out, send_sem, recv_sem, landed):
        self.src, self.out, self.landed = src, out, landed
        self.send_sem, self.recv_sem = send_sem, recv_sem

    def copy(self, k):
        place, target, others = SUM[k]
        return pltpu.make_async_remote_copy(
            src_ref=self.landed.at[others[0]] if others else part(self.src, tp_at(*place)),
            dst_ref=self.landed.at[k],
            send_sem=self.send_sem.at[k],
            recv_sem=self.recv_sem.at[k],
            device_id={"tp": tp_at(*target)},
            device_id_type=MESH,
        )

    def total(self, place, others, dst):
        start = tp_at(*place) * ROWS

        @pl.loop(0, ROWS // 16)
        def _(i):
            at = pl.multiple_of(i * 16, 16)
            value = self.src[pl.ds(pl.multiple_of(start + at, 16), 16), :].astype(F32)
            for k in others:
                value = value + self.landed[k, pl.ds(at, 16), :].astype(F32)
            dst[pl.ds(at, 16), :] = value.astype(dst.dtype)

    def relay(self, k):
        place, _, others = SUM[k]
        for other in others:
            self.copy(other).wait_recv()
        self.total(place, others, self.landed.at[others[0]])
        self.copy(k).start()

    def stage(self, number):
        if number == 0:
            for k in range(4):
                self.copy(k).start()
        elif number == 1:
            self.relay(4)
            self.relay(5)
        elif number == 2:
            self.relay(6)
        else:
            for k in LAST:
                self.copy(k).wait_recv()
            self.total((0, 0), LAST, self.out)
            for k in range(7):
                self.copy(k).wait_send()


def experts_body(
    tokens_ref, dy_ref, router_ref, chosen_ref, rank_ref, rank_t,
    gate_ref, up_ref, down_ref,
    moe_ref, grad_ref, pair_ref,
    give_all, slots_all, dgate_all, gates_ref, parts, got, send_sem, recv_sem,
    picked_all, gate_parts, up_parts, slot_gates, dy_all, combined_ref, *scratch,
):
    step = pl.program_id(0)
    lane = lax.broadcasted_iota(jnp.int32, (1, 128), 1)
    core = lax.rem(lax.axis_index("fsdp"), 2)
    dy_gather = StepGather(dy_ref, dy_all, *scratch[:3])
    moe_sum = StepSum(combined_ref, moe_ref, *scratch[3:])
    local = lax.rem(step, LOCAL)
    expert = lax.axis_index("tp") * LOCAL + local
    expert_lane = lane == expert
    rows = pl.ds(pl.multiple_of(local * PLACES, PLACES), SLOTS)

    def take():
        slot = lax.broadcasted_iota(jnp.int32, (SLOTS, GROUP), 0)
        return jnp.where(slot == rank_t[pl.ds(expert, 1), :].astype(jnp.int32), 1.0, 0.0).astype(BF16)

    def across(number):
        slot = lax.rem(number, 2)
        return pltpu.make_async_remote_copy(
            src_ref=parts.at[slot, :, :, 1 - core],
            dst_ref=got.at[number],
            send_sem=send_sem.at[slot],
            recv_sem=recv_sem.at[number],
            device_id={"fsdp": core_partner()},
            device_id_type=MESH,
        )

    @pl.when(step == 0)
    def _():
        barrier = pltpu.get_barrier_semaphore()
        for device in ({"tp": tp_at(1, 0)}, {"tp": tp_at(3, 0)}, {"tp": tp_at(0, 1)}, {"fsdp": core_partner()}):
            pl.semaphore_signal(barrier, inc=1, device_id=device, device_id_type=MESH)
        pl.semaphore_wait(barrier, 4)
        dy_gather.stage(0)
        slots_all[...] = jnp.zeros_like(slots_all)
        dgate_all[...] = jnp.zeros_like(dgate_all)
        logits = jnp.where(chosen_ref[...] > 0.0, dot(tokens_ref[...], router_ref[0]), -1e30)
        raised = jnp.exp(logits - jnp.max(logits, axis=-1, keepdims=True))
        gates = raised / jnp.sum(raised, axis=-1, keepdims=True)
        high = gates.astype(BF16)
        gates_ref[:, 0:128] = high
        gates_ref[:, 128:256] = (gates - high.astype(F32)).astype(BF16)

    for number, at in ((1, 1), (2, 2), (3, LOCAL)):
        pl.when(step == at)(functools.partial(dy_gather.stage, number))

    @pl.when(step < LOCAL)
    def _():
        taken = take()
        slot_gate = dot(taken, gates_ref[...])
        slot_gate = jnp.where(expert_lane, slot_gate[:, 0:128] + slot_gate[:, 128:256], 0.0)
        slot_gate = jnp.sum(slot_gate, axis=1, keepdims=True)
        slot_gates[local] = jnp.broadcast_to(slot_gate, (SLOTS, 128))
        picked = dot(taken, tokens_ref[...]).astype(BF16)
        picked_all[local] = picked
        gate_part = dot(picked, gate_ref[0])
        up_part = dot(picked, up_ref[0])
        gate_parts[local] = gate_part
        up_parts[local] = up_part
        hidden = gate_part * (1.0 / (1.0 + jnp.exp(-gate_part))) * up_part
        weighted = (hidden * slot_gate).astype(BF16)
        slots_all[rows, :] = dot(weighted, down_ref[0], ((1,), (1,))).astype(BF16)
        rank_column = jnp.sum(jnp.where(expert_lane, rank_ref[...], 0.0), axis=1, keepdims=True)
        place = lax.broadcasted_iota(jnp.int32, (GROUP, PLACES), 1)
        give = jnp.where(place == rank_column.astype(jnp.int32), 1.0, 0.0)
        give_all[:, pl.ds(pl.multiple_of(local * PLACES, PLACES), PLACES)] = give.astype(BF16)

    @pl.when(step == LOCAL - 1)
    def _():
        for i in range(4):
            columns = slice(256 * i, 256 * (i + 1))
            combined_ref[:, columns] = dot(give_all[...], slots_all[:, columns]).astype(BF16)
        moe_sum.stage(0)

    for number, at in ((1, LOCAL + 2), (2, LOCAL + 3)):
        pl.when(step == at)(functools.partial(moe_sum.stage, number))

    @pl.when((step >= LOCAL) & (step < 2 * LOCAL))
    def _():
        slot_gate = slot_gates[local][:, 0:1]
        gate_part, up_part = gate_parts[local], up_parts[local]
        sigmoid = 1.0 / (1.0 + jnp.exp(-gate_part))
        silu = gate_part * sigmoid
        hidden = silu * up_part
        dy = dot(take(), dy_all[...]).astype(BF16)
        dhidden = dot(dy, down_ref[0])
        dgate = jnp.sum(hidden * dhidden, axis=1, keepdims=True)
        weighted = (hidden * slot_gate).astype(BF16)
        dhidden = dhidden * slot_gate
        dgate_part = (dhidden * up_part * (sigmoid * (1.0 + gate_part * (1.0 - sigmoid)))).astype(BF16)
        dup_part = (dhidden * silu).astype(BF16)

        @pl.when(local >= 2)
        def _():
            across(local - 2).wait_send()

        slot_now = lax.rem(local, 2)
        picked_t, dy_t = picked_all[local].T, dy.T
        for k, (left, right) in enumerate(
            ((picked_t, dgate_part), (picked_t, dup_part), (dy_t, weighted))
        ):
            parts[slot_now, k] = dot(left, right).astype(BF16).reshape(8, 2, BLOCK, HIDDEN)
        across(local).start()
        dpicked = dot(dgate_part, gate_ref[0], ((1,), (1,)))
        slots_all[rows, :] = (dpicked + dot(dup_part, up_ref[0], ((1,), (1,)))).astype(BF16)
        dgate_all[rows, :] = jnp.where(expert_lane, dgate, 0.0).astype(BF16)

    @pl.when(step == 2 * LOCAL)
    def _():
        for i in range(4):
            columns = slice(256 * i, 256 * (i + 1))
            grad_ref[:, columns] = dot(give_all[...], slots_all[:, columns]).astype(BF16)
        grad_ref[:, D:WIDE] = dot(give_all[...], dgate_all[...]).astype(BF16)
        moe_sum.stage(3)

    @pl.when(step >= LOCAL + 1)
    def _():
        before = step - LOCAL - 1
        across(before).wait_recv()
        slot_before = lax.rem(before, 2)

        @pl.loop(0, 24)
        def _(i):
            kind, chip = i // 8, lax.rem(i, 8)
            total = parts[slot_before, kind, chip, core].astype(F32) + got[before, kind, chip].astype(F32)
            pair_ref[0, kind, chip] = total.astype(BF16)

    @pl.when(step == 2 * LOCAL)
    def _():
        for number in (LOCAL - 2, LOCAL - 1):
            across(number).wait_send()


def experts(tokens, dy, router, chosen, rank, rank_t, gate, up, down):
    def whole(*shape):
        return pl.BlockSpec(shape, lambda i: (0,) * len(shape))

    def own(*shape):
        return pl.BlockSpec(
            (1,) + shape,
            lambda i: (lax.rem(jnp.minimum(i, 2 * LOCAL - 1), LOCAL),) + (0,) * len(shape),
        )

    slots = LOCAL * PLACES
    return pl.pallas_call(
        experts_body,
        name="experts",
        grid=(2 * LOCAL + 1,),
        in_specs=[
            whole(GROUP, D),
            whole(ROWS, D),
            pl.BlockSpec((1, D, 128), lambda i: (0, 0, 3)),
            whole(GROUP, 128),
            whole(GROUP, 128),
            whole(128, GROUP),
            own(D, HIDDEN),
            own(D, HIDDEN),
            own(D, HIDDEN),
        ],
        out_specs=[
            whole(ROWS, D),
            whole(GROUP, WIDE),
            pl.BlockSpec(
                (1, 3, 8, BLOCK, HIDDEN), lambda i: (jnp.maximum(i - LOCAL - 1, 0), 0, 0, 0, 0)
            ),
        ],
        scratch_shapes=[
            pltpu.VMEM((GROUP, slots), BF16),
            pltpu.VMEM((slots, D), BF16),
            pltpu.VMEM((slots, 128), BF16),
            pltpu.VMEM((GROUP, 256), BF16),
            pltpu.VMEM((2, 3, 8, 2, BLOCK, HIDDEN), BF16),
            pltpu.VMEM((LOCAL, 3, 8, BLOCK, HIDDEN), BF16),
            dma(2),
            dma(LOCAL),
            pltpu.VMEM((LOCAL, SLOTS, D), BF16),
            pltpu.VMEM((LOCAL, SLOTS, HIDDEN), F32),
            pltpu.VMEM((LOCAL, SLOTS, HIDDEN), F32),
            pltpu.VMEM((LOCAL, SLOTS, 128), F32),
            pltpu.VMEM((GROUP, D), BF16),
            pltpu.VMEM((GROUP, D), BF16),
        ]
        + StepGather.scratch
        + StepSum.scratch,
        out_shape=[
            jax.ShapeDtypeStruct((ROWS, D), F32),
            jax.ShapeDtypeStruct((GROUP, WIDE), BF16),
            jax.ShapeDtypeStruct((LOCAL, 3, 8, BLOCK, HIDDEN), BF16),
        ],
        compiler_params=pltpu.CompilerParams(
            collective_id=3, has_side_effects=True, vmem_limit_bytes=62 * 2**20
        ),
    )(tokens, dy, router, chosen, rank, rank_t, gate, up, down)


def finish_body(*refs):
    sources, outs = refs[:7], refs[7:19]
    small, attention, sems = refs[19:]
    copies = []
    for k, (source, target) in enumerate(
        zip(sources, (outs[0], outs[1], small, attention, outs[9], outs[10], outs[11]))
    ):
        copies.append(pltpu.make_async_copy(source, target, sems.at[k]))
        copies[k].start()
    for copy in copies:
        copy.wait()
    outs[2][...] = attention[:, 0:128]
    outs[3][...] = attention[:, 128:192]
    outs[4][...] = attention[:, 192:256]
    outs[5][...] = attention[:, 256:384].T
    outs[6][...] = small[:, 0:EXPERTS]
    columns = small[...].T
    outs[7][...] = columns[EXPERTS + 1 : EXPERTS + 2, :]
    outs[8][...] = columns[EXPERTS : EXPERTS + 1, :]


def finish(*arrays):
    def shape(*dims, dtype=F32):
        return jax.ShapeDtypeStruct(dims, dtype)

    vmem = pl.BlockSpec(memory_space=pltpu.VMEM)
    far = pl.BlockSpec(memory_space=pl.ANY)
    return pl.pallas_call(
        finish_body,
        name="finish",
        out_shape=[
            shape(ROWS, D, dtype=BF16),
            shape(ROWS, D),
            shape(BLOCK, 128),
            shape(BLOCK, BLOCK),
            shape(BLOCK, BLOCK),
            shape(128, BLOCK),
            shape(8, EXPERTS),
            shape(1, 8),
            shape(1, 8),
        ]
        + [shape(LOCAL, BLOCK, HIDDEN)] * 3,
        in_specs=[far] * 7,
        out_specs=[vmem] * 12,
        scratch_shapes=[pltpu.VMEM((8, 128), F32), pltpu.VMEM((BLOCK, 384), F32), dma(7)],
        compiler_params=pltpu.CompilerParams(vmem_limit_bytes=60 * 2**20),
    )(*arrays)


def per_device(
    inputs,
    lengths,
    routes,
    attn_gain,
    query_weight,
    key_weight,
    value_weight,
    output_weight,
    moe_gain,
    router_weight,
    gate_weight,
    up_weight,
    down_weight,
    cotangent,
):
    small = jnp.concatenate(
        [
            query_weight,
            key_weight,
            value_weight,
            output_weight.T,
            router_weight,
            attn_gain[:, None],
            moe_gain[:, None],
            jnp.zeros((BLOCK, 128 - EXPERTS - 2), BF16),
        ],
        axis=1,
    )
    (
        x_all, w_all, gate_all, up_all, down_all, tokens,
        normed, query, pair, lse, mixed, middle, own, chosen, rank, rank_t, gains, cosine, sine, output_all,
    ) = head(
        lengths, inputs, small[None], gate_weight, up_weight, down_weight.transpose(0, 2, 1),
        routes.T,
    )
    moe, grads, pairs = experts(
        tokens, cotangent, w_all, chosen, rank, rank_t, gate_all, up_all, down_all
    )
    results = tail(
        lengths, grads, moe, pairs,
        inputs, cotangent, middle, own, chosen, gains, lse, mixed,
        x_all, w_all, normed, query, pair, cosine, sine, output_all,
    )
    (
        outputs, input_grad, query_grad, key_grad, value_grad, output_grad, router_grad, attn_gain_grad, moe_gain_grad,
        gate_grad, up_grad, down_grad,
    ) = finish(*results)
    return (
        outputs,
        input_grad,
        attn_gain_grad.reshape(8),
        query_grad,
        key_grad,
        value_grad,
        output_grad,
        moe_gain_grad.reshape(8),
        router_grad,
        gate_grad,
        up_grad,
        down_grad.transpose(0, 2, 1),
    )


def solution(mesh):
    return jax.shard_map(
        per_device,
        mesh=mesh,
        in_specs=(
            P(("fsdp", "tp"), None),
            P("fsdp", None),
            P("fsdp", None),
            P("fsdp"),
            P("fsdp", "tp"),
            P("fsdp", "tp"),
            P("fsdp", "tp"),
            P("tp", "fsdp"),
            P("fsdp"),
            P("fsdp", None),
            P("tp", "fsdp", None),
            P("tp", "fsdp", None),
            P("tp", None, "fsdp"),
            P(("fsdp", "tp"), None),
        ),
        out_specs=(
            P(("fsdp", "tp"), None),
            P(("fsdp", "tp"), None),
            P(("fsdp", "tp")),
            P("fsdp", "tp"),
            P("fsdp", "tp"),
            P("fsdp", "tp"),
            P("tp", "fsdp"),
            P(("fsdp", "tp")),
            P(("fsdp", "tp"), None),
            P("tp", "fsdp", None),
            P("tp", "fsdp", None),
            P("tp", None, "fsdp"),
        ),
        check_vma=False,
    )
```

```python
import functools
import math

import jax
import jax.numpy as jnp
from jax import lax
from jax.experimental import pallas as pl
from jax.experimental.pallas import tpu as pltpu
from jax.sharding import PartitionSpec as P

MESH = pl.DeviceIdType.MESH
D = 1024
HEAD_DIM = 64
EXPERTS = 32
HIDDEN = 512
GROUP = 1024
ROWS = 128
SLOTS = 352
PLACES = 384
LOCAL = 4
BLOCK = 64
WIDE = D + 128

eps_norm = 1e-06
rope_base = 10000.0
score_scale = 1.0 / HEAD_DIM
F32 = jnp.float32
BF16 = jnp.bfloat16


def tp_at(along, across):
    tp = lax.axis_index("tp")
    return lax.rem(tp // 2 + along, 4) * 2 + lax.rem(tp + across, 2)


def fsdp_at(along, across):
    fsdp = lax.axis_index("fsdp")
    chip = lax.rem(fsdp // 8 + across, 2) * 4 + lax.rem(fsdp // 2 + along, 4)
    return chip * 2 + lax.rem(fsdp, 2)


def core_partner():
    fsdp = lax.axis_index("fsdp")
    return fsdp // 2 * 2 + 1 - lax.rem(fsdp, 2)


def send(src, dst, send_sem, recv_sem, device):
    copy = pltpu.make_async_remote_copy(
        src_ref=src,
        dst_ref=dst,
        send_sem=send_sem,
        recv_sem=recv_sem,
        device_id=device,
        device_id_type=MESH,
    )
    copy.start()
    return copy


def greet():
    barrier = pltpu.get_barrier_semaphore()
    for place in EVERY:
        for device in ({"tp": tp_at(*place)}, {"fsdp": fsdp_at(*place)}):
            pl.semaphore_signal(barrier, inc=1, device_id=device, device_id_type=MESH)
    pl.semaphore_signal(barrier, inc=1, device_id={"fsdp": core_partner()}, device_id_type=MESH)
    pl.semaphore_wait(barrier, 15)


def dma(count):
    return pltpu.SemaphoreType.DMA((count,))


EVERY = ((2, 0), (2, 1), (1, 1), (3, 1), (1, 0), (3, 0), (0, 1))
GATHER = (
    ((0, 0), (0, 1), None),
    ((0, 0), (1, 0), None),
    ((0, 0), (3, 0), None),
    ((0, 1), (1, 0), 0),
    ((0, 1), (3, 0), 0),
    ((3, 0), (1, 0), 1),
    ((1, 1), (3, 0), 4),
)
ARRIVES = ((0, 1), (3, 0), (1, 0), (3, 1), (1, 1), (2, 0), (2, 1))
SUM = (
    ((2, 0), (1, 0), ()),
    ((2, 1), (3, 0), ()),
    ((1, 1), (1, 0), ()),
    ((3, 0), (3, 0), ()),
    ((1, 0), (1, 0), (0,)),
    ((3, 1), (3, 0), (1,)),
    ((0, 1), (0, 1), (2, 5)),
)
LAST = (3, 4, 6)


class GatherTp:
    def __init__(self, rows, columns):
        self.rows = rows
        self.scratch = [dma(7), dma(7), pltpu.SemaphoreType.DMA(())]

    def run(self, src, out, send_sem, recv_sem, own_sem):
        def block(place):
            return out.at[pl.ds(pl.multiple_of(tp_at(*place) * self.rows, self.rows), self.rows)]

        own = pltpu.make_async_copy(src, block((0, 0)), own_sem)
        own.start()
        copies, arrived = [], set()
        for k, (place, target, after) in enumerate(GATHER):
            if after is not None and after not in arrived:
                yield
                copies[after].wait_recv()
                arrived.add(after)
            copies.append(
                send(
                    src if place == (0, 0) else block(place),
                    block(place),
                    send_sem.at[k],
                    recv_sem.at[k],
                    {"tp": tp_at(*target)},
                )
            )
        yield
        for k, copy in enumerate(copies):
            if k not in arrived:
                copy.wait_recv()
            copy.wait_send()
        own.wait()


class SumTp:
    def __init__(self, rows, columns):
        self.rows = rows
        self.scratch = [dma(7), dma(7), pltpu.VMEM((7, rows, columns), BF16)]

    def run(self, src, out, send_sem, recv_sem, landed):
        def first(place):
            return pl.multiple_of(tp_at(*place) * self.rows, self.rows)

        def total(place, others, dst):
            start = first(place)

            @pl.loop(0, self.rows // 16)
            def _(i):
                at = pl.multiple_of(i * 16, 16)
                value = src[pl.ds(pl.multiple_of(start + at, 16), 16), :].astype(F32)
                for k in others:
                    value = value + landed[k, pl.ds(at, 16), :].astype(F32)
                dst[pl.ds(at, 16), :] = value.astype(dst.dtype)

        copies, arrived = [], set()
        for k, (place, target, others) in enumerate(SUM):
            if others:
                yield
                for other in others:
                    copies[other].wait_recv()
                    arrived.add(other)
                part = landed.at[others[0]]
                total(place, others, part)
            else:
                part = src.at[pl.ds(first(place), self.rows)]
            copies.append(
                send(part, landed.at[k], send_sem.at[k], recv_sem.at[k], {"tp": tp_at(*target)})
            )
        yield
        for k in LAST:
            copies[k].wait_recv()
        total((0, 0), LAST, out)
        for copy in copies:
            copy.wait_send()


class ExchangeTp:
    def __init__(self):
        self.scratch = [dma(7), dma(7), pltpu.SemaphoreType.DMA(())]

    def run(self, block, place, send_sem, recv_sem, own_sem):
        here = lax.axis_index("tp")
        copies = [
            send(block(peer), place(here), send_sem.at[k], recv_sem.at[k], {"tp": peer})
            for k, peer in enumerate(tp_at(*step) for step in EVERY)
        ]
        own = pltpu.make_async_copy(block(here), place(here), own_sem)
        own.start()
        yield
        for copy in copies:
            copy.wait()
        own.wait()


class GatherFsdp:
    def __init__(self, experts, columns):
        self.scratch = [dma(7), dma(7), dma(8), dma(8), pltpu.SemaphoreType.DMA(())]

    def run(self, src, out, send_sem, recv_sem, core_send, core_recv, own_sem):
        def block(place):
            return out.at[:, pl.ds(pl.multiple_of(fsdp_at(*place) * BLOCK, BLOCK), BLOCK)]

        own = pltpu.make_async_copy(src, block((0, 0)), own_sem)
        own.start()
        copies, arrived, crossed = [], set(), []

        def arrive(k):
            copies[k].wait_recv()
            arrived.add(k)
            here = block(ARRIVES[k])
            crossed.append(
                send(here, here, core_send.at[k], core_recv.at[k], {"fsdp": core_partner()})
            )

        for k, (place, target, after) in enumerate(GATHER):
            if after is not None and after not in arrived:
                yield
                arrive(after)
            copies.append(
                send(
                    src if place == (0, 0) else block(place),
                    block(place),
                    send_sem.at[k],
                    recv_sem.at[k],
                    {"fsdp": fsdp_at(*target)},
                )
            )
        crossed.append(
            send(src, block((0, 0)), core_send.at[7], core_recv.at[7], {"fsdp": core_partner()})
        )
        for k in range(7):
            if k not in arrived:
                yield
                arrive(k)
        yield
        for copy in copies:
            copy.wait_send()
        for copy in crossed:
            copy.wait()
        own.wait()


class SumFsdp:
    def __init__(self, columns, dtype):
        blocks = pltpu.VMEM((8, BLOCK, columns), dtype)
        self.scratch = [dma(7), dma(7), dma(2), blocks, blocks]

    def run(self, src, out, send_sem, recv_sem, core_sem, pair, landed):
        core = lax.rem(lax.axis_index("fsdp"), 2)
        across = send(
            src.at[:, 1 - core], pair, core_sem.at[0], core_sem.at[1], {"fsdp": core_partner()}
        )
        yield
        across.wait_recv()

        @pl.loop(0, 8)
        def _(chip):
            pair[chip] = (src[chip, core].astype(F32) + pair[chip].astype(F32)).astype(pair.dtype)

        copies = []
        for k, place in enumerate(EVERY):
            device = fsdp_at(*place)
            copies.append(
                send(pair.at[device // 2], landed.at[k], send_sem.at[k], recv_sem.at[k], {"fsdp": device})
            )
        yield
        value = pair[lax.axis_index("fsdp") // 2].astype(F32)
        for k, copy in enumerate(copies):
            copy.wait_recv()
            value = value + landed[k].astype(F32)
        out[...] = value
        across.wait_send()
        for copy in copies:
            copy.wait_send()


class SumChips:
    def __init__(self, kind):
        self.kind = kind
        self.scratch = [
            dma(7),
            dma(7),
            dma(4),
            pltpu.VMEM((4, LOCAL, BLOCK, HIDDEN), BF16),
            pltpu.VMEM((7, LOCAL, BLOCK, HIDDEN), BF16),
        ]

    def run(self, src, out, send_sem, recv_sem, own_sem, own, landed):
        def block(place):
            return src.at[:, self.kind, fsdp_at(*place) // 2]

        def total(k, others, dst):
            @pl.loop(0, LOCAL * (BLOCK // 16))
            def _(i):
                expert, at = i // (BLOCK // 16), pl.multiple_of(lax.rem(i, BLOCK // 16) * 16, 16)
                value = own[k, expert, pl.ds(at, 16), :].astype(F32)
                for other in others:
                    value = value + landed[other, expert, pl.ds(at, 16), :].astype(F32)
                dst[expert, pl.ds(at, 16), :] = value.astype(dst.dtype)

        copies, arrived, kept = [], set(), []
        for k, (place, target, others) in enumerate(SUM):
            if others:
                yield
                for other in others:
                    copies[other].wait_recv()
                kept[k - 4].wait()
                part = landed.at[others[0]]
                total(k - 4, others, part)
            else:
                part = block(place)
            copies.append(
                send(part, landed.at[k], send_sem.at[k], recv_sem.at[k], {"fsdp": fsdp_at(*target)})
            )
            if k == 3:
                for place in [place for place, _, _ in SUM[4:]] + [(0, 0)]:
                    j = len(kept)
                    kept.append(pltpu.make_async_copy(block(place), own.at[j], own_sem.at[j]))
                    kept[j].start()
        yield
        for k in LAST:
            copies[k].wait_recv()
        kept[3].wait()
        total(3, LAST, out)
        for copy in copies:
            copy.wait_send()


class SumAll:
    def __init__(self, columns):
        self.over_fsdp = SumFsdp(columns, F32)
        self.scratch = self.over_fsdp.scratch + [
            pltpu.VMEM((BLOCK, columns), F32),
            dma(7),
            dma(7),
            pltpu.VMEM((7, 8, columns), F32),
        ]

    def run(self, src, out, *scratch):
        total, send_sem, recv_sem, landed = scratch[-4:]
        yield from self.over_fsdp.run(src, total, *scratch[:-4])

        def rows(tp):
            return pl.ds(pl.multiple_of(tp * 8, 8), 8)

        copies = []
        for k, place in enumerate(EVERY):
            peer = tp_at(*place)
            copies.append(
                send(total.at[rows(peer)], landed.at[k], send_sem.at[k], recv_sem.at[k], {"tp": peer})
            )
        yield
        value = total[rows(lax.axis_index("tp")), :]
        for k, copy in enumerate(copies):
            copy.wait()
            value = value + landed[k]
        out[...] = value


def pump(runs):
    for run in list(runs):
        if next(run, "done") == "done":
            runs.remove(run)
    return bool(runs)


def drain(run, behind=(), steps=1):
    for _ in run:
        for _ in range(steps):
            pump(behind)


def part(ref, index):
    return ref.at[pl.ds(pl.multiple_of(index * ROWS, ROWS), ROWS)]


def run_task(task, scratch, src, out):
    count = len(task.scratch)
    mine, scratch[:] = scratch[:count], scratch[count:]
    return task.run(src, out, *mine)


def dot(a, b, dims=((1,), (0,))):
    return lax.dot_general(a, b, (dims, ((), ())), preferred_element_type=F32)


def lanes(rows):
    return lax.broadcasted_iota(jnp.int32, (rows, 128), 1)


def turn(values):
    low_half = lax.rem(lanes(values.shape[0]), HEAD_DIM) < HEAD_DIM // 2
    return jnp.where(low_half, pltpu.roll(values, 96, 1), pltpu.roll(values, 32, 1))


def both_halves(pair):
    low = lanes(pair.shape[0]) < HEAD_DIM
    other = pltpu.roll(pair, HEAD_DIM, 1)
    return jnp.where(low, pair, other), jnp.where(low, other, pair)


def head_lanes(values, head):
    return jnp.where(lanes(values.shape[0]) // HEAD_DIM == head, values, 0.0)


def doc_of(position, lengths):
    first = lengths[0, 0]
    return jnp.where(position >= first, 1, 0) + jnp.where(position >= first + lengths[0, 1], 1, 0)


def allowed(keys, first, lengths):
    key_at = lax.broadcasted_iota(jnp.int32, (keys, 1), 0)
    query_at = first + lax.broadcasted_iota(jnp.int32, (1, QUERIES), 1)
    return (key_at <= query_at) & (doc_of(key_at, lengths) == doc_of(query_at, lengths))


def inverse_root(values):
    return lax.rsqrt(jnp.mean(values * values, axis=-1, keepdims=True) + eps_norm)


def rms_back(grad_out, unit, inverse, gain):
    grad_unit = grad_out * gain
    return inverse * (grad_unit - unit * jnp.mean(grad_unit * unit, axis=-1, keepdims=True))


def key_tables(cosine, sine):
    key = lanes(cosine.shape[0]) < HEAD_DIM
    return jnp.where(key, cosine, 1.0), jnp.where(key, sine, 0.0)


QUERIES = 256


def attend(x_ref, w_ref, gain_ref, cos_ref, sin_ref, lengths, normed_ref, query_ref, pair_ref, lse_ref, mixed_ref, mixed_t, mixed_rows, between):
    @pl.loop(0, GROUP // 128)
    def _(i):
        rows = pl.ds(pl.multiple_of(i * 128, 128), 128)
        x = x_ref[rows, :].astype(F32)
        normed = (x * inverse_root(x) * gain_ref[0:1, :]).astype(BF16)
        normed_ref[rows, :] = normed
        raw = dot(normed, w_ref[0, :, 0:256])
        query, pair = raw[:, 0:128], raw[:, 128:256]
        cosine, sine = cos_ref[rows, :], sin_ref[rows, :]
        query_ref[rows, :] = (query * cosine + turn(query) * sine).astype(BF16)
        cosine, sine = key_tables(cosine, sine)
        pair_ref[rows, :] = (pair * cosine + turn(pair) * sine).astype(BF16)

    between()
    keys, values = both_halves(pair_ref[...].astype(F32))
    keys, values_t = keys.astype(BF16), values.T.astype(BF16)

    for first in range(0, GROUP, QUERIES):
        count = first + QUERIES
        mask = allowed(count, first, lengths)
        for head in range(2):
            query = head_lanes(query_ref[first : first + QUERIES, :].astype(F32), head).astype(BF16)
            scores = dot(keys[:count], query, ((1,), (1,))) * score_scale
            scores = jnp.where(mask, scores, -1e30)
            top = jnp.max(scores, axis=0, keepdims=True)
            raised = jnp.exp(scores - top)
            total = jnp.sum(raised, axis=0, keepdims=True)
            lse_ref[head : head + 1, first : first + QUERIES] = top + jnp.log(total)
            weights = (raised * (1.0 / total)).astype(BF16)
            mixed_t[HEAD_DIM * head : HEAD_DIM * (head + 1), first : first + QUERIES] = dot(
                values_t[HEAD_DIM * head : HEAD_DIM * (head + 1), :count], weights
            )
        between()
    mixed_ref[...] = mixed_t[...].astype(BF16)
    mixed_rows[...] = mixed_t[...].T.astype(BF16)


def attend_back(x_ref, w_ref, query_ref, pair_ref, lse_ref, cos_ref, sin_ref, lengths, grad_ref, gain_grad, dmixed_ref, dquery_t, dpair_ref, raw_ref, raw_t, between):
    keys, values = both_halves(pair_ref[...].astype(F32))
    keys_t = keys.T.astype(BF16)
    keys, values = keys.astype(BF16), values.astype(BF16)
    dpair_ref[...] = jnp.zeros_like(dpair_ref)

    for first in range(0, GROUP, QUERIES):
        count = first + QUERIES
        mask = allowed(count, first, lengths)
        for head in range(2):
            query = head_lanes(query_ref[first : first + QUERIES, :].astype(F32), head).astype(BF16)
            dmixed = head_lanes(dmixed_ref[first : first + QUERIES, :].astype(F32), head).astype(BF16)
            scores = dot(keys[:count], query, ((1,), (1,))) * score_scale
            scores = jnp.where(mask, scores, -1e30)
            weights = jnp.exp(scores - lse_ref[head : head + 1, first : first + QUERIES])
            dweights = dot(values[:count], dmixed, ((1,), (1,)))
            inner = jnp.sum(weights * dweights, axis=0, keepdims=True)
            dscores = (weights * (dweights - inner)).astype(BF16)
            dquery_t[HEAD_DIM * head : HEAD_DIM * (head + 1), first : first + QUERIES] = (
                dot(keys_t[HEAD_DIM * head : HEAD_DIM * (head + 1), :count], dscores) * score_scale
            )
            dpair_ref[0, :count, :] += dot(dscores, query) * score_scale
            dpair_ref[1, :count, :] += dot(weights.astype(BF16), dmixed)
        between()

    gain_grad[...] = jnp.zeros_like(gain_grad)

    @pl.loop(0, GROUP // 128)
    def _(i):
        at = pl.multiple_of(i * 128, 128)
        rows = pl.ds(at, 128)
        dquery = dquery_t[:, rows].T
        dkey, dvalue = dpair_ref[0, rows, :], dpair_ref[1, rows, :]
        dkey = dkey + pltpu.roll(dkey, HEAD_DIM, 1)
        dvalue = dvalue + pltpu.roll(dvalue, HEAD_DIM, 1)
        dpair = jnp.where(lanes(128) < HEAD_DIM, dkey, dvalue)
        cosine, sine = cos_ref[rows, :], sin_ref[rows, :]
        dquery = dquery * cosine + turn(dquery * sine)
        cosine, sine = key_tables(cosine, sine)
        dpair = dpair * cosine + turn(dpair * sine)
        raw_ref[rows, 0:128] = dquery.astype(BF16)
        raw_ref[rows, 128:256] = dpair.astype(BF16)
        raw_t[0:128, rows] = dquery.T.astype(BF16)
        raw_t[128:256, rows] = dpair.T.astype(BF16)
        dnormed = dot(raw_ref[rows, :], w_ref[0, :, 0:256], ((1,), (1,)))
        grad_ref[rows, :] = dnormed.astype(BF16)
        x = x_ref[rows, :].astype(F32)
        gain_grad[...] += jnp.sum(dnormed * (x * inverse_root(x)), axis=0, keepdims=True)


HEAD_TASKS = (
    GatherTp(ROWS, D),
    GatherFsdp(1, 512),
    GatherFsdp(LOCAL, HIDDEN),
    GatherFsdp(LOCAL, HIDDEN),
    GatherFsdp(LOCAL, HIDDEN),
    GatherTp(D, ROWS),
    ExchangeTp(),
    GatherTp(ROWS, D),
)


def head_body(
    lengths, x_ref, small_ref, gate_ref, up_ref, down_ref, routes_ref,
    x_out, w_out, gate_all, up_all, down_all, tokens,
    normed_out, query_out, pair_out, lse_ref, mixed_ref, middle_ref, own_ref, chosen_out, rank_out, rank_t_out, gains_ref, cos_out, sin_out, output_out,
    x_all, w_all, normed_ref, query_ref, pair_ref, chosen_ref, rank_ref, rank_t, cos_ref, sin_ref, store_sem,
    mixed_t, mixed_rows, mixed_own, output_all, *scratch,
):
    scratch = list(scratch)
    stores = []

    def store(src, dst):
        stores.append(pltpu.make_async_copy(src, dst, store_sem.at[len(stores)]))
        stores[-1].start()

    greet()
    pairs = (
        (x_ref, x_all), (small_ref, w_all), (gate_ref, gate_all), (up_ref, up_all), (down_ref, down_all),
        (w_all.at[0, :, 256:384], output_all),
        (functools.partial(part, mixed_rows), lambda tp: mixed_own.at[tp]), (own_ref, tokens),
    )
    x_run, w_run, gate_run, up_run, down_run, output_run, mixed_run, token_run = [
        run_task(task, scratch, *pair) for task, pair in zip(HEAD_TASKS, pairs)
    ]
    front = [x_run, w_run]
    pump(front)

    lane = lanes(GROUP)
    routes = routes_ref[...].astype(F32).T.astype(jnp.int32)
    chosen = lane == routes[:, 0:1]
    for k in range(1, 8):
        chosen = chosen | (lane == routes[:, k : k + 1])
    chosen = jnp.where(chosen, 1.0, 0.0)
    chosen_ref[...] = chosen
    pump(front)
    chosen = chosen.astype(BF16)
    for i in range(4):
        rows = slice(256 * i, 256 * (i + 1))
        later = 256 * i + lax.broadcasted_iota(jnp.int32, (256, GROUP), 0)
        until = jnp.where(later >= lax.broadcasted_iota(jnp.int32, (256, GROUP), 1), 1.0, 0.0)
        running = dot(until.astype(BF16), chosen)
        rank = jnp.where(chosen_ref[rows, :] > 0.0, running - 1.0, -1.0)
        rank_ref[rows, :] = rank
        rank_t[:, rows] = rank.T
    pump(front)
    position = lax.broadcasted_iota(jnp.int32, (GROUP, 1), 0)
    ends = (lengths[0, 0], lengths[0, 0] + lengths[0, 1])
    start = jnp.where(position >= ends[1], ends[1], jnp.where(position >= ends[0], ends[0], 0))
    half = lax.rem(lane[0:1], HEAD_DIM // 2).astype(F32)
    frequency = jnp.exp(half * (-2.0 / HEAD_DIM * math.log(rope_base)))
    angles = (position - start).astype(F32) * frequency
    cos_ref[...] = jnp.cos(angles)
    sine = jnp.sin(angles)
    sin_ref[...] = jnp.where(lax.rem(lane, HEAD_DIM) < HEAD_DIM // 2, -sine, sine)
    for pair in ((chosen_ref, chosen_out), (rank_ref, rank_out), (rank_t, rank_t_out), (cos_ref, cos_out), (sin_ref, sin_out)):
        store(*pair)
    drain(w_run)
    behind = [gate_run, up_run, down_run]
    pump(behind)
    store(w_all, w_out)
    gains_ref[...] = w_all[0, :, 384:512].astype(F32).T[32:40, :]
    drain(x_run)
    pump(behind)
    store(x_all, x_out)
    far = [output_run]
    pump(far)
    calls = [0]

    def between():
        calls[0] += 1
        if calls[0] in (3, 4, 5):
            pump(far)
        if calls[0] in (2, 5):
            pump(behind)

    attend(
        x_all, w_all, gains_ref, cos_ref, sin_ref, lengths,
        normed_ref, query_ref, pair_ref, lse_ref, mixed_ref, mixed_t, mixed_rows, between,
    )
    next(mixed_run)
    store(normed_ref, normed_out)
    store(query_ref, query_out)
    store(pair_ref, pair_out)
    drain(output_run)
    store(output_all, output_out)
    drain(mixed_run)
    middle = x_ref[...].astype(F32)
    for tp in range(8):
        middle = middle + dot(mixed_own[tp], output_all[tp * D : (tp + 1) * D, :], ((1,), (1,)))
    middle_ref[...] = middle
    own_ref[...] = (middle * inverse_root(middle) * gains_ref[1:2, :]).astype(BF16)
    next(token_run)
    pump(behind)
    drain(token_run, behind)
    while pump(behind):
        pass
    for copy in stores:
        copy.wait()


def head(lengths, x, small, gate, up, down, routes):
    def shape(*dims, dtype=BF16):
        return jax.ShapeDtypeStruct(dims, dtype)

    vmem = pl.BlockSpec(memory_space=pltpu.VMEM)
    far = pl.BlockSpec(memory_space=pl.ANY)
    weight = shape(LOCAL, D, HIDDEN)
    return pl.pallas_call(
        head_body,
        name="head",
        out_shape=[
            shape(GROUP, D),
            shape(1, D, 512),
            weight,
            weight,
            weight,
            shape(GROUP, D),
            shape(GROUP, D),
            shape(GROUP, 128),
            shape(GROUP, 128),
            shape(2, GROUP, dtype=F32),
            shape(128, GROUP),
            shape(ROWS, D, dtype=F32),
            shape(ROWS, D),
            shape(GROUP, 128, dtype=F32),
            shape(GROUP, 128, dtype=F32),
            shape(128, GROUP, dtype=F32),
            shape(8, D, dtype=F32),
            shape(GROUP, 128, dtype=F32),
            shape(GROUP, 128, dtype=F32),
            shape(8 * D, ROWS),
        ],
        in_specs=[pl.BlockSpec(memory_space=pltpu.SMEM)] + [vmem] * 6,
        out_specs=[far] * 5 + [vmem] + [far] * 3 + [vmem] * 4 + [far] * 3 + [vmem] + [far] * 3,
        scratch_shapes=[
            pltpu.VMEM((GROUP, D), BF16),
            pltpu.VMEM((1, D, 512), BF16),
            pltpu.VMEM((GROUP, D), BF16),
            pltpu.VMEM((GROUP, 128), BF16),
            pltpu.VMEM((GROUP, 128), BF16),
            pltpu.VMEM((GROUP, 128), F32),
            pltpu.VMEM((GROUP, 128), F32),
            pltpu.VMEM((128, GROUP), F32),
            pltpu.VMEM((GROUP, 128), F32),
            pltpu.VMEM((GROUP, 128), F32),
            dma(12),
            pltpu.VMEM((128, GROUP), F32),
            pltpu.VMEM((GROUP, 128), BF16),
            pltpu.VMEM((8, ROWS, 128), BF16),
            pltpu.VMEM((8 * D, ROWS), BF16),
        ]
        + [buffer for task in HEAD_TASKS for buffer in task.scratch],
        compiler_params=pltpu.CompilerParams(
            collective_id=1, has_side_effects=True, vmem_limit_bytes=56 * 2**20
        ),
    )(lengths, x, small, gate, up, down, routes)


TAIL_TASKS = (
    SumTp(ROWS, WIDE),
    SumChips(0),
    SumChips(1),
    SumChips(2),
    ExchangeTp(),
    GatherTp(ROWS, D),
    SumTp(ROWS, D),
    SumFsdp(384, BF16),
    SumAll(128),
)


def tail_body(
    lengths, grads_ref, moe_sum, pairs_ref,
    x_ref, dy_ref, middle_ref, own_ref, chosen_ref, gains_ref, lse_ref, mixed_ref,
    x_in, w_in, normed_in, query_in, pair_in, cos_in, sin_in, output_in,
    outputs_ref, input_grad, small_grad, attention_grad, gate_grad, up_grad, down_grad,
    x_all, w_all, normed_ref, query_ref, pair_ref, cos_ref, sin_ref, output_all, dmixed_own, load_sem,
    grads_sum, datt_own, datt_all, dmiddle_ref, dnormed_part, dnormed_sum, weights_part, small_part, gain_grads,
    gain_row, dmixed_ref, dquery_t, dpair_ref, raw_ref, raw_t, *scratch,
):
    scratch = list(scratch)
    greet()
    pairs = (
        (grads_ref, grads_sum), (pairs_ref, gate_grad), (pairs_ref, up_grad), (pairs_ref, down_grad),
        (lambda tp: dmixed_own.at[tp], functools.partial(part, dmixed_ref)),
        (datt_own, datt_all), (dnormed_part, dnormed_sum),
        (weights_part, attention_grad), (small_part, small_grad),
    )
    grads_run, gate_run, up_run, down_run, dmixed_run, datt_run, dnormed_run, weights_run, small_run = [
        run_task(task, scratch, *pair) for task, pair in zip(TAIL_TASKS, pairs)
    ]
    behind = [gate_run, up_run, down_run]
    next(grads_run)
    pump(behind)
    loads = []
    for k, (src, dst) in enumerate(
        (
            (w_in, w_all), (x_in, x_all), (normed_in, normed_ref), (query_in, query_ref),
            (pair_in, pair_ref), (cos_in, cos_ref), (sin_in, sin_ref), (output_in, output_all),
        )
    ):
        loads.append(pltpu.make_async_copy(src, dst, load_sem.at[k]))
        loads[k].start()
    drain(grads_run)

    for copy in loads:
        copy.wait()
    middle = middle_ref[...]
    inverse = inverse_root(middle)
    unit = middle * inverse
    router = w_all[0, :, 384:512]
    own_rows = pl.ds(pl.multiple_of(lax.axis_index("tp") * ROWS, ROWS), ROWS)
    logits = jnp.where(chosen_ref[own_rows, :] > 0.0, dot(own_ref[...], router), -1e30)
    raised = jnp.exp(logits - jnp.max(logits, axis=-1, keepdims=True))
    gates = raised / jnp.sum(raised, axis=-1, keepdims=True)
    dgates = grads_sum[:, D:WIDE]
    dlogits = gates * (dgates - jnp.sum(gates * dgates, axis=-1, keepdims=True))
    dlogits = dlogits.astype(BF16)
    dtokens = grads_sum[:, 0:D] + dot(dlogits, router, ((1,), (1,)))
    dmiddle = dy_ref[...].astype(F32) + rms_back(dtokens, unit, inverse, gains_ref[1:2, :])
    dmiddle_ref[...] = dmiddle
    datt_own[...] = dmiddle.astype(BF16)
    for tp in range(8):
        dmixed_own[tp] = dot(datt_own[...], output_all[tp * D : (tp + 1) * D, :]).astype(BF16)
    next(dmixed_run)
    next(datt_run)
    pump(behind)
    pump(behind)
    small_part[...] = dot(own_ref[...], dlogits, ((0,), (0,))).reshape(small_part.shape)
    gain_grads[...] = jnp.zeros_like(gain_grads)
    gain_grads[EXPERTS : EXPERTS + 1, :] = jnp.sum(dtokens * unit, axis=0, keepdims=True)
    drain(dmixed_run)
    far = [datt_run]
    pump(far)
    calls = [0]

    def between():
        calls[0] += 1
        if calls[0] in (3, 4):
            pump(far)
        if calls[0] == 4:
            pump(behind)

    attend_back(
        x_all, w_all, query_ref, pair_ref, lse_ref, cos_ref, sin_ref, lengths,
        dnormed_part, gain_row, dmixed_ref, dquery_t, dpair_ref, raw_ref, raw_t, between,
    )
    next(dnormed_run)
    gain_grads[EXPERTS + 1 : EXPERTS + 2, :] = gain_row[...]
    small_part[...] += gain_grads[...].T.reshape(small_part.shape)
    next(small_run)
    drain(datt_run)

    @pl.loop(0, 4)
    def _(i):
        at = pl.ds(pl.multiple_of(i * 256, 256), 256)
        chips = pl.ds(i * 2, 2)
        into_qkv = dot(raw_t[...], normed_ref[:, at]).T.astype(BF16)
        weights_part[chips, :, :, 0:256] = into_qkv.reshape(2, 2, BLOCK, 256)
        into_output = dot(mixed_ref[...], datt_all[:, at]).T.astype(BF16)
        weights_part[chips, :, :, 256:384] = into_output.reshape(2, 2, BLOCK, 128)

    last = [dnormed_run, weights_run, small_run] + behind
    while pump(last):
        pass
    outputs_ref[...] = (middle_ref[...] + moe_sum[...]).astype(BF16)
    x = x_ref[...].astype(F32)
    inverse = inverse_root(x)
    input_grad[...] = dmiddle_ref[...] + rms_back(dnormed_sum[...], x * inverse, inverse, gains_ref[0:1, :])


def tail(*arrays):
    def shape(*dims, dtype=F32):
        return jax.ShapeDtypeStruct(dims, dtype)

    vmem = pl.BlockSpec(memory_space=pltpu.VMEM)
    far = pl.BlockSpec(memory_space=pl.ANY)
    weight = shape(LOCAL, BLOCK, HIDDEN)
    return pl.pallas_call(
        tail_body,
        name="tail",
        out_shape=[
            shape(ROWS, D, dtype=BF16),
            shape(ROWS, D),
            shape(8, 128),
            shape(BLOCK, 384),
            weight,
            weight,
            weight,
        ],
        in_specs=[pl.BlockSpec(memory_space=pltpu.SMEM)] + [vmem] * 2 + [far] + [vmem] * 8 + [far] * 8,
        out_specs=[vmem] * 7,
        scratch_shapes=[
            pltpu.VMEM((GROUP, D), BF16),
            pltpu.VMEM((1, D, 512), BF16),
            pltpu.VMEM((GROUP, D), BF16),
            pltpu.VMEM((GROUP, 128), BF16),
            pltpu.VMEM((GROUP, 128), BF16),
            pltpu.VMEM((GROUP, 128), F32),
            pltpu.VMEM((GROUP, 128), F32),
            pltpu.VMEM((8 * D, ROWS), BF16),
            pltpu.VMEM((8, ROWS, 128), BF16),
            dma(9),
            pltpu.VMEM((ROWS, WIDE), F32),
            pltpu.VMEM((ROWS, D), BF16),
            pltpu.VMEM((GROUP, D), BF16),
            pltpu.VMEM((ROWS, D), F32),
            pltpu.VMEM((GROUP, D), BF16),
            pltpu.VMEM((ROWS, D), F32),
            pltpu.VMEM((8, 2, BLOCK, 384), BF16),
            pltpu.VMEM((8, 2, BLOCK, 128), F32),
            pltpu.VMEM((128, D), F32),
            pltpu.VMEM((1, D), F32),
            pltpu.VMEM((GROUP, 128), BF16),
            pltpu.VMEM((128, GROUP), F32),
            pltpu.VMEM((2, GROUP, 128), F32),
            pltpu.VMEM((GROUP, 256), BF16),
            pltpu.VMEM((256, GROUP), BF16),
        ]
        + [buffer for task in TAIL_TASKS for buffer in task.scratch],
        compiler_params=pltpu.CompilerParams(
            collective_id=2, has_side_effects=True, vmem_limit_bytes=62 * 2**20
        ),
    )(*arrays)


class StepGather:
    scratch = [dma(7), dma(7), pltpu.SemaphoreType.DMA(())]

    def __init__(self, src, out, send_sem, recv_sem, own_sem):
        self.src, self.out, self.send_sem, self.recv_sem = src, out, send_sem, recv_sem
        self.own = pltpu.make_async_copy(src, part(out, lax.axis_index("tp")), own_sem)

    def copy(self, k):
        place, target, _ = GATHER[k]
        block = part(self.out, tp_at(*place))
        return pltpu.make_async_remote_copy(
            src_ref=self.src if place == (0, 0) else block,
            dst_ref=block,
            send_sem=self.send_sem.at[k],
            recv_sem=self.recv_sem.at[k],
            device_id={"tp": tp_at(*target)},
            device_id_type=MESH,
        )

    def stage(self, number):
        if number == 0:
            self.own.start()
            for k in (0, 1, 2):
                self.copy(k).start()
        elif number == 1:
            self.copy(0).wait_recv()
            self.copy(3).start()
            self.copy(4).start()
        elif number == 2:
            self.copy(1).wait_recv()
            self.copy(5).start()
        elif number == 3:
            self.copy(4).wait_recv()
            self.copy(6).start()
        else:
            for k in (2, 3, 5, 6):
                self.copy(k).wait_recv()
            for k in range(7):
                self.copy(k).wait_send()
            self.own.wait()


class StepSum:
    scratch = [dma(7), dma(7), pltpu.VMEM((7, ROWS, D), BF16)]

    def __init__(self, src, out, send_sem, recv_sem, landed):
        self.src, self.out, self.landed = src, out, landed
        self.send_sem, self.recv_sem = send_sem, recv_sem

    def copy(self, k):
        place, target, others = SUM[k]
        return pltpu.make_async_remote_copy(
            src_ref=self.landed.at[others[0]] if others else part(self.src, tp_at(*place)),
            dst_ref=self.landed.at[k],
            send_sem=self.send_sem.at[k],
            recv_sem=self.recv_sem.at[k],
            device_id={"tp": tp_at(*target)},
            device_id_type=MESH,
        )

    def total(self, place, others, dst):
        start = tp_at(*place) * ROWS

        @pl.loop(0, ROWS // 16)
        def _(i):
            at = pl.multiple_of(i * 16, 16)
            value = self.src[pl.ds(pl.multiple_of(start + at, 16), 16), :].astype(F32)
            for k in others:
                value = value + self.landed[k, pl.ds(at, 16), :].astype(F32)
            dst[pl.ds(at, 16), :] = value.astype(dst.dtype)

    def relay(self, k):
        place, _, others = SUM[k]
        for other in others:
            self.copy(other).wait_recv()
        self.total(place, others, self.landed.at[others[0]])
        self.copy(k).start()

    def stage(self, number):
        if number == 0:
            for k in range(4):
                self.copy(k).start()
        elif number == 1:
            self.relay(4)
            self.relay(5)
        elif number == 2:
            self.relay(6)
        else:
            for k in LAST:
                self.copy(k).wait_recv()
            self.total((0, 0), LAST, self.out)
            for k in range(7):
                self.copy(k).wait_send()


def experts_body(
    tokens_ref, dy_ref, router_ref, chosen_ref, rank_ref, rank_t,
    gate_ref, up_ref, down_ref,
    moe_ref, grad_ref, pair_ref,
    give_all, slots_all, dgate_all, gates_ref, parts, got, send_sem, recv_sem,
    picked_all, gate_parts, up_parts, slot_gates, dy_all, combined_ref, *scratch,
):
    step = pl.program_id(0)
    lane = lax.broadcasted_iota(jnp.int32, (1, 128), 1)
    core = lax.rem(lax.axis_index("fsdp"), 2)
    dy_gather = StepGather(dy_ref, dy_all, *scratch[:3])
    moe_sum = StepSum(combined_ref, moe_ref, *scratch[3:])
    local = lax.rem(step, LOCAL)
    expert = lax.axis_index("tp") * LOCAL + local
    expert_lane = lane == expert
    rows = pl.ds(pl.multiple_of(local * PLACES, PLACES), SLOTS)

    def take():
        slot = lax.broadcasted_iota(jnp.int32, (SLOTS, GROUP), 0)
        return jnp.where(slot == rank_t[pl.ds(expert, 1), :].astype(jnp.int32), 1.0, 0.0).astype(BF16)

    def across(number):
        slot = lax.rem(number, 2)
        return pltpu.make_async_remote_copy(
            src_ref=parts.at[slot, :, :, 1 - core],
            dst_ref=got.at[number],
            send_sem=send_sem.at[slot],
            recv_sem=recv_sem.at[number],
            device_id={"fsdp": core_partner()},
            device_id_type=MESH,
        )

    @pl.when(step == 0)
    def _():
        barrier = pltpu.get_barrier_semaphore()
        for device in ({"tp": tp_at(1, 0)}, {"tp": tp_at(3, 0)}, {"tp": tp_at(0, 1)}, {"fsdp": core_partner()}):
            pl.semaphore_signal(barrier, inc=1, device_id=device, device_id_type=MESH)
        pl.semaphore_wait(barrier, 4)
        dy_gather.stage(0)
        slots_all[...] = jnp.zeros_like(slots_all)
        dgate_all[...] = jnp.zeros_like(dgate_all)
        logits = jnp.where(chosen_ref[...] > 0.0, dot(tokens_ref[...], router_ref[0]), -1e30)
        raised = jnp.exp(logits - jnp.max(logits, axis=-1, keepdims=True))
        gates = raised / jnp.sum(raised, axis=-1, keepdims=True)
        high = gates.astype(BF16)
        gates_ref[:, 0:128] = high
        gates_ref[:, 128:256] = (gates - high.astype(F32)).astype(BF16)

    for number, at in ((1, 1), (2, 2), (3, 3), (4, LOCAL)):
        pl.when(step == at)(functools.partial(dy_gather.stage, number))

    @pl.when(step < LOCAL)
    def _():
        taken = take()
        slot_gate = dot(taken, gates_ref[...])
        slot_gate = jnp.where(expert_lane, slot_gate[:, 0:128] + slot_gate[:, 128:256], 0.0)
        slot_gate = jnp.sum(slot_gate, axis=1, keepdims=True)
        slot_gates[local] = jnp.broadcast_to(slot_gate, (SLOTS, 128))
        picked = dot(taken, tokens_ref[...]).astype(BF16)
        picked_all[local] = picked
        gate_part = dot(picked, gate_ref[0])
        up_part = dot(picked, up_ref[0])
        gate_parts[local] = gate_part
        up_parts[local] = up_part
        hidden = gate_part * (1.0 / (1.0 + jnp.exp(-gate_part))) * up_part
        weighted = (hidden * slot_gate).astype(BF16)
        slots_all[rows, :] = dot(weighted, down_ref[0], ((1,), (1,))).astype(BF16)
        rank_column = jnp.sum(jnp.where(expert_lane, rank_ref[...], 0.0), axis=1, keepdims=True)
        place = lax.broadcasted_iota(jnp.int32, (GROUP, PLACES), 1)
        give = jnp.where(place == rank_column.astype(jnp.int32), 1.0, 0.0)
        give_all[:, pl.ds(pl.multiple_of(local * PLACES, PLACES), PLACES)] = give.astype(BF16)

    @pl.when(step == LOCAL - 1)
    def _():
        for i in range(4):
            columns = slice(256 * i, 256 * (i + 1))
            combined_ref[:, columns] = dot(give_all[...], slots_all[:, columns]).astype(BF16)
        moe_sum.stage(0)

    for number, at in ((1, LOCAL + 2), (2, LOCAL + 3)):
        pl.when(step == at)(functools.partial(moe_sum.stage, number))

    @pl.when((step >= LOCAL) & (step < 2 * LOCAL))
    def _():
        slot_gate = slot_gates[local][:, 0:1]
        gate_part, up_part = gate_parts[local], up_parts[local]
        sigmoid = 1.0 / (1.0 + jnp.exp(-gate_part))
        silu = gate_part * sigmoid
        hidden = silu * up_part
        dy = dot(take(), dy_all[...]).astype(BF16)
        dhidden = dot(dy, down_ref[0])
        dgate = jnp.sum(hidden * dhidden, axis=1, keepdims=True)
        weighted = (hidden * slot_gate).astype(BF16)
        dhidden = dhidden * slot_gate
        dgate_part = (dhidden * up_part * (sigmoid * (1.0 + gate_part * (1.0 - sigmoid)))).astype(BF16)
        dup_part = (dhidden * silu).astype(BF16)

        @pl.when(local >= 2)
        def _():
            across(local - 2).wait_send()

        slot_now = lax.rem(local, 2)
        picked_t, dy_t = picked_all[local].T, dy.T
        for k, (left, right) in enumerate(
            ((picked_t, dgate_part), (picked_t, dup_part), (dy_t, weighted))
        ):
            parts[slot_now, k] = dot(left, right).astype(BF16).reshape(8, 2, BLOCK, HIDDEN)
        across(local).start()
        dpicked = dot(dgate_part, gate_ref[0], ((1,), (1,)))
        slots_all[rows, :] = (dpicked + dot(dup_part, up_ref[0], ((1,), (1,)))).astype(BF16)
        dgate_all[rows, :] = jnp.where(expert_lane, dgate, 0.0).astype(BF16)

    @pl.when(step == 2 * LOCAL)
    def _():
        for i in range(4):
            columns = slice(256 * i, 256 * (i + 1))
            grad_ref[:, columns] = dot(give_all[...], slots_all[:, columns]).astype(BF16)
        grad_ref[:, D:WIDE] = dot(give_all[...], dgate_all[...]).astype(BF16)
        moe_sum.stage(3)

    @pl.when(step >= LOCAL + 1)
    def _():
        before = step - LOCAL - 1
        across(before).wait_recv()
        slot_before = lax.rem(before, 2)

        @pl.loop(0, 24)
        def _(i):
            kind, chip = i // 8, lax.rem(i, 8)
            total = parts[slot_before, kind, chip, core].astype(F32) + got[before, kind, chip].astype(F32)
            pair_ref[0, kind, chip] = total.astype(BF16)

    @pl.when(step == 2 * LOCAL)
    def _():
        for number in (LOCAL - 2, LOCAL - 1):
            across(number).wait_send()


def experts(tokens, dy, router, chosen, rank, rank_t, gate, up, down):
    def whole(*shape):
        return pl.BlockSpec(shape, lambda i: (0,) * len(shape))

    def own(*shape):
        return pl.BlockSpec(
            (1,) + shape,
            lambda i: (lax.rem(jnp.minimum(i, 2 * LOCAL - 1), LOCAL),) + (0,) * len(shape),
        )

    slots = LOCAL * PLACES
    return pl.pallas_call(
        experts_body,
        name="experts",
        grid=(2 * LOCAL + 1,),
        in_specs=[
            whole(GROUP, D),
            whole(ROWS, D),
            pl.BlockSpec((1, D, 128), lambda i: (0, 0, 3)),
            whole(GROUP, 128),
            whole(GROUP, 128),
            whole(128, GROUP),
            own(D, HIDDEN),
            own(D, HIDDEN),
            own(D, HIDDEN),
        ],
        out_specs=[
            whole(ROWS, D),
            whole(GROUP, WIDE),
            pl.BlockSpec(
                (1, 3, 8, BLOCK, HIDDEN), lambda i: (jnp.maximum(i - LOCAL - 1, 0), 0, 0, 0, 0)
            ),
        ],
        scratch_shapes=[
            pltpu.VMEM((GROUP, slots), BF16),
            pltpu.VMEM((slots, D), BF16),
            pltpu.VMEM((slots, 128), BF16),
            pltpu.VMEM((GROUP, 256), BF16),
            pltpu.VMEM((2, 3, 8, 2, BLOCK, HIDDEN), BF16),
            pltpu.VMEM((LOCAL, 3, 8, BLOCK, HIDDEN), BF16),
            dma(2),
            dma(LOCAL),
            pltpu.VMEM((LOCAL, SLOTS, D), BF16),
            pltpu.VMEM((LOCAL, SLOTS, HIDDEN), F32),
            pltpu.VMEM((LOCAL, SLOTS, HIDDEN), F32),
            pltpu.VMEM((LOCAL, SLOTS, 128), F32),
            pltpu.VMEM((GROUP, D), BF16),
            pltpu.VMEM((GROUP, D), BF16),
        ]
        + StepGather.scratch
        + StepSum.scratch,
        out_shape=[
            jax.ShapeDtypeStruct((ROWS, D), F32),
            jax.ShapeDtypeStruct((GROUP, WIDE), BF16),
            jax.ShapeDtypeStruct((LOCAL, 3, 8, BLOCK, HIDDEN), BF16),
        ],
        compiler_params=pltpu.CompilerParams(
            collective_id=3, has_side_effects=True, vmem_limit_bytes=62 * 2**20
        ),
    )(tokens, dy, router, chosen, rank, rank_t, gate, up, down)


def finish_body(*refs):
    sources, outs = refs[:7], refs[7:19]
    small, attention, sems = refs[19:]
    copies = []
    for k, (source, target) in enumerate(
        zip(sources, (outs[0], outs[1], small, attention, outs[9], outs[10], outs[11]))
    ):
        copies.append(pltpu.make_async_copy(source, target, sems.at[k]))
        copies[k].start()
    for copy in copies:
        copy.wait()
    outs[2][...] = attention[:, 0:128]
    outs[3][...] = attention[:, 128:192]
    outs[4][...] = attention[:, 192:256]
    outs[5][...] = attention[:, 256:384].T
    outs[6][...] = small[:, 0:EXPERTS]
    columns = small[...].T
    outs[7][...] = columns[EXPERTS + 1 : EXPERTS + 2, :]
    outs[8][...] = columns[EXPERTS : EXPERTS + 1, :]


def finish(*arrays):
    def shape(*dims, dtype=F32):
        return jax.ShapeDtypeStruct(dims, dtype)

    vmem = pl.BlockSpec(memory_space=pltpu.VMEM)
    far = pl.BlockSpec(memory_space=pl.ANY)
    return pl.pallas_call(
        finish_body,
        name="finish",
        out_shape=[
            shape(ROWS, D, dtype=BF16),
            shape(ROWS, D),
            shape(BLOCK, 128),
            shape(BLOCK, BLOCK),
            shape(BLOCK, BLOCK),
            shape(128, BLOCK),
            shape(8, EXPERTS),
            shape(1, 8),
            shape(1, 8),
        ]
        + [shape(LOCAL, BLOCK, HIDDEN)] * 3,
        in_specs=[far] * 7,
        out_specs=[vmem] * 12,
        scratch_shapes=[pltpu.VMEM((8, 128), F32), pltpu.VMEM((BLOCK, 384), F32), dma(7)],
        compiler_params=pltpu.CompilerParams(vmem_limit_bytes=60 * 2**20),
    )(*arrays)


def per_device(
    inputs,
    lengths,
    routes,
    attn_gain,
    query_weight,
    key_weight,
    value_weight,
    output_weight,
    moe_gain,
    router_weight,
    gate_weight,
    up_weight,
    down_weight,
    cotangent,
):
    small = jnp.concatenate(
        [
            query_weight,
            key_weight,
            value_weight,
            output_weight.T,
            router_weight,
            attn_gain[:, None],
            moe_gain[:, None],
            jnp.zeros((BLOCK, 128 - EXPERTS - 2), BF16),
        ],
        axis=1,
    )
    (
        x_all, w_all, gate_all, up_all, down_all, tokens,
        normed, query, pair, lse, mixed, middle, own, chosen, rank, rank_t, gains, cosine, sine, output_all,
    ) = head(
        lengths, inputs, small[None], gate_weight, up_weight, down_weight.transpose(0, 2, 1),
        routes.T,
    )
    moe, grads, pairs = experts(
        tokens, cotangent, w_all, chosen, rank, rank_t, gate_all, up_all, down_all
    )
    results = tail(
        lengths, grads, moe, pairs,
        inputs, cotangent, middle, own, chosen, gains, lse, mixed,
        x_all, w_all, normed, query, pair, cosine, sine, output_all,
    )
    (
        outputs, input_grad, query_grad, key_grad, value_grad, output_grad, router_grad, attn_gain_grad, moe_gain_grad,
        gate_grad, up_grad, down_grad,
    ) = finish(*results)
    return (
        outputs,
        input_grad,
        attn_gain_grad.reshape(8),
        query_grad,
        key_grad,
        value_grad,
        output_grad,
        moe_gain_grad.reshape(8),
        router_grad,
        gate_grad,
        up_grad,
        down_grad.transpose(0, 2, 1),
    )


def solution(mesh):
    return jax.shard_map(
        per_device,
        mesh=mesh,
        in_specs=(
            P(("fsdp", "tp"), None),
            P("fsdp", None),
            P("fsdp", None),
            P("fsdp"),
            P("fsdp", "tp"),
            P("fsdp", "tp"),
            P("fsdp", "tp"),
            P("tp", "fsdp"),
            P("fsdp"),
            P("fsdp", None),
            P("tp", "fsdp", None),
            P("tp", "fsdp", None),
            P("tp", None, "fsdp"),
            P(("fsdp", "tp"), None),
        ),
        out_specs=(
            P(("fsdp", "tp"), None),
            P(("fsdp", "tp"), None),
            P(("fsdp", "tp")),
            P("fsdp", "tp"),
            P("fsdp", "tp"),
            P("fsdp", "tp"),
            P("tp", "fsdp"),
            P(("fsdp", "tp")),
            P(("fsdp", "tp"), None),
            P("tp", "fsdp", None),
            P("tp", "fsdp", None),
            P("tp", None, "fsdp"),
        ),
        check_vma=False,
    )
```

```python
import functools
import math

import jax
import jax.numpy as jnp
from jax import lax
from jax.experimental import pallas as pl
from jax.experimental.pallas import tpu as pltpu
from jax.sharding import PartitionSpec as P

MESH = pl.DeviceIdType.MESH
D = 1024
HEAD_DIM = 64
EXPERTS = 32
HIDDEN = 512
GROUP = 1024
ROWS = 128
SLOTS = 352
PLACES = 384
LOCAL = 4
BLOCK = 64
WIDE = D + 128

eps_norm = 1e-06
rope_base = 10000.0
score_scale = 1.0 / HEAD_DIM
F32 = jnp.float32
BF16 = jnp.bfloat16


def tp_at(along, across):
    tp = lax.axis_index("tp")
    return lax.rem(tp // 2 + along, 4) * 2 + lax.rem(tp + across, 2)


def fsdp_at(along, across):
    fsdp = lax.axis_index("fsdp")
    chip = lax.rem(fsdp // 8 + across, 2) * 4 + lax.rem(fsdp // 2 + along, 4)
    return chip * 2 + lax.rem(fsdp, 2)


def core_partner():
    fsdp = lax.axis_index("fsdp")
    return fsdp // 2 * 2 + 1 - lax.rem(fsdp, 2)


def send(src, dst, send_sem, recv_sem, device):
    copy = pltpu.make_async_remote_copy(
        src_ref=src,
        dst_ref=dst,
        send_sem=send_sem,
        recv_sem=recv_sem,
        device_id=device,
        device_id_type=MESH,
    )
    copy.start()
    return copy


def greet():
    barrier = pltpu.get_barrier_semaphore()
    for place in EVERY:
        for device in ({"tp": tp_at(*place)}, {"fsdp": fsdp_at(*place)}):
            pl.semaphore_signal(barrier, inc=1, device_id=device, device_id_type=MESH)
    pl.semaphore_signal(barrier, inc=1, device_id={"fsdp": core_partner()}, device_id_type=MESH)
    pl.semaphore_wait(barrier, 15)


def dma(count):
    return pltpu.SemaphoreType.DMA((count,))


EVERY = ((2, 0), (2, 1), (1, 1), (3, 1), (1, 0), (3, 0), (0, 1))
GATHER = (
    ((0, 0), (0, 1), None),
    ((0, 0), (1, 0), None),
    ((0, 0), (3, 0), None),
    ((0, 1), (1, 0), 0),
    ((0, 1), (3, 0), 0),
    ((3, 0), (1, 0), 1),
    ((1, 1), (3, 0), 4),
)
ARRIVES = ((0, 1), (3, 0), (1, 0), (3, 1), (1, 1), (2, 0), (2, 1))
SUM = (
    ((2, 0), (1, 0), ()),
    ((2, 1), (3, 0), ()),
    ((1, 1), (1, 0), ()),
    ((3, 0), (3, 0), ()),
    ((1, 0), (1, 0), (0,)),
    ((3, 1), (3, 0), (1,)),
    ((0, 1), (0, 1), (2, 5)),
)
LAST = (3, 4, 6)


class GatherTp:
    def __init__(self, rows, columns):
        self.rows = rows
        self.scratch = [dma(7), dma(7), pltpu.SemaphoreType.DMA(())]

    def run(self, src, out, send_sem, recv_sem, own_sem):
        def block(place):
            return out.at[pl.ds(pl.multiple_of(tp_at(*place) * self.rows, self.rows), self.rows)]

        own = pltpu.make_async_copy(src, block((0, 0)), own_sem)
        own.start()
        copies, arrived = [], set()
        for k, (place, target, after) in enumerate(GATHER):
            if after is not None and after not in arrived:
                yield
                copies[after].wait_recv()
                arrived.add(after)
            copies.append(
                send(
                    src if place == (0, 0) else block(place),
                    block(place),
                    send_sem.at[k],
                    recv_sem.at[k],
                    {"tp": tp_at(*target)},
                )
            )
        yield
        for k, copy in enumerate(copies):
            if k not in arrived:
                copy.wait_recv()
            copy.wait_send()
        own.wait()


class SumTp:
    def __init__(self, rows, columns):
        self.rows = rows
        self.scratch = [dma(7), dma(7), pltpu.VMEM((7, rows, columns), BF16)]

    def run(self, src, out, send_sem, recv_sem, landed):
        def first(place):
            return pl.multiple_of(tp_at(*place) * self.rows, self.rows)

        def total(place, others, dst):
            start = first(place)

            @pl.loop(0, self.rows // 16)
            def _(i):
                at = pl.multiple_of(i * 16, 16)
                value = src[pl.ds(pl.multiple_of(start + at, 16), 16), :].astype(F32)
                for k in others:
                    value = value + landed[k, pl.ds(at, 16), :].astype(F32)
                dst[pl.ds(at, 16), :] = value.astype(dst.dtype)

        copies, arrived = [], set()
        for k, (place, target, others) in enumerate(SUM):
            if others:
                yield
                for other in others:
                    copies[other].wait_recv()
                    arrived.add(other)
                part = landed.at[others[0]]
                total(place, others, part)
            else:
                part = src.at[pl.ds(first(place), self.rows)]
            copies.append(
                send(part, landed.at[k], send_sem.at[k], recv_sem.at[k], {"tp": tp_at(*target)})
            )
        yield
        for k in LAST:
            copies[k].wait_recv()
        total((0, 0), LAST, out)
        for copy in copies:
            copy.wait_send()


class ExchangeTp:
    def __init__(self):
        self.scratch = [dma(7), dma(7), pltpu.SemaphoreType.DMA(())]

    def run(self, block, place, send_sem, recv_sem, own_sem):
        here = lax.axis_index("tp")
        copies = [
            send(block(peer), place(here), send_sem.at[k], recv_sem.at[k], {"tp": peer})
            for k, peer in enumerate(tp_at(*step) for step in EVERY)
        ]
        own = pltpu.make_async_copy(block(here), place(here), own_sem)
        own.start()
        yield
        for copy in copies:
            copy.wait()
        own.wait()


class GatherFsdp:
    def __init__(self, experts, columns):
        self.scratch = [dma(7), dma(7), dma(8), dma(8), pltpu.SemaphoreType.DMA(())]

    def run(self, src, out, send_sem, recv_sem, core_send, core_recv, own_sem):
        def block(place):
            return out.at[:, pl.ds(pl.multiple_of(fsdp_at(*place) * BLOCK, BLOCK), BLOCK)]

        own = pltpu.make_async_copy(src, block((0, 0)), own_sem)
        own.start()
        copies, arrived, crossed = [], set(), []

        def arrive(k):
            copies[k].wait_recv()
            arrived.add(k)
            here = block(ARRIVES[k])
            crossed.append(
                send(here, here, core_send.at[k], core_recv.at[k], {"fsdp": core_partner()})
            )

        for k, (place, target, after) in enumerate(GATHER):
            if after is not None and after not in arrived:
                yield
                arrive(after)
            copies.append(
                send(
                    src if place == (0, 0) else block(place),
                    block(place),
                    send_sem.at[k],
                    recv_sem.at[k],
                    {"fsdp": fsdp_at(*target)},
                )
            )
        crossed.append(
            send(src, block((0, 0)), core_send.at[7], core_recv.at[7], {"fsdp": core_partner()})
        )
        for k in range(7):
            if k not in arrived:
                yield
                arrive(k)
        yield
        for copy in copies:
            copy.wait_send()
        for copy in crossed:
            copy.wait()
        own.wait()


class SumFsdp:
    def __init__(self, columns, dtype):
        blocks = pltpu.VMEM((8, BLOCK, columns), dtype)
        self.scratch = [dma(7), dma(7), dma(2), blocks, blocks]

    def run(self, src, out, send_sem, recv_sem, core_sem, pair, landed):
        core = lax.rem(lax.axis_index("fsdp"), 2)
        across = send(
            src.at[:, 1 - core], pair, core_sem.at[0], core_sem.at[1], {"fsdp": core_partner()}
        )
        yield
        across.wait_recv()

        @pl.loop(0, 8)
        def _(chip):
            pair[chip] = (src[chip, core].astype(F32) + pair[chip].astype(F32)).astype(pair.dtype)

        copies = []
        for k, place in enumerate(EVERY):
            device = fsdp_at(*place)
            copies.append(
                send(pair.at[device // 2], landed.at[k], send_sem.at[k], recv_sem.at[k], {"fsdp": device})
            )
        yield
        value = pair[lax.axis_index("fsdp") // 2].astype(F32)
        for k, copy in enumerate(copies):
            copy.wait_recv()
            value = value + landed[k].astype(F32)
        out[...] = value
        across.wait_send()
        for copy in copies:
            copy.wait_send()


class SumChips:
    def __init__(self, kind):
        self.kind = kind
        self.scratch = [
            dma(7),
            dma(7),
            dma(4),
            pltpu.VMEM((4, LOCAL, BLOCK, HIDDEN), BF16),
            pltpu.VMEM((7, LOCAL, BLOCK, HIDDEN), BF16),
        ]

    def run(self, src, out, send_sem, recv_sem, own_sem, own, landed):
        def block(place):
            return src.at[:, self.kind, fsdp_at(*place) // 2]

        def total(k, others, dst):
            @pl.loop(0, LOCAL * (BLOCK // 16))
            def _(i):
                expert, at = i // (BLOCK // 16), pl.multiple_of(lax.rem(i, BLOCK // 16) * 16, 16)
                value = own[k, expert, pl.ds(at, 16), :].astype(F32)
                for other in others:
                    value = value + landed[other, expert, pl.ds(at, 16), :].astype(F32)
                dst[expert, pl.ds(at, 16), :] = value.astype(dst.dtype)

        copies, arrived, kept = [], set(), []
        for k, (place, target, others) in enumerate(SUM):
            if others:
                yield
                for other in others:
                    copies[other].wait_recv()
                kept[k - 4].wait()
                part = landed.at[others[0]]
                total(k - 4, others, part)
            else:
                part = block(place)
            copies.append(
                send(part, landed.at[k], send_sem.at[k], recv_sem.at[k], {"fsdp": fsdp_at(*target)})
            )
            if k == 3:
                for place in [place for place, _, _ in SUM[4:]] + [(0, 0)]:
                    j = len(kept)
                    kept.append(pltpu.make_async_copy(block(place), own.at[j], own_sem.at[j]))
                    kept[j].start()
        yield
        for k in LAST:
            copies[k].wait_recv()
        kept[3].wait()
        total(3, LAST, out)
        for copy in copies:
            copy.wait_send()


class SumAll:
    def __init__(self, columns):
        self.over_fsdp = SumFsdp(columns, F32)
        self.scratch = self.over_fsdp.scratch + [
            pltpu.VMEM((BLOCK, columns), F32),
            dma(7),
            dma(7),
            pltpu.VMEM((7, 8, columns), F32),
        ]

    def run(self, src, out, *scratch):
        total, send_sem, recv_sem, landed = scratch[-4:]
        yield from self.over_fsdp.run(src, total, *scratch[:-4])

        def rows(tp):
            return pl.ds(pl.multiple_of(tp * 8, 8), 8)

        copies = []
        for k, place in enumerate(EVERY):
            peer = tp_at(*place)
            copies.append(
                send(total.at[rows(peer)], landed.at[k], send_sem.at[k], recv_sem.at[k], {"tp": peer})
            )
        yield
        value = total[rows(lax.axis_index("tp")), :]
        for k, copy in enumerate(copies):
            copy.wait()
            value = value + landed[k]
        out[...] = value


def pump(runs):
    for run in list(runs):
        if next(run, "done") == "done":
            runs.remove(run)
    return bool(runs)


def drain(run, behind=(), steps=1):
    for _ in run:
        for _ in range(steps):
            pump(behind)


def part(ref, index):
    return ref.at[pl.ds(pl.multiple_of(index * ROWS, ROWS), ROWS)]


def run_task(task, scratch, src, out):
    count = len(task.scratch)
    mine, scratch[:] = scratch[:count], scratch[count:]
    return task.run(src, out, *mine)


def dot(a, b, dims=((1,), (0,))):
    return lax.dot_general(a, b, (dims, ((), ())), preferred_element_type=F32)


def lanes(rows):
    return lax.broadcasted_iota(jnp.int32, (rows, 128), 1)


def turn(values):
    low_half = lax.rem(lanes(values.shape[0]), HEAD_DIM) < HEAD_DIM // 2
    return jnp.where(low_half, pltpu.roll(values, 96, 1), pltpu.roll(values, 32, 1))


def both_halves(pair):
    low = lanes(pair.shape[0]) < HEAD_DIM
    other = pltpu.roll(pair, HEAD_DIM, 1)
    return jnp.where(low, pair, other), jnp.where(low, other, pair)


def head_lanes(values, head):
    return jnp.where(lanes(values.shape[0]) // HEAD_DIM == head, values, 0.0)


def doc_of(position, lengths):
    first = lengths[0, 0]
    return jnp.where(position >= first, 1, 0) + jnp.where(position >= first + lengths[0, 1], 1, 0)


def allowed(keys, first, lengths):
    key_at = lax.broadcasted_iota(jnp.int32, (keys, 1), 0)
    query_at = first + lax.broadcasted_iota(jnp.int32, (1, QUERIES), 1)
    return (key_at <= query_at) & (doc_of(key_at, lengths) == doc_of(query_at, lengths))


def inverse_root(values):
    return lax.rsqrt(jnp.mean(values * values, axis=-1, keepdims=True) + eps_norm)


def rms_back(grad_out, unit, inverse, gain):
    grad_unit = grad_out * gain
    return inverse * (grad_unit - unit * jnp.mean(grad_unit * unit, axis=-1, keepdims=True))


def key_tables(cosine, sine):
    key = lanes(cosine.shape[0]) < HEAD_DIM
    return jnp.where(key, cosine, 1.0), jnp.where(key, sine, 0.0)


QUERIES = 256


def attend(x_ref, w_ref, gain_ref, cos_ref, sin_ref, lengths, normed_ref, query_ref, pair_ref, lse_ref, mixed_ref, mixed_t, mixed_rows, between):
    @pl.loop(0, GROUP // 128)
    def _(i):
        rows = pl.ds(pl.multiple_of(i * 128, 128), 128)
        x = x_ref[rows, :].astype(F32)
        normed = (x * inverse_root(x) * gain_ref[0:1, :]).astype(BF16)
        normed_ref[rows, :] = normed
        raw = dot(normed, w_ref[0, :, 0:256])
        query, pair = raw[:, 0:128], raw[:, 128:256]
        cosine, sine = cos_ref[rows, :], sin_ref[rows, :]
        query_ref[rows, :] = (query * cosine + turn(query) * sine).astype(BF16)
        cosine, sine = key_tables(cosine, sine)
        pair_ref[rows, :] = (pair * cosine + turn(pair) * sine).astype(BF16)

    between()
    keys, values = both_halves(pair_ref[...].astype(F32))
    keys, values_t = keys.astype(BF16), values.T.astype(BF16)

    for first in range(0, GROUP, QUERIES):
        count = first + QUERIES
        mask = allowed(count, first, lengths)
        for head in range(2):
            query = head_lanes(query_ref[first : first + QUERIES, :].astype(F32), head).astype(BF16)
            scores = dot(keys[:count], query, ((1,), (1,))) * score_scale
            scores = jnp.where(mask, scores, -1e30)
            top = jnp.max(scores, axis=0, keepdims=True)
            raised = jnp.exp(scores - top)
            total = jnp.sum(raised, axis=0, keepdims=True)
            lse_ref[head : head + 1, first : first + QUERIES] = top + jnp.log(total)
            weights = (raised * (1.0 / total)).astype(BF16)
            mixed_t[HEAD_DIM * head : HEAD_DIM * (head + 1), first : first + QUERIES] = dot(
                values_t[HEAD_DIM * head : HEAD_DIM * (head + 1), :count], weights
            )
        between()
    mixed_ref[...] = mixed_t[...].astype(BF16)
    mixed_rows[...] = mixed_t[...].T.astype(BF16)


def attend_back(x_ref, w_ref, query_ref, pair_ref, lse_ref, cos_ref, sin_ref, lengths, grad_ref, gain_grad, dmixed_ref, dquery_t, dpair_ref, raw_ref, raw_t, between):
    keys, values = both_halves(pair_ref[...].astype(F32))
    keys_t = keys.T.astype(BF16)
    keys, values = keys.astype(BF16), values.astype(BF16)
    dpair_ref[...] = jnp.zeros_like(dpair_ref)

    for first in range(0, GROUP, QUERIES):
        count = first + QUERIES
        mask = allowed(count, first, lengths)
        for head in range(2):
            query = head_lanes(query_ref[first : first + QUERIES, :].astype(F32), head).astype(BF16)
            dmixed = head_lanes(dmixed_ref[first : first + QUERIES, :].astype(F32), head).astype(BF16)
            scores = dot(keys[:count], query, ((1,), (1,))) * score_scale
            scores = jnp.where(mask, scores, -1e30)
            weights = jnp.exp(scores - lse_ref[head : head + 1, first : first + QUERIES])
            dweights = dot(values[:count], dmixed, ((1,), (1,)))
            inner = jnp.sum(weights * dweights, axis=0, keepdims=True)
            dscores = (weights * (dweights - inner)).astype(BF16)
            dquery_t[HEAD_DIM * head : HEAD_DIM * (head + 1), first : first + QUERIES] = (
                dot(keys_t[HEAD_DIM * head : HEAD_DIM * (head + 1), :count], dscores) * score_scale
            )
            dpair_ref[0, :count, :] += dot(dscores, query) * score_scale
            dpair_ref[1, :count, :] += dot(weights.astype(BF16), dmixed)
        between()

    gain_grad[...] = jnp.zeros_like(gain_grad)

    @pl.loop(0, GROUP // 128)
    def _(i):
        at = pl.multiple_of(i * 128, 128)
        rows = pl.ds(at, 128)
        dquery = dquery_t[:, rows].T
        dkey, dvalue = dpair_ref[0, rows, :], dpair_ref[1, rows, :]
        dkey = dkey + pltpu.roll(dkey, HEAD_DIM, 1)
        dvalue = dvalue + pltpu.roll(dvalue, HEAD_DIM, 1)
        dpair = jnp.where(lanes(128) < HEAD_DIM, dkey, dvalue)
        cosine, sine = cos_ref[rows, :], sin_ref[rows, :]
        dquery = dquery * cosine + turn(dquery * sine)
        cosine, sine = key_tables(cosine, sine)
        dpair = dpair * cosine + turn(dpair * sine)
        raw_ref[rows, 0:128] = dquery.astype(BF16)
        raw_ref[rows, 128:256] = dpair.astype(BF16)
        raw_t[0:128, rows] = dquery.T.astype(BF16)
        raw_t[128:256, rows] = dpair.T.astype(BF16)
        dnormed = dot(raw_ref[rows, :], w_ref[0, :, 0:256], ((1,), (1,)))
        grad_ref[rows, :] = dnormed.astype(BF16)
        x = x_ref[rows, :].astype(F32)
        gain_grad[...] += jnp.sum(dnormed * (x * inverse_root(x)), axis=0, keepdims=True)


HEAD_TASKS = (
    GatherTp(ROWS, D),
    GatherFsdp(1, 512),
    GatherFsdp(LOCAL, HIDDEN),
    GatherFsdp(LOCAL, HIDDEN),
    GatherFsdp(LOCAL, HIDDEN),
    GatherTp(D, ROWS),
    ExchangeTp(),
    GatherTp(ROWS, D),
)


def head_body(
    lengths, x_ref, small_ref, gate_ref, up_ref, down_ref, routes_ref,
    x_out, w_out, gate_all, up_all, down_all, tokens,
    normed_out, query_out, pair_out, lse_ref, mixed_ref, middle_ref, own_ref, chosen_out, rank_out, rank_t_out, gains_ref, cos_out, sin_out, output_out,
    x_all, w_all, normed_ref, query_ref, pair_ref, chosen_ref, rank_ref, rank_t, cos_ref, sin_ref, store_sem,
    mixed_t, mixed_rows, mixed_own, output_all, *scratch,
):
    scratch = list(scratch)
    stores = []

    def store(src, dst):
        stores.append(pltpu.make_async_copy(src, dst, store_sem.at[len(stores)]))
        stores[-1].start()

    greet()
    pairs = (
        (x_ref, x_all), (small_ref, w_all), (gate_ref, gate_all), (up_ref, up_all), (down_ref, down_all),
        (w_all.at[0, :, 256:384], output_all),
        (functools.partial(part, mixed_rows), lambda tp: mixed_own.at[tp]), (own_ref, tokens),
    )
    x_run, w_run, gate_run, up_run, down_run, output_run, mixed_run, token_run = [
        run_task(task, scratch, *pair) for task, pair in zip(HEAD_TASKS, pairs)
    ]
    front = [x_run, w_run]
    pump(front)

    lane = lanes(GROUP)
    routes = routes_ref[...].astype(F32).T.astype(jnp.int32)
    chosen = lane == routes[:, 0:1]
    for k in range(1, 8):
        chosen = chosen | (lane == routes[:, k : k + 1])
    chosen = jnp.where(chosen, 1.0, 0.0)
    chosen_ref[...] = chosen
    pump(front)
    chosen = chosen.astype(BF16)
    for i in range(4):
        rows = slice(256 * i, 256 * (i + 1))
        later = 256 * i + lax.broadcasted_iota(jnp.int32, (256, GROUP), 0)
        until = jnp.where(later >= lax.broadcasted_iota(jnp.int32, (256, GROUP), 1), 1.0, 0.0)
        running = dot(until.astype(BF16), chosen)
        rank = jnp.where(chosen_ref[rows, :] > 0.0, running - 1.0, -1.0)
        rank_ref[rows, :] = rank
        rank_t[:, rows] = rank.T
    pump(front)
    position = lax.broadcasted_iota(jnp.int32, (GROUP, 1), 0)
    ends = (lengths[0, 0], lengths[0, 0] + lengths[0, 1])
    start = jnp.where(position >= ends[1], ends[1], jnp.where(position >= ends[0], ends[0], 0))
    half = lax.rem(lane[0:1], HEAD_DIM // 2).astype(F32)
    frequency = jnp.exp(half * (-2.0 / HEAD_DIM * math.log(rope_base)))
    angles = (position - start).astype(F32) * frequency
    cos_ref[...] = jnp.cos(angles)
    sine = jnp.sin(angles)
    sin_ref[...] = jnp.where(lax.rem(lane, HEAD_DIM) < HEAD_DIM // 2, -sine, sine)
    for pair in ((chosen_ref, chosen_out), (rank_ref, rank_out), (rank_t, rank_t_out), (cos_ref, cos_out), (sin_ref, sin_out)):
        store(*pair)
    drain(w_run)
    pump([x_run])
    behind = [gate_run, up_run, down_run]
    pump(behind)
    store(w_all, w_out)
    gains_ref[...] = w_all[0, :, 384:512].astype(F32).T[32:40, :]
    drain(x_run)
    pump(behind)
    store(x_all, x_out)
    far = [output_run]
    pump(far)
    calls = [0]

    def between():
        calls[0] += 1
        if calls[0] in (3, 4, 5):
            pump(far)
        if calls[0] in (2, 5):
            pump(behind)

    attend(
        x_all, w_all, gains_ref, cos_ref, sin_ref, lengths,
        normed_ref, query_ref, pair_ref, lse_ref, mixed_ref, mixed_t, mixed_rows, between,
    )
    next(mixed_run)
    store(normed_ref, normed_out)
    store(query_ref, query_out)
    store(pair_ref, pair_out)
    drain(output_run)
    store(output_all, output_out)
    drain(mixed_run)
    middle = x_ref[...].astype(F32)
    for tp in range(8):
        middle = middle + dot(mixed_own[tp], output_all[tp * D : (tp + 1) * D, :], ((1,), (1,)))
    middle_ref[...] = middle
    own_ref[...] = (middle * inverse_root(middle) * gains_ref[1:2, :]).astype(BF16)
    next(token_run)
    pump(behind)
    drain(token_run, behind)
    while pump(behind):
        pass
    for copy in stores:
        copy.wait()


def head(lengths, x, small, gate, up, down, routes):
    def shape(*dims, dtype=BF16):
        return jax.ShapeDtypeStruct(dims, dtype)

    vmem = pl.BlockSpec(memory_space=pltpu.VMEM)
    far = pl.BlockSpec(memory_space=pl.ANY)
    weight = shape(LOCAL, D, HIDDEN)
    return pl.pallas_call(
        head_body,
        name="head",
        out_shape=[
            shape(GROUP, D),
            shape(1, D, 512),
            weight,
            weight,
            weight,
            shape(GROUP, D),
            shape(GROUP, D),
            shape(GROUP, 128),
            shape(GROUP, 128),
            shape(2, GROUP, dtype=F32),
            shape(128, GROUP),
            shape(ROWS, D, dtype=F32),
            shape(ROWS, D),
            shape(GROUP, 128, dtype=F32),
            shape(GROUP, 128, dtype=F32),
            shape(128, GROUP, dtype=F32),
            shape(8, D, dtype=F32),
            shape(GROUP, 128, dtype=F32),
            shape(GROUP, 128, dtype=F32),
            shape(8 * D, ROWS),
        ],
        in_specs=[pl.BlockSpec(memory_space=pltpu.SMEM)] + [vmem] * 6,
        out_specs=[far] * 5 + [vmem] + [far] * 3 + [vmem] * 4 + [far] * 3 + [vmem] + [far] * 3,
        scratch_shapes=[
            pltpu.VMEM((GROUP, D), BF16),
            pltpu.VMEM((1, D, 512), BF16),
            pltpu.VMEM((GROUP, D), BF16),
            pltpu.VMEM((GROUP, 128), BF16),
            pltpu.VMEM((GROUP, 128), BF16),
            pltpu.VMEM((GROUP, 128), F32),
            pltpu.VMEM((GROUP, 128), F32),
            pltpu.VMEM((128, GROUP), F32),
            pltpu.VMEM((GROUP, 128), F32),
            pltpu.VMEM((GROUP, 128), F32),
            dma(12),
            pltpu.VMEM((128, GROUP), F32),
            pltpu.VMEM((GROUP, 128), BF16),
            pltpu.VMEM((8, ROWS, 128), BF16),
            pltpu.VMEM((8 * D, ROWS), BF16),
        ]
        + [buffer for task in HEAD_TASKS for buffer in task.scratch],
        compiler_params=pltpu.CompilerParams(
            collective_id=1, has_side_effects=True, vmem_limit_bytes=56 * 2**20
        ),
    )(lengths, x, small, gate, up, down, routes)


TAIL_TASKS = (
    SumTp(ROWS, WIDE),
    SumChips(0),
    SumChips(1),
    SumChips(2),
    ExchangeTp(),
    GatherTp(ROWS, D),
    SumTp(ROWS, D),
    SumFsdp(384, BF16),
    SumAll(128),
)


def tail_body(
    lengths, grads_ref, moe_sum, pairs_ref,
    x_ref, dy_ref, middle_ref, own_ref, chosen_ref, gains_ref, lse_ref, mixed_ref,
    x_in, w_in, normed_in, query_in, pair_in, cos_in, sin_in, output_in,
    outputs_ref, input_grad, small_grad, attention_grad, gate_grad, up_grad, down_grad,
    x_all, w_all, normed_ref, query_ref, pair_ref, cos_ref, sin_ref, output_all, dmixed_own, load_sem,
    grads_sum, datt_own, datt_all, dmiddle_ref, dnormed_part, dnormed_sum, weights_part, small_part, gain_grads,
    gain_row, dmixed_ref, dquery_t, dpair_ref, raw_ref, raw_t, *scratch,
):
    scratch = list(scratch)
    greet()
    pairs = (
        (grads_ref, grads_sum), (pairs_ref, gate_grad), (pairs_ref, up_grad), (pairs_ref, down_grad),
        (lambda tp: dmixed_own.at[tp], functools.partial(part, dmixed_ref)),
        (datt_own, datt_all), (dnormed_part, dnormed_sum),
        (weights_part, attention_grad), (small_part, small_grad),
    )
    grads_run, gate_run, up_run, down_run, dmixed_run, datt_run, dnormed_run, weights_run, small_run = [
        run_task(task, scratch, *pair) for task, pair in zip(TAIL_TASKS, pairs)
    ]
    behind = [gate_run, up_run, down_run]
    next(grads_run)
    pump(behind)
    loads = []
    for k, (src, dst) in enumerate(
        (
            (w_in, w_all), (x_in, x_all), (normed_in, normed_ref), (query_in, query_ref),
            (pair_in, pair_ref), (cos_in, cos_ref), (sin_in, sin_ref), (output_in, output_all),
        )
    ):
        loads.append(pltpu.make_async_copy(src, dst, load_sem.at[k]))
        loads[k].start()
    drain(grads_run)

    for copy in loads:
        copy.wait()
    middle = middle_ref[...]
    inverse = inverse_root(middle)
    unit = middle * inverse
    router = w_all[0, :, 384:512]
    own_rows = pl.ds(pl.multiple_of(lax.axis_index("tp") * ROWS, ROWS), ROWS)
    logits = jnp.where(chosen_ref[own_rows, :] > 0.0, dot(own_ref[...], router), -1e30)
    raised = jnp.exp(logits - jnp.max(logits, axis=-1, keepdims=True))
    gates = raised / jnp.sum(raised, axis=-1, keepdims=True)
    dgates = grads_sum[:, D:WIDE]
    dlogits = gates * (dgates - jnp.sum(gates * dgates, axis=-1, keepdims=True))
    dlogits = dlogits.astype(BF16)
    dtokens = grads_sum[:, 0:D] + dot(dlogits, router, ((1,), (1,)))
    dmiddle = dy_ref[...].astype(F32) + rms_back(dtokens, unit, inverse, gains_ref[1:2, :])
    dmiddle_ref[...] = dmiddle
    datt_own[...] = dmiddle.astype(BF16)
    for tp in range(8):
        dmixed_own[tp] = dot(datt_own[...], output_all[tp * D : (tp + 1) * D, :]).astype(BF16)
    next(dmixed_run)
    next(datt_run)
    pump(behind)
    pump(behind)
    small_part[...] = dot(own_ref[...], dlogits, ((0,), (0,))).reshape(small_part.shape)
    gain_grads[...] = jnp.zeros_like(gain_grads)
    gain_grads[EXPERTS : EXPERTS + 1, :] = jnp.sum(dtokens * unit, axis=0, keepdims=True)
    drain(dmixed_run)
    far = [datt_run]
    pump(far)
    calls = [0]

    def between():
        calls[0] += 1
        if calls[0] in (3, 4):
            pump(far)
        if calls[0] == 4:
            pump(behind)

    attend_back(
        x_all, w_all, query_ref, pair_ref, lse_ref, cos_ref, sin_ref, lengths,
        dnormed_part, gain_row, dmixed_ref, dquery_t, dpair_ref, raw_ref, raw_t, between,
    )
    next(dnormed_run)
    gain_grads[EXPERTS + 1 : EXPERTS + 2, :] = gain_row[...]
    small_part[...] += gain_grads[...].T.reshape(small_part.shape)
    next(small_run)
    drain(datt_run)

    @pl.loop(0, 4)
    def _(i):
        at = pl.ds(pl.multiple_of(i * 256, 256), 256)
        chips = pl.ds(i * 2, 2)
        into_qkv = dot(raw_t[...], normed_ref[:, at]).T.astype(BF16)
        weights_part[chips, :, :, 0:256] = into_qkv.reshape(2, 2, BLOCK, 256)
        into_output = dot(mixed_ref[...], datt_all[:, at]).T.astype(BF16)
        weights_part[chips, :, :, 256:384] = into_output.reshape(2, 2, BLOCK, 128)

    last = [dnormed_run, weights_run, small_run] + behind
    while pump(last):
        pass
    outputs_ref[...] = (middle_ref[...] + moe_sum[...]).astype(BF16)
    x = x_ref[...].astype(F32)
    inverse = inverse_root(x)
    input_grad[...] = dmiddle_ref[...] + rms_back(dnormed_sum[...], x * inverse, inverse, gains_ref[0:1, :])


def tail(*arrays):
    def shape(*dims, dtype=F32):
        return jax.ShapeDtypeStruct(dims, dtype)

    vmem = pl.BlockSpec(memory_space=pltpu.VMEM)
    far = pl.BlockSpec(memory_space=pl.ANY)
    weight = shape(LOCAL, BLOCK, HIDDEN)
    return pl.pallas_call(
        tail_body,
        name="tail",
        out_shape=[
            shape(ROWS, D, dtype=BF16),
            shape(ROWS, D),
            shape(8, 128),
            shape(BLOCK, 384),
            weight,
            weight,
            weight,
        ],
        in_specs=[pl.BlockSpec(memory_space=pltpu.SMEM)] + [vmem] * 2 + [far] + [vmem] * 8 + [far] * 8,
        out_specs=[vmem] * 7,
        scratch_shapes=[
            pltpu.VMEM((GROUP, D), BF16),
            pltpu.VMEM((1, D, 512), BF16),
            pltpu.VMEM((GROUP, D), BF16),
            pltpu.VMEM((GROUP, 128), BF16),
            pltpu.VMEM((GROUP, 128), BF16),
            pltpu.VMEM((GROUP, 128), F32),
            pltpu.VMEM((GROUP, 128), F32),
            pltpu.VMEM((8 * D, ROWS), BF16),
            pltpu.VMEM((8, ROWS, 128), BF16),
            dma(9),
            pltpu.VMEM((ROWS, WIDE), F32),
            pltpu.VMEM((ROWS, D), BF16),
            pltpu.VMEM((GROUP, D), BF16),
            pltpu.VMEM((ROWS, D), F32),
            pltpu.VMEM((GROUP, D), BF16),
            pltpu.VMEM((ROWS, D), F32),
            pltpu.VMEM((8, 2, BLOCK, 384), BF16),
            pltpu.VMEM((8, 2, BLOCK, 128), F32),
            pltpu.VMEM((128, D), F32),
            pltpu.VMEM((1, D), F32),
            pltpu.VMEM((GROUP, 128), BF16),
            pltpu.VMEM((128, GROUP), F32),
            pltpu.VMEM((2, GROUP, 128), F32),
            pltpu.VMEM((GROUP, 256), BF16),
            pltpu.VMEM((256, GROUP), BF16),
        ]
        + [buffer for task in TAIL_TASKS for buffer in task.scratch],
        compiler_params=pltpu.CompilerParams(
            collective_id=2, has_side_effects=True, vmem_limit_bytes=62 * 2**20
        ),
    )(*arrays)


class StepGather:
    scratch = [dma(7), dma(7), pltpu.SemaphoreType.DMA(())]

    def __init__(self, src, out, send_sem, recv_sem, own_sem):
        self.src, self.out, self.send_sem, self.recv_sem = src, out, send_sem, recv_sem
        self.own = pltpu.make_async_copy(src, part(out, lax.axis_index("tp")), own_sem)

    def copy(self, k):
        place, target, _ = GATHER[k]
        block = part(self.out, tp_at(*place))
        return pltpu.make_async_remote_copy(
            src_ref=self.src if place == (0, 0) else block,
            dst_ref=block,
            send_sem=self.send_sem.at[k],
            recv_sem=self.recv_sem.at[k],
            device_id={"tp": tp_at(*target)},
            device_id_type=MESH,
        )

    def stage(self, number):
        if number == 0:
            self.own.start()
            for k in (0, 1, 2):
                self.copy(k).start()
        elif number == 1:
            self.copy(0).wait_recv()
            self.copy(3).start()
            self.copy(4).start()
        elif number == 2:
            self.copy(1).wait_recv()
            self.copy(5).start()
        elif number == 3:
            self.copy(4).wait_recv()
            self.copy(6).start()
        else:
            for k in (2, 3, 5, 6):
                self.copy(k).wait_recv()
            for k in range(7):
                self.copy(k).wait_send()
            self.own.wait()


class StepSum:
    scratch = [dma(7), dma(7), pltpu.VMEM((7, ROWS, D), BF16)]

    def __init__(self, src, out, send_sem, recv_sem, landed):
        self.src, self.out, self.landed = src, out, landed
        self.send_sem, self.recv_sem = send_sem, recv_sem

    def copy(self, k):
        place, target, others = SUM[k]
        return pltpu.make_async_remote_copy(
            src_ref=self.landed.at[others[0]] if others else part(self.src, tp_at(*place)),
            dst_ref=self.landed.at[k],
            send_sem=self.send_sem.at[k],
            recv_sem=self.recv_sem.at[k],
            device_id={"tp": tp_at(*target)},
            device_id_type=MESH,
        )

    def total(self, place, others, dst):
        start = tp_at(*place) * ROWS

        @pl.loop(0, ROWS // 16)
        def _(i):
            at = pl.multiple_of(i * 16, 16)
            value = self.src[pl.ds(pl.multiple_of(start + at, 16), 16), :].astype(F32)
            for k in others:
                value = value + self.landed[k, pl.ds(at, 16), :].astype(F32)
            dst[pl.ds(at, 16), :] = value.astype(dst.dtype)

    def relay(self, k):
        place, _, others = SUM[k]
        for other in others:
            self.copy(other).wait_recv()
        self.total(place, others, self.landed.at[others[0]])
        self.copy(k).start()

    def stage(self, number):
        if number == 0:
            for k in range(4):
                self.copy(k).start()
        elif number == 1:
            self.relay(4)
            self.relay(5)
        elif number == 2:
            self.relay(6)
        else:
            for k in LAST:
                self.copy(k).wait_recv()
            self.total((0, 0), LAST, self.out)
            for k in range(7):
                self.copy(k).wait_send()


def experts_body(
    tokens_ref, dy_ref, router_ref, chosen_ref, rank_ref, rank_t,
    gate_ref, up_ref, down_ref,
    moe_ref, grad_ref, pair_ref,
    give_all, slots_all, dgate_all, gates_ref, parts, got, send_sem, recv_sem,
    picked_all, gate_parts, up_parts, slot_gates, dy_all, combined_ref, *scratch,
):
    step = pl.program_id(0)
    lane = lax.broadcasted_iota(jnp.int32, (1, 128), 1)
    core = lax.rem(lax.axis_index("fsdp"), 2)
    dy_gather = StepGather(dy_ref, dy_all, *scratch[:3])
    moe_sum = StepSum(combined_ref, moe_ref, *scratch[3:])
    local = lax.rem(step, LOCAL)
    expert = lax.axis_index("tp") * LOCAL + local
    expert_lane = lane == expert
    rows = pl.ds(pl.multiple_of(local * PLACES, PLACES), SLOTS)

    def take():
        slot = lax.broadcasted_iota(jnp.int32, (SLOTS, GROUP), 0)
        return jnp.where(slot == rank_t[pl.ds(expert, 1), :].astype(jnp.int32), 1.0, 0.0).astype(BF16)

    def across(number):
        slot = lax.rem(number, 2)
        return pltpu.make_async_remote_copy(
            src_ref=parts.at[slot, :, :, 1 - core],
            dst_ref=got.at[number],
            send_sem=send_sem.at[slot],
            recv_sem=recv_sem.at[number],
            device_id={"fsdp": core_partner()},
            device_id_type=MESH,
        )

    @pl.when(step == 0)
    def _():
        barrier = pltpu.get_barrier_semaphore()
        for device in ({"tp": tp_at(1, 0)}, {"tp": tp_at(3, 0)}, {"tp": tp_at(0, 1)}, {"fsdp": core_partner()}):
            pl.semaphore_signal(barrier, inc=1, device_id=device, device_id_type=MESH)
        pl.semaphore_wait(barrier, 4)
        dy_gather.stage(0)
        for i in range(LOCAL):
            slots_all[i * PLACES + SLOTS : (i + 1) * PLACES, :] = jnp.zeros((PLACES - SLOTS, D), BF16)
        dgate_all[...] = jnp.zeros_like(dgate_all)
        logits = jnp.where(chosen_ref[...] > 0.0, dot(tokens_ref[...], router_ref[0]), -1e30)
        raised = jnp.exp(logits - jnp.max(logits, axis=-1, keepdims=True))
        gates = raised / jnp.sum(raised, axis=-1, keepdims=True)
        high = gates.astype(BF16)
        gates_ref[:, 0:128] = high
        gates_ref[:, 128:256] = (gates - high.astype(F32)).astype(BF16)

    for number, at in ((1, 1), (2, 2), (3, 3), (4, LOCAL)):
        pl.when(step == at)(functools.partial(dy_gather.stage, number))

    @pl.when(step < LOCAL)
    def _():
        taken = take()
        slot_gate = dot(taken, gates_ref[...])
        slot_gate = jnp.where(expert_lane, slot_gate[:, 0:128] + slot_gate[:, 128:256], 0.0)
        slot_gate = jnp.sum(slot_gate, axis=1, keepdims=True)
        slot_gates[local] = jnp.broadcast_to(slot_gate, (SLOTS, 128))
        picked = dot(taken, tokens_ref[...]).astype(BF16)
        picked_all[local] = picked
        gate_part = dot(picked, gate_ref[0])
        up_part = dot(picked, up_ref[0])
        gate_parts[local] = gate_part
        up_parts[local] = up_part
        hidden = gate_part * (1.0 / (1.0 + jnp.exp(-gate_part))) * up_part
        weighted = (hidden * slot_gate).astype(BF16)
        slots_all[rows, :] = dot(weighted, down_ref[0], ((1,), (1,))).astype(BF16)
        rank_column = jnp.sum(jnp.where(expert_lane, rank_ref[...], 0.0), axis=1, keepdims=True)
        place = lax.broadcasted_iota(jnp.int32, (GROUP, PLACES), 1)
        give = jnp.where(place == rank_column.astype(jnp.int32), 1.0, 0.0)
        give_all[:, pl.ds(pl.multiple_of(local * PLACES, PLACES), PLACES)] = give.astype(BF16)

    @pl.when(step == LOCAL - 1)
    def _():
        for i in range(4):
            columns = slice(256 * i, 256 * (i + 1))
            combined_ref[:, columns] = dot(give_all[...], slots_all[:, columns]).astype(BF16)
        moe_sum.stage(0)

    for number, at in ((1, LOCAL + 2), (2, LOCAL + 3)):
        pl.when(step == at)(functools.partial(moe_sum.stage, number))

    @pl.when((step >= LOCAL) & (step < 2 * LOCAL))
    def _():
        slot_gate = slot_gates[local][:, 0:1]
        gate_part, up_part = gate_parts[local], up_parts[local]
        sigmoid = 1.0 / (1.0 + jnp.exp(-gate_part))
        silu = gate_part * sigmoid
        hidden = silu * up_part
        dy = dot(take(), dy_all[...]).astype(BF16)
        dhidden = dot(dy, down_ref[0])
        dgate = jnp.sum(hidden * dhidden, axis=1, keepdims=True)
        weighted = (hidden * slot_gate).astype(BF16)
        dhidden = dhidden * slot_gate
        dgate_part = (dhidden * up_part * (sigmoid * (1.0 + gate_part * (1.0 - sigmoid)))).astype(BF16)
        dup_part = (dhidden * silu).astype(BF16)

        @pl.when(local >= 2)
        def _():
            across(local - 2).wait_send()

        slot_now = lax.rem(local, 2)
        picked_t, dy_t = picked_all[local].T, dy.T
        for k, (left, right) in enumerate(
            ((picked_t, dgate_part), (picked_t, dup_part), (dy_t, weighted))
        ):
            parts[slot_now, k] = dot(left, right).astype(BF16).reshape(8, 2, BLOCK, HIDDEN)
        across(local).start()
        dpicked = dot(dgate_part, gate_ref[0], ((1,), (1,)))
        slots_all[rows, :] = (dpicked + dot(dup_part, up_ref[0], ((1,), (1,)))).astype(BF16)
        dgate_all[rows, :] = jnp.where(expert_lane, dgate, 0.0).astype(BF16)

    @pl.when(step == 2 * LOCAL)
    def _():
        for i in range(4):
            columns = slice(256 * i, 256 * (i + 1))
            grad_ref[:, columns] = dot(give_all[...], slots_all[:, columns]).astype(BF16)
        grad_ref[:, D:WIDE] = dot(give_all[...], dgate_all[...]).astype(BF16)
        moe_sum.stage(3)

    @pl.when(step >= LOCAL + 1)
    def _():
        before = step - LOCAL - 1
        across(before).wait_recv()
        slot_before = lax.rem(before, 2)

        @pl.loop(0, 24)
        def _(i):
            kind, chip = i // 8, lax.rem(i, 8)
            total = parts[slot_before, kind, chip, core].astype(F32) + got[before, kind, chip].astype(F32)
            pair_ref[0, kind, chip] = total.astype(BF16)

    @pl.when(step == 2 * LOCAL)
    def _():
        for number in (LOCAL - 2, LOCAL - 1):
            across(number).wait_send()


def experts(tokens, dy, router, chosen, rank, rank_t, gate, up, down):
    def whole(*shape):
        return pl.BlockSpec(shape, lambda i: (0,) * len(shape))

    def own(*shape):
        return pl.BlockSpec(
            (1,) + shape,
            lambda i: (lax.rem(jnp.minimum(i, 2 * LOCAL - 1), LOCAL),) + (0,) * len(shape),
        )

    slots = LOCAL * PLACES
    return pl.pallas_call(
        experts_body,
        name="experts",
        grid=(2 * LOCAL + 1,),
        in_specs=[
            whole(GROUP, D),
            whole(ROWS, D),
            pl.BlockSpec((1, D, 128), lambda i: (0, 0, 3)),
            whole(GROUP, 128),
            whole(GROUP, 128),
            whole(128, GROUP),
            own(D, HIDDEN),
            own(D, HIDDEN),
            own(D, HIDDEN),
        ],
        out_specs=[
            whole(ROWS, D),
            whole(GROUP, WIDE),
            pl.BlockSpec(
                (1, 3, 8, BLOCK, HIDDEN), lambda i: (jnp.maximum(i - LOCAL - 1, 0), 0, 0, 0, 0)
            ),
        ],
        scratch_shapes=[
            pltpu.VMEM((GROUP, slots), BF16),
            pltpu.VMEM((slots, D), BF16),
            pltpu.VMEM((slots, 128), BF16),
            pltpu.VMEM((GROUP, 256), BF16),
            pltpu.VMEM((2, 3, 8, 2, BLOCK, HIDDEN), BF16),
            pltpu.VMEM((LOCAL, 3, 8, BLOCK, HIDDEN), BF16),
            dma(2),
            dma(LOCAL),
            pltpu.VMEM((LOCAL, SLOTS, D), BF16),
            pltpu.VMEM((LOCAL, SLOTS, HIDDEN), F32),
            pltpu.VMEM((LOCAL, SLOTS, HIDDEN), F32),
            pltpu.VMEM((LOCAL, SLOTS, 128), F32),
            pltpu.VMEM((GROUP, D), BF16),
            pltpu.VMEM((GROUP, D), BF16),
        ]
        + StepGather.scratch
        + StepSum.scratch,
        out_shape=[
            jax.ShapeDtypeStruct((ROWS, D), F32),
            jax.ShapeDtypeStruct((GROUP, WIDE), BF16),
            jax.ShapeDtypeStruct((LOCAL, 3, 8, BLOCK, HIDDEN), BF16),
        ],
        compiler_params=pltpu.CompilerParams(
            collective_id=3, has_side_effects=True, vmem_limit_bytes=62 * 2**20
        ),
    )(tokens, dy, router, chosen, rank, rank_t, gate, up, down)


def finish_body(*refs):
    sources, outs = refs[:7], refs[7:19]
    small, attention, sems = refs[19:]
    copies = []
    for k, (source, target) in enumerate(
        zip(sources, (outs[0], outs[1], small, attention, outs[9], outs[10], outs[11]))
    ):
        copies.append(pltpu.make_async_copy(source, target, sems.at[k]))
        copies[k].start()
    for copy in copies:
        copy.wait()
    outs[2][...] = attention[:, 0:128]
    outs[3][...] = attention[:, 128:192]
    outs[4][...] = attention[:, 192:256]
    outs[5][...] = attention[:, 256:384].T
    outs[6][...] = small[:, 0:EXPERTS]
    columns = small[...].T
    outs[7][...] = columns[EXPERTS + 1 : EXPERTS + 2, :]
    outs[8][...] = columns[EXPERTS : EXPERTS + 1, :]


def finish(*arrays):
    def shape(*dims, dtype=F32):
        return jax.ShapeDtypeStruct(dims, dtype)

    vmem = pl.BlockSpec(memory_space=pltpu.VMEM)
    far = pl.BlockSpec(memory_space=pl.ANY)
    return pl.pallas_call(
        finish_body,
        name="finish",
        out_shape=[
            shape(ROWS, D, dtype=BF16),
            shape(ROWS, D),
            shape(BLOCK, 128),
            shape(BLOCK, BLOCK),
            shape(BLOCK, BLOCK),
            shape(128, BLOCK),
            shape(8, EXPERTS),
            shape(1, 8),
            shape(1, 8),
        ]
        + [shape(LOCAL, BLOCK, HIDDEN)] * 3,
        in_specs=[far] * 7,
        out_specs=[vmem] * 12,
        scratch_shapes=[pltpu.VMEM((8, 128), F32), pltpu.VMEM((BLOCK, 384), F32), dma(7)],
        compiler_params=pltpu.CompilerParams(vmem_limit_bytes=60 * 2**20),
    )(*arrays)


def per_device(
    inputs,
    lengths,
    routes,
    attn_gain,
    query_weight,
    key_weight,
    value_weight,
    output_weight,
    moe_gain,
    router_weight,
    gate_weight,
    up_weight,
    down_weight,
    cotangent,
):
    small = jnp.concatenate(
        [
            query_weight,
            key_weight,
            value_weight,
            output_weight.T,
            router_weight,
            attn_gain[:, None],
            moe_gain[:, None],
            jnp.zeros((BLOCK, 128 - EXPERTS - 2), BF16),
        ],
        axis=1,
    )
    (
        x_all, w_all, gate_all, up_all, down_all, tokens,
        normed, query, pair, lse, mixed, middle, own, chosen, rank, rank_t, gains, cosine, sine, output_all,
    ) = head(
        lengths, inputs, small[None], gate_weight, up_weight, down_weight.transpose(0, 2, 1),
        routes.T,
    )
    moe, grads, pairs = experts(
        tokens, cotangent, w_all, chosen, rank, rank_t, gate_all, up_all, down_all
    )
    results = tail(
        lengths, grads, moe, pairs,
        inputs, cotangent, middle, own, chosen, gains, lse, mixed,
        x_all, w_all, normed, query, pair, cosine, sine, output_all,
    )
    (
        outputs, input_grad, query_grad, key_grad, value_grad, output_grad, router_grad, attn_gain_grad, moe_gain_grad,
        gate_grad, up_grad, down_grad,
    ) = finish(*results)
    return (
        outputs,
        input_grad,
        attn_gain_grad.reshape(8),
        query_grad,
        key_grad,
        value_grad,
        output_grad,
        moe_gain_grad.reshape(8),
        router_grad,
        gate_grad,
        up_grad,
        down_grad.transpose(0, 2, 1),
    )


def solution(mesh):
    return jax.shard_map(
        per_device,
        mesh=mesh,
        in_specs=(
            P(("fsdp", "tp"), None),
            P("fsdp", None),
            P("fsdp", None),
            P("fsdp"),
            P("fsdp", "tp"),
            P("fsdp", "tp"),
            P("fsdp", "tp"),
            P("tp", "fsdp"),
            P("fsdp"),
            P("fsdp", None),
            P("tp", "fsdp", None),
            P("tp", "fsdp", None),
            P("tp", None, "fsdp"),
            P(("fsdp", "tp"), None),
        ),
        out_specs=(
            P(("fsdp", "tp"), None),
            P(("fsdp", "tp"), None),
            P(("fsdp", "tp")),
            P("fsdp", "tp"),
            P("fsdp", "tp"),
            P("fsdp", "tp"),
            P("tp", "fsdp"),
            P(("fsdp", "tp")),
            P(("fsdp", "tp"), None),
            P("tp", "fsdp", None),
            P("tp", "fsdp", None),
            P("tp", None, "fsdp"),
        ),
        check_vma=False,
    )
```
